512 devices in a mesh: gx: 16 (over z_lo, x, core), gy: 4 (over z_hi), gz: 8 (over y).
Axes of the slice: x: 4, y: 8, z: 8 (z_hi: 4, z_lo: 2; z = z_hi * 2 + z_lo), core: 2. Of those that a mesh axis runs over, the one named last changes fastest.
Arguments:
- positions: float32 [3, 131072], P(None, ('gx', 'gy', 'gz')), may hold values from 0 to 4
- species: int32 [131072], P(('gx', 'gy', 'gz')), may hold values from 0 to 5
- live_count: int32 [512], P(('gx', 'gy', 'gz')), may hold values from 22 to 256, as said below
- send_lists: int32 [6, 16384], P(None, ('gx', 'gy', 'gz')), may hold values from 0 to 383, as said below
- neighbours: int32 [524288], P(('gx', 'gy', 'gz')), may hold values from 0 to 447, as said below
- embed: float32 [128, 6], replicated, may hold values from -6 to 6
- radial_in: float32 [2, 64, 8], replicated, may hold values from -2 to 2
- radial_out: float32 [2, 384, 64], replicated, may hold values from -0.75 to 0.75
- w_up: float32 [2, 128, 128], replicated, may hold values from -0.5 to 0.5
- w_skip: float32 [2, 128, 128], replicated, may hold values from -0.5 to 0.5
- w_mix: float32 [2, 128, 512], replicated, may hold values from -0.25 to 0.25
- readout: float32 [2, 128], replicated, may hold values from -0.5 to 0.5
Outputs:
- atom_energy: float32 [131072], P(('gx', 'gy', 'gz'))
- forces: float32 [3, 131072], P(None, ('gx', 'gy', 'gz'))
The draws below stay inside these ranges and needn't reach their ends.
Inputs may be any that keep to these rules, and one draw needn't show every extreme that they name: `live_count`: each brick's count is at least 22; some brick is full in every draw; the mean is near a third of 256. `send_lists`: section s lists name only live own rows or rows appended in earlier sections of the same brick, that is rows below the count or from 256 to 256 + 2 s * 32 - 1; rows may repeat. `neighbours`: for a live centre a the row is a live own row other than a or a ghost row; slots of empty centres hold arbitrary rows of the table.
All inputs are finite; a program needn't handle non-finite values.
Results may differ from the reference program's by a relative error of at most 0.0003.
Values sent between devices are 32-bit elements; how exact they have to be, the bound alone decides.
A program may use at most 64 MiB of HBM per device.

```python
import math
import jax
import jax.numpy as jnp
from jax import lax

CHAN = 128
NBASIS = 8
RHID = 64
SPECIES = 6
LAYERS = 2
NEIGH = 4
ATOM_DEV = 256
GHOST = 32
ATOMS = 131072
N_GX = 16
N_GY = 4
N_GZ = 8
DEVICES = 512


def brick_counts(key):
    key = jax.random.fold_in(key, 11)
    counts = jax.random.randint(key, (DEVICES,), ATOM_DEV // 12 + 1, 7 * ATOM_DEV // 12 + 1)
    fullest = jax.random.randint(jax.random.fold_in(key, 1), (), 0, DEVICES)
    return jnp.where(jnp.arange(DEVICES) == fullest, ATOM_DEV, counts).astype(jnp.int32)


def draw_live_count(key, part):
    return brick_counts(key)


def draw_send_lists(key, part):
    counts = brick_counts(key)
    key = jax.random.fold_in(key, 5)
    sections = jnp.arange(6) // 2
    upper_end = counts[None, :, None] + 2 * GHOST * sections[:, None, None]
    uniform_ints = jax.random.randint(key, (6, DEVICES, GHOST), 0, upper_end)
    picked = jnp.where(uniform_ints < counts[None, :, None], uniform_ints, uniform_ints - counts[None, :, None] + ATOM_DEV)
    return picked.reshape(6, DEVICES * GHOST).astype(jnp.int32)


def draw_neighbours(key, part):
    counts = brick_counts(key)
    key = jax.random.fold_in(key, 7)
    centre = jnp.arange(ATOM_DEV * NEIGH) // NEIGH
    upper_end = counts[:, None] + 6 * GHOST - 1
    uniform_ints = jax.random.randint(key, (DEVICES, ATOM_DEV * NEIGH), 0, upper_end)
    uniform_ints = uniform_ints + (uniform_ints >= centre[None, :]).astype(jnp.int32)
    picked = jnp.where(uniform_ints < counts[:, None], uniform_ints, uniform_ints - counts[:, None] + ATOM_DEV)
    return picked.reshape(-1).astype(jnp.int32)


def set_ends(values, own_key, smallest, top_value):
    longest = values.shape.index(max(values.shape))
    spots = []
    for shift in (0, 1):
        where = [jax.random.randint(jax.random.fold_in(own_key, axis), (), 0, length) for axis, length in enumerate(values.shape)]
        where[longest] = (where[longest] + shift) % values.shape[longest]
        spots.append(tuple(where))
    return values.at[spots[0]].set(smallest).at[spots[1]].set(top_value)


def block_scale(stream_key, shape, cuts, least, largest):
    level, own = 1.0, jax.random.fold_in(stream_key, 6)
    for axis_at, blocks in cuts:
        steps = jnp.exp(jax.random.uniform(jax.random.fold_in(own, axis_at), (blocks,), jnp.float32, least / len(cuts), largest / len(cuts)))
        level = level * jnp.repeat(steps, shape[axis_at] // blocks).reshape([-1 if axis == axis_at else 1 for axis in range(len(shape))])
    return level


def gaussian(rng, dims, spread, reach, held_as=jnp.bfloat16):
    result = spread * jax.random.normal(rng, dims, jnp.float32)
    return jnp.clip(result, min=-reach, max=reach).astype(held_as)


def setup_inputs(seed: int = 0) -> dict:
    seeds = jax.random.split(jax.random.key(seed), 13)
    positions = jnp.clip(4.0 * jax.random.uniform(seeds[0], (3, ATOMS), jnp.float32) ** block_scale(seeds[0], (3, ATOMS), ((1, 512),), -0.2, 0.2), 0.0, 4.0)
    species = set_ends(jax.random.randint(seeds[1], (ATOMS,), 0, SPECIES), jax.random.fold_in(seeds[1], 1), 0, SPECIES - 1).astype(jnp.int32)
    live_count = draw_live_count(jax.random.fold_in(seeds[12], 71), 0)
    send_lists = draw_send_lists(jax.random.fold_in(seeds[12], 71), 0)
    neighbours = draw_neighbours(jax.random.fold_in(seeds[12], 71), 0)
    embed = gaussian(seeds[5], (CHAN, SPECIES), 1.0, 6.0, jnp.float32)
    radial_in = gaussian(seeds[6], (LAYERS, RHID, NBASIS), NBASIS ** -0.5, 2.0, jnp.float32)
    radial_out = gaussian(seeds[7], (LAYERS, 3 * CHAN, RHID), RHID ** -0.5, 0.75, jnp.float32)
    w_up = gaussian(seeds[8], (LAYERS, CHAN, CHAN), CHAN ** -0.5, 0.5, jnp.float32)
    w_skip = gaussian(seeds[9], (LAYERS, CHAN, CHAN), CHAN ** -0.5, 0.5, jnp.float32)
    w_mix = gaussian(seeds[10], (LAYERS, CHAN, 4 * CHAN), (4 * CHAN) ** -0.5, 0.25, jnp.float32)
    readout = gaussian(seeds[11], (LAYERS, CHAN), CHAN ** -0.5, 0.5, jnp.float32)
    return {"positions": positions, "species": species, "live_count": live_count, "send_lists": send_lists, "neighbours": neighbours, "embed": embed, "radial_in": radial_in, "radial_out": radial_out, "w_up": w_up, "w_skip": w_skip, "w_mix": w_mix, "readout": readout}


highest = lax.Precision.HIGHEST
cutoff = 4.0
floor_sq = 0.04
box_edge = 4.0

def harmonics(direction):
    ux, uy, uz = (direction[0], direction[1], direction[2])
    root3 = math.sqrt(3.0)
    root15 = math.sqrt(15.0)
    root5 = math.sqrt(5.0)
    return jnp.stack([jnp.ones_like(ux), root3 * ux, root3 * uy, root3 * uz, root15 * ux * uy, root15 * uy * uz, 0.5 * root5 * (3.0 * uz * uz - 1.0), root15 * ux * uz, 0.5 * root15 * (ux * ux - uy * uy)])

def bessel(distance, number):
    orders = jnp.arange(1, number + 1).astype(distance.dtype)[:, None]
    envelope = jnp.where(distance < cutoff, (1.0 - (distance / cutoff) ** 2) ** 2, 0.0 * distance)
    return math.sqrt(2.0 / cutoff) * jnp.sin(orders * math.pi * distance / cutoff) / distance * envelope

def interact(feat_table, pos_table, neigh, live, layer_in, layer_out, layer_up, layer_skip, layer_mix):
    atom_count = live.shape[0]
    channels = layer_up.shape[0]
    slots = neigh.shape[0]
    per_atom = slots // atom_count
    centre_pos = jnp.repeat(pos_table[:, :atom_count], per_atom, axis=1)
    offset_vec = jnp.take(pos_table, neigh, axis=1) - centre_pos
    distance = jnp.sqrt(lax.optimization_barrier(jnp.sum(offset_vec * offset_vec, axis=0)) + floor_sq)
    angular = harmonics(offset_vec / distance)
    basis = bessel(distance, layer_in.shape[1])
    hidden = jax.nn.silu(jnp.dot(layer_in, basis, precision=highest))
    radial = jnp.dot(layer_out, hidden, precision=highest).reshape(3, channels, slots)
    projected = jnp.dot(layer_up, feat_table, precision=highest)
    moved = jnp.take(projected, neigh, axis=1) * jnp.repeat(live, per_atom)[None, :]
    blocks = [angular[0:1], angular[1:4], angular[4:9]]
    scale = 1.0 / math.sqrt(per_atom)
    parts = []
    for degree in range(3):
        weighted = (radial[degree] * moved).reshape(channels, atom_count, per_atom)
        harm = blocks[degree].reshape(-1, atom_count, per_atom)
        parts.append(jnp.einsum('cak,mak->mca', weighted, harm, precision=highest) * scale)
    invariants = jnp.concatenate([parts[0][0], lax.optimization_barrier(jnp.mean(parts[0] ** 2, axis=0)), lax.optimization_barrier(jnp.mean(parts[1] ** 2, axis=0)), lax.optimization_barrier(jnp.mean(parts[2] ** 2, axis=0))], axis=0)
    return jnp.dot(layer_skip, feat_table[:, :atom_count], precision=highest) + jnp.dot(layer_mix, invariants, precision=highest)

def spread_all(table, sends, with_pos):
    picker = jax.vmap(lambda tab, rows: jnp.take(tab, rows, axis=1))
    for section_index in range(3):
        down_send = picker(table, sends[:, 2 * section_index])
        up_send = picker(table, sends[:, 2 * section_index + 1])
        grid_shape = (N_GX, N_GY, N_GZ) + down_send.shape[1:]
        from_lower = jnp.roll(up_send.reshape(grid_shape), 1, axis=section_index).reshape(down_send.shape)
        from_upper = jnp.roll(down_send.reshape(grid_shape), -1, axis=section_index).reshape(down_send.shape)
        if with_pos:
            from_lower = from_lower.at[:, section_index].add(-box_edge)
            from_upper = from_upper.at[:, section_index].add(box_edge)
        table = jnp.concatenate([table, from_lower, from_upper], axis=2)
    return table

def reference(positions, species, live_count, send_lists, neighbours, embed, radial_in, radial_out, w_up, w_skip, w_mix, readout):

    def per_device(array, rows):
        return array.reshape(rows, DEVICES, -1).transpose(1, 0, 2)
    sends = per_device(send_lists, 6)
    neigh_dev = neighbours.reshape(DEVICES, -1)
    kinds = species.reshape(DEVICES, ATOM_DEV)
    live = (jnp.arange(ATOM_DEV)[None, :] < live_count[:, None]).astype(jnp.float32)
    onehot = (kinds[:, None, :] == jnp.arange(SPECIES)[None, :, None]).astype(jnp.float32)
    start = jnp.einsum('cs,dsa->dca', embed, onehot, precision=highest)

    def run_layer(tables, pos_tables, layer):

        def one_brick(items):
            return interact(items[0], items[1], items[2], items[3], radial_in[layer], radial_out[layer], w_up[layer], w_skip[layer], w_mix[layer])
        return lax.map(jax.checkpoint(one_brick), (tables, pos_tables, neigh_dev, live))

    def total(pos_dev):
        table0 = spread_all(jnp.concatenate([pos_dev, start], axis=1), sends, True)
        pos_table = table0[:, :3]
        first = run_layer(table0[:, 3:], pos_table, 0)
        second = run_layer(spread_all(first, sends, False), pos_table, 1)
        energy = (jnp.einsum('c,dca->da', readout[0], first, precision=highest) + jnp.einsum('c,dca->da', readout[1], second, precision=highest)) * live
        return (jnp.sum(energy), energy)
    grads, energy = jax.grad(total, has_aux=True)(per_device(positions, 3))
    forces = -grads.transpose(1, 0, 2).reshape(3, ATOMS)
    return (energy.reshape(ATOMS), forces)
```

```python
import functools
import itertools
import math

import jax
import jax.numpy as jnp
from jax import lax
from jax.experimental import pallas as pl
from jax.experimental.pallas import tpu as pltpu
from jax.sharding import PartitionSpec as P

AXES = ("gx", "gy", "gz")
MESH = pl.DeviceIdType.MESH
OFFSETS = [o for o in itertools.product((-1, 0, 1), repeat=3) if any(o)]
SLOT = {o: j for j, o in enumerate(OFFSETS)}
HOPS_FIRST = sorted(OFFSETS, key=lambda o: -(abs(o[0]) + 2 * abs(o[1]) + abs(o[2])))
f32 = jnp.float32
bf16 = jnp.bfloat16
HIGHEST = lax.Precision.HIGHEST
ATOMS = 256
SLOTS = 1024
CHAN = 128
TABLE = 512
DEGREE = (0, 1, 1, 1, 2, 2, 2, 2, 2)
ROOT3 = math.sqrt(3.0)
ROOT5 = math.sqrt(5.0)
ROOT15 = math.sqrt(15.0)
X_BRICKS = [(0, 0), (0, -1), (0, 1), (-1, 0), (1, 0), (-1, -1), (1, -1), (-1, 1), (1, 1)]
Y_BRICKS = [-1, 0, 1]


def place(d):
    dx, dy, dz = d
    if dz:
        n = (dx + 1) * 3 + dy + 1
        return 3 + n // 2, (n % 2) * 2 + (0 if dz > 0 else 1)
    if dy:
        return dx + 1, 2 if dy > 0 else 3
    return 0, 0 if dx > 0 else 1


def negated(o):
    return (-o[0], -o[1], -o[2])


def iota(shape, dim):
    return lax.broadcasted_iota(jnp.int32, shape, dim)


def dot(a, b):
    return jnp.dot(a, b, preferred_element_type=f32)


def dot_t(a, b):
    return lax.dot_general(a, b, (((1,), (1,)), ((), ())), preferred_element_type=f32)


def exact_dot(a, b):
    return jnp.dot(a, b, precision=HIGHEST, preferred_element_type=f32)


def split(x):
    hi = x.astype(bf16)
    return hi, (x - hi.astype(f32)).astype(bf16)


def terms(x, count):
    out = []
    for _ in range(count):
        hi = x.astype(bf16).astype(f32)
        out.append(hi)
        x = x - hi
    return jnp.concatenate(out, axis=0).astype(bf16)


def gathered(x, onehot, count):
    rows = x.shape[0]
    wide = dot(terms(x, count), onehot)
    return sum(wide[i * rows : (i + 1) * rows] for i in range(count))


def scattered(x, onehot):
    rows = x.shape[0]
    wide = dot_t(terms(x, 2), onehot)
    return wide[:rows] + wide[rows:]


def ones_where(mask):
    return jnp.where(mask, 1.0, 0.0).astype(bf16)


def dot3(a_hi, a_lo, b):
    b_hi, b_lo = split(b)
    return dot(a_hi, b_hi) + (dot(a_hi, b_lo) + dot(a_lo, b_hi))


def column(row):
    eye = iota((128, 128), 0) == iota((128, 128), 1)
    return jnp.sum(jnp.where(eye, row, 0.0), axis=1, keepdims=True)


def kernel(
    sizes,
    pos_ref,
    species_ref,
    count_ref,
    sends_ref,
    neigh_ref,
    embed_ref,
    readout_ref,
    rin_hbm,
    rout_hbm,
    up_hbm,
    skip_hbm,
    mix_hbm,
    energy_ref,
    force_ref,
    rin_ref,
    rout_ref,
    up_ref,
    skip_ref,
    mix_ref,
    own_ref,
    r1_ref,
    s2_ref,
    r2_ref,
    s3_ref,
    r3_ref,
    s4_ref,
    r4_ref,
    hot_ref,
    route_ref,
    win_ref,
    wout_ref,
    mix0_ref,
    mix0t_ref,
    up1_ref,
    up1t_ref,
    tl_ref,
    dl_ref,
    dinv_ref,
    rad_ref,
    m_ref,
    a_ref,
    y_ref,
    inv_ref,
    dm_ref,
    red_ref,
    geo_ref,
    env_ref,
    load_sem,
    send_sem,
    recv_sem,
):
    def device(o):
        out = {}
        for axis, step in zip(AXES, o):
            here = lax.axis_index(axis)
            out[axis] = here if step == 0 else lax.rem(here + (sizes[axis] + step), sizes[axis])
        return out

    loads = [
        pltpu.make_async_copy(src, dst, load_sem.at[i])
        for i, (src, dst) in enumerate(
            (
                (rin_hbm, rin_ref),
                (rout_hbm, rout_ref),
                (up_hbm, up_ref),
                (skip_hbm, skip_ref),
                (mix_hbm, mix_ref),
            )
        )
    ]
    for load in loads:
        load.start()
    barrier = pltpu.get_barrier_semaphore()
    for o in HOPS_FIRST:
        pl.semaphore_signal(barrier, inc=1, device_id=device(o), device_id_type=MESH)

    def send(stage, source, inbox):
        for o in HOPS_FIRST:
            pltpu.make_async_remote_copy(
                src_ref=source(o),
                dst_ref=inbox.at[SLOT[negated(o)]],
                send_sem=send_sem.at[stage],
                recv_sem=recv_sem.at[stage],
                device_id=device(o),
                device_id_type=MESH,
            ).start()

    def whole(stage, inbox):
        return pltpu.make_async_remote_copy(
            src_ref=inbox,
            dst_ref=inbox,
            send_sem=send_sem.at[stage],
            recv_sem=recv_sem.at[stage],
            device_id=device((1, 0, 0)),
            device_id_type=MESH,
        )

    own_ref[0:3, :] = pos_ref[...]
    own_ref[3:4, :] = species_ref[...].astype(f32)
    lists = sends_ref[...].astype(f32)
    lists = jnp.concatenate([lists, lists, lists, lists], axis=1)
    own_ref[4:8, 0:128] = lists[0:4]
    own_ref[4:6, 128:256] = lists[4:6]
    own_ref[6:8, 128:256] = jnp.zeros((2, 128), f32)

    lane = iota((1, 128), 1)
    quarter = lane // 32
    live = jnp.where(iota((1, ATOMS), 1) < count_ref[0], 1.0, 0.0)
    live4 = jnp.concatenate([live] * 4, axis=1)

    neigh = neigh_ref[...]
    halves = jnp.concatenate([neigh >> 8, neigh & 255], axis=0).astype(f32).astype(bf16)
    sel_row = iota((128, SLOTS), 0)
    sel_col = iota((128, SLOTS), 1)
    chosen = dot(halves, ones_where(sel_row == 4 * (sel_col & 31) + (sel_col >> 8)))
    chosen = chosen[0:8] * 256.0 + chosen[8:16]
    group = iota((8, SLOTS), 0) == ((iota((8, SLOTS), 1) & 255) >> 5)
    neigh_row = jnp.sum(jnp.where(group, chosen, 0.0), axis=0, keepdims=True).astype(jnp.int32)

    def hot_step(i, carry):
        first = pl.multiple_of(i * 64, 64)
        hot_ref[pl.ds(first, 64), :] = ones_where(iota((64, SLOTS), 0) + i * 64 == neigh_row)
        return carry

    lax.fori_loop(0, TABLE // 64, hot_step, 0)

    pl.semaphore_wait(barrier, len(OFFSETS))
    send(0, lambda o: own_ref, r1_ref)

    for load in loads:
        load.wait()
    spread8 = (iota((8, 128), 1) & 7) == iota((8, 128), 0)
    spread8 = jnp.where(spread8 & (iota((8, 128), 1) < 24), 1.0, 0.0)
    wide_lane = iota((128, 128), 1)
    for layer in range(2):
        rin = exact_dot(rin_ref[layer], spread8)
        hi = rin.astype(bf16).astype(f32)
        lo = rin - hi
        win_ref[layer] = jnp.where(iota((64, 128), 1) < 16, hi, lo)[:, :32].astype(bf16)
        hi, lo = split(rout_ref[layer])
        wout_ref[layer] = jnp.concatenate([hi, hi, lo], axis=1)
    mix0 = mix_ref[0]
    mix0_ref[0], mix0_ref[1] = split(mix0)
    mix0t_ref[0], mix0t_ref[1] = split(mix0.T)
    up1 = up_ref[1]
    up1_ref[0], up1_ref[1] = split(up1)
    up1t_ref[0], up1t_ref[1] = split(up1.T)
    embed3 = exact_dot(embed_ref[...], spread8[0:6])

    def three_terms(x):
        hi = x.astype(bf16).astype(f32)
        mid = (x - hi).astype(bf16).astype(f32)
        lo = x - hi - mid
        x = jnp.where(wide_lane < 8, hi, jnp.where(wide_lane < 16, mid, lo))
        return x[:, :32].astype(bf16)

    up_kinds = three_terms(exact_dot(up_ref[0], embed3))
    skip_kinds = three_terms(exact_dot(skip_ref[0], embed3))
    ro0 = readout_ref[0:1, :]
    ro1 = readout_ref[1:2, :]
    dl_ref[...] = column(ro0 + exact_dot(ro1, skip_ref[1])) * live
    mixed = exact_dot(ro1, mix_ref[1])
    for k in range(4):
        tl_ref[k * 128 : (k + 1) * 128, :] = column(mixed[:, k * 128 : (k + 1) * 128]) * live

    def kind_hot(row):
        width = row.shape[1]
        sub = iota((32, width), 0)
        return ones_where(((sub & 7).astype(f32) == row) & (sub < 24))

    whole(0, r1_ref).wait_recv()

    def table(o):
        return r1_ref[SLOT[o]] if any(o) else own_ref[...]

    def rows(o, which):
        ref = r1_ref.at[SLOT[o]] if any(o) else own_ref
        if which < 4:
            return ref[4 + which : 5 + which, 0:128]
        return ref[which : which + 1, 128:256]

    def by_quarter(parts):
        parts = list(parts) + [parts[-1]] * (4 - len(parts))
        out = parts[3]
        for q in (2, 1, 0):
            out = jnp.where(quarter == q, parts[q], out)
        return out

    def pick(tables, indices, section):
        index = by_quarter(indices).astype(jnp.int32)
        depth = tables[0].shape[1]
        onehot = ones_where(iota((depth, 128), 0) == index)
        stack = jnp.concatenate(tables, axis=0)
        out = gathered(stack, onehot, 3)
        out = by_quarter([out[8 * i : 8 * i + 8] for i in range(len(tables))])
        shift = jnp.where((quarter & 1) == 0, -4.0, 4.0)
        return out + jnp.where(iota((8, 128), 0) == section, shift, 0.0)

    x_tiles = []
    for t in range(0, 9, 2):
        tables, indices = [], []
        for oy, oz in X_BRICKS[t : t + 2]:
            tables += [table((-1, oy, oz)), table((1, oy, oz))]
            indices += [rows((-1, oy, oz), 1), rows((1, oy, oz), 0)]
        x_tiles.append(pick(tables, indices, 0))

    y_tiles = []
    for t in range(0, 3, 2):
        tables, indices = [], []
        for oz in Y_BRICKS[t : t + 2]:
            for oy, which in ((-1, 3), (1, 2)):
                at = X_BRICKS.index((oy, oz))
                tables.append(jnp.concatenate([table((0, oy, oz)), x_tiles[at // 2]], axis=1))
                index = rows((0, oy, oz), which)
                indices.append(index + jnp.where(index < 256.0, 0.0, 64.0 * (at % 2)))
        y_tiles.append(pick(tables, indices, 1))

    tables, indices = [], []
    for oz, which in ((-1, 5), (1, 4)):
        at = X_BRICKS.index((0, oz))
        at_y = Y_BRICKS.index(oz)
        tables.append(
            jnp.concatenate([table((0, 0, oz)), x_tiles[at // 2], y_tiles[at_y // 2]], axis=1)
        )
        index = rows((0, 0, oz), which)
        far = jnp.where(index < 320.0, 64.0 * (at % 2), 64.0 + 64.0 * (at_y % 2))
        indices.append(index + jnp.where(index < 256.0, 0.0, far))
    z_tile = pick(tables, indices, 2)
    ghost0 = jnp.where(lane < 64, x_tiles[0], y_tiles[0])
    ghost1 = jnp.where(lane < 64, z_tile, 0.0)
    full = jnp.concatenate([own_ref[...], ghost0, ghost1], axis=1)

    here = (0, 0, 0)
    direct_lower = rows(here, 1) + 1.0
    direct_upper = rows(here, 0) + 1.0

    def own_only(index):
        return jnp.where(index < 256.0, index + 1.0, 0.0)

    def looked_up(index, lowest, offset):
        inside = (index >= lowest) & (index < lowest + 32.0)
        return jnp.where(inside, index + offset, -1.0)

    def compose(keys, entries):
        depth = entries.shape[1]
        onehot = ones_where(iota((depth, keys.shape[1]), 0) == keys.astype(jnp.int32))
        entries = jnp.broadcast_to(entries, (8, depth)).astype(bf16)
        return dot(entries, onehot)[0:1]

    zero_row = jnp.zeros((1, 128), f32)
    x_entries = by_quarter([direct_lower, direct_upper, zero_row, zero_row])
    keys = []
    for dx, lowest in ((-1, 288.0), (1, 256.0)):
        o = (dx, 0, 0)
        parts = [looked_up(rows(o, which), lowest, -256.0) for which in (3, 2)]
        keys.append(by_quarter([zero_row - 1.0, zero_row - 1.0] + parts))
    found = compose(jnp.concatenate(keys, axis=1), x_entries)
    route = [
        by_quarter([direct_lower, direct_upper, found[:, 0:128], found[:, 0:128]]),
        by_quarter([zero_row, zero_row, own_only(rows(here, 3)), own_only(rows(here, 2))]),
        by_quarter([zero_row, zero_row, found[:, 128:256], found[:, 128:256]]),
    ]
    keys, directs = [], []
    for n in range(0, 10, 2):
        key, direct = [], []
        for at in (n, n + 1):
            dx, dy = at // 3 - 1, at % 3 - 1
            for which in (5, 4):
                if at > 8:
                    key.append(zero_row - 1.0)
                    direct.append(zero_row)
                elif dx == 0 and dy == 0:
                    key.append(zero_row - 1.0)
                    direct.append(own_only(rows(here, which)))
                else:
                    if dy:
                        lowest = 320.0 if dy > 0 else 352.0
                        offset = 128.0 * (dx + 1) - 256.0
                    else:
                        lowest = 256.0 if dx > 0 else 288.0
                        offset = -256.0
                    key.append(looked_up(rows((dx, dy, 0), which), lowest, offset))
                    direct.append(zero_row)
        keys.append(by_quarter(key))
        directs.append(by_quarter(direct))
    found = compose(jnp.concatenate(keys, axis=1), jnp.concatenate(route, axis=1))
    found = found + jnp.concatenate(directs, axis=1)
    route_row = jnp.concatenate(route + [found], axis=1).astype(jnp.int32)

    def route_step(i, carry):
        first = pl.multiple_of(i * 64, 64)
        route_ref[pl.ds(first, 64), :] = ones_where(iota((64, SLOTS), 0) + (i * 64 + 1) == route_row)
        return carry

    lax.fori_loop(0, ATOMS // 64, route_step, 0)

    centres = jnp.concatenate([full[:, :ATOMS]] * 4, axis=1)
    is_coord = iota((8, SLOTS), 0) < 3
    moved = gathered(full, hot_ref[...], 3)
    slots_own = moved - jnp.where(is_coord, centres, 0.0)
    for k in range(4):
        env_ref[4 * k : 4 * k + 4, :] = slots_own[0:4, k * ATOMS : (k + 1) * ATOMS]
    spread_env = gathered(env_ref[...], route_ref[...], 3)
    for g in range(8):
        s2_ref[g] = spread_env[:, g * 128 : (g + 1) * 128]
    send(1, lambda o: s2_ref.at[place(o)[0]], r2_ref)

    def geometry(at, slots):
        vx, vy, vz = slots[0:1], slots[1:2], slots[2:3]
        r_sq = vx * vx + vy * vy + vz * vz + 0.04
        inv = lax.rsqrt(r_sq)
        r = r_sq * inv
        ux, uy, uz = vx * inv, vy * inv, vz * inv
        geo_ref[at, 0:1, :] = ux
        geo_ref[at, 1:2, :] = uy
        geo_ref[at, 2:3, :] = uz
        geo_ref[at, 3:4, :] = inv
        harm = [
            ROOT3 * ux,
            ROOT3 * uy,
            ROOT3 * uz,
            ROOT15 * ux * uy,
            ROOT15 * uy * uz,
            0.5 * ROOT5 * (3.0 * uz * uz - 1.0),
            ROOT15 * ux * uz,
            0.5 * ROOT15 * (ux * ux - uy * uy),
        ]
        for m in range(8):
            y_ref[at, m] = jnp.broadcast_to(0.5 * harm[m], (8, SLOTS))
        x = r * 0.25
        order = (iota((8, SLOTS), 0) + 1).astype(f32)
        phase = order * x
        near = jnp.floor(phase + 0.5)
        part = phase - near
        sign = 1.0 - 2.0 * (near - 2.0 * jnp.floor(near * 0.5))
        angle = part * math.pi
        square = angle * angle
        sin = 1.0
        for k in (14, 12, 10, 8, 6, 4, 2):
            sin = 1.0 - square * sin * (1.0 / (k * (k + 1)))
        sin = sign * angle * sin
        cos = 1.0
        for k in (14, 12, 10, 8, 6, 4, 2):
            cos = 1.0 - square * cos * (1.0 / (k * (k - 1)))
        cos = sign * cos
        gap = 1.0 - x * x
        within = x < 1.0
        env = jnp.where(within, gap * gap, 0.0)
        env_d = jnp.where(within, -x * gap, 0.0)
        scale = math.sqrt(0.5)
        base = scale * sin * inv
        basis = base * env
        basis_d = (scale * (math.pi / 4.0) * order * cos * inv - base * inv) * env + base * env_d
        wide = jnp.concatenate([basis, basis_d], axis=1)
        hi = wide.astype(bf16).astype(f32)
        lo = wide - hi
        return jnp.concatenate([hi, lo, hi, jnp.zeros_like(hi)], axis=0).astype(bf16)

    def radial(at, layer, basis):
        z = dot(win_ref[layer], basis)
        slope, z = z[:, SLOTS:], z[:, :SLOTS]
        gate = 1.0 / (1.0 + jnp.exp(-z))
        hidden = z * gate
        hidden_d = gate * (1.0 + z * (1.0 - gate)) * slope
        for half, x in enumerate((hidden, hidden_d)):
            hi, lo = split(x)
            rad_ref[at, half * 384 : (half + 1) * 384, :] = dot(
                wout_ref[layer], jnp.concatenate([hi, lo, hi], axis=0)
            )

    def forward(at, y_at):
        def step(i, carry):
            first = pl.multiple_of(i * 8, 8)
            m = m_ref[at, pl.ds(first, 8), :]
            weighted = [rad_ref[at, pl.ds(k * 128 + first, 8), :] * m for k in range(3)]
            squares = [None, None, None]
            for n in range(9):
                x = weighted[DEGREE[n]]
                x = 0.5 * x if n == 0 else y_ref[y_at, n - 1] * x
                total = (x[:, 0:256] + x[:, 256:512]) + (x[:, 512:768] + x[:, 768:1024])
                a_ref[at, pl.ds(n * 128 + first, 8), :] = total
                if n == 0:
                    inv_ref[pl.ds(first, 8), :] = total
                square = total * total
                old = squares[DEGREE[n]]
                squares[DEGREE[n]] = square if old is None else old + square
            inv_ref[pl.ds(128 + first, 8), :] = squares[0]
            inv_ref[pl.ds(256 + first, 8), :] = squares[1] * (1.0 / 3.0)
            inv_ref[pl.ds(384 + first, 8), :] = squares[2] * (1.0 / 5.0)
            return carry

        lax.fori_loop(0, CHAN // 8, step, 0)

    def moment_grads(at, grads):
        def step(i, carry):
            first = pl.multiple_of(i * 8, 8)
            lead = grads[pl.ds(first, 8), :]
            factors = [
                2.0 * grads[pl.ds(128 + first, 8), :],
                (2.0 / 3.0) * grads[pl.ds(256 + first, 8), :],
                (2.0 / 5.0) * grads[pl.ds(384 + first, 8), :],
            ]
            for n in range(9):
                x = a_ref[at, pl.ds(n * 128 + first, 8), :] * factors[DEGREE[n]]
                a_ref[at, pl.ds(n * 128 + first, 8), :] = x + lead if n == 0 else x
            return carry

        lax.fori_loop(0, CHAN // 8, step, 0)

    def backward(at, y_at, with_features):
        for k in range(4):
            lanes = slice(k * ATOMS, (k + 1) * ATOMS)

            def step(i, totals):
                first = pl.multiple_of(i * 8, 8)
                m = m_ref[at, pl.ds(first, 8), lanes]
                rad = [rad_ref[at, pl.ds(j * 128 + first, 8), lanes] for j in range(3)]
                rad_d = [rad_ref[at, pl.ds(384 + j * 128 + first, 8), lanes] for j in range(3)]
                weighted = [x * m for x in rad]
                grads = [None, None, None]
                out = []
                for n in range(9):
                    da = a_ref[at, pl.ds(n * 128 + first, 8), :]
                    if n == 0:
                        grads[0] = 0.5 * da
                        continue
                    out.append(totals[n - 1] + da * weighted[DEGREE[n]])
                    x = da * y_ref[y_at, n - 1, :, lanes]
                    old = grads[DEGREE[n]]
                    grads[DEGREE[n]] = x if old is None else old + x
                slope = grads[0] * rad_d[0] + grads[1] * rad_d[1] + grads[2] * rad_d[2]
                out.append(totals[8] + slope * m)
                if with_features:
                    dm_ref[pl.ds(first, 8), lanes] = (
                        grads[0] * rad[0] + grads[1] * rad[1] + grads[2] * rad[2]
                    )
                return tuple(out)

            zero = jnp.zeros((8, ATOMS), f32)
            totals = lax.fori_loop(0, CHAN // 8, step, (zero,) * 9)
            for n in range(9):
                red_ref[at, n : n + 1, lanes] = jnp.sum(totals[n], axis=0, keepdims=True)

    def vector_grads(at, y_at):
        g = [None] + [0.5 * red_ref[at, n : n + 1, :] for n in range(8)]
        slope = red_ref[at, 8:9, :]
        ux = geo_ref[y_at, 0:1, :]
        uy = geo_ref[y_at, 1:2, :]
        uz = geo_ref[y_at, 2:3, :]
        inv = geo_ref[y_at, 3:4, :]
        gx = ROOT3 * g[1] + ROOT15 * (uy * g[4] + uz * g[7] + ux * g[8])
        gy = ROOT3 * g[2] + ROOT15 * (ux * g[4] + uz * g[5] - uy * g[8])
        gz = ROOT3 * g[3] + ROOT15 * (uy * g[5] + ux * g[7]) + (3.0 * ROOT5) * uz * g[6]
        along = slope - (ux * gx + uy * gy + uz * gz) * inv
        return [gx * inv + ux * along, gy * inv + uy * along, gz * inv + uz * along]

    basis_own = geometry(0, slots_own)
    radial(0, 0, basis_own)
    m_ref[0] = dot(up_kinds, kind_hot(slots_own[3:4])) * live4
    forward(0, 0)
    skip = dot(skip_kinds, kind_hot(full[3:4, :]))
    first_own = skip[:, :ATOMS] + dot3(mix0_ref[0], mix0_ref[1], inv_ref[...])
    radial(2, 1, basis_own)

    whole(1, r2_ref).wait_recv()
    sums = [jnp.zeros((16, 128), f32), jnp.zeros((16, 128), f32)]
    for o in OFFSETS:
        at = 1 if o[2] else 0
        sums[at] = sums[at] + jnp.where(quarter == place(negated(o))[1], r2_ref[SLOT[o]], 0.0)
    sums[1] = jnp.where(lane < 64, sums[1] + pltpu.roll(sums[1], 64, 1), 0.0)
    ghost_env = jnp.concatenate(sums, axis=1)
    slots_ghost = jnp.concatenate([ghost_env[4 * k : 4 * k + 4] for k in range(4)], axis=1)
    radial(1, 0, geometry(1, slots_ghost))
    m_ref[1] = dot(up_kinds, kind_hot(slots_ghost[3:4]))
    forward(1, 1)
    first_ghost = skip[:, ATOMS:] + dot3(mix0_ref[0], mix0_ref[1], inv_ref[...])

    first = jnp.concatenate([first_own, first_ghost], axis=1)
    projected = dot3(up1_ref[0], up1_ref[1], first)
    m_ref[2] = gathered(projected, hot_ref[...], 2) * live4
    forward(2, 0)
    energy_ref[...] = jnp.sum(dl_ref[...] * first_own, axis=0, keepdims=True) + jnp.sum(
        tl_ref[...] * inv_ref[...], axis=0, keepdims=True
    )
    moment_grads(2, tl_ref)
    backward(2, 0, True)
    back = scattered(dm_ref[...], hot_ref[...])
    back = dot3(up1t_ref[0], up1t_ref[1], back)

    dinv_ref[...] = dot3(mix0t_ref[0], mix0t_ref[1], back[:, ATOMS:])
    moment_grads(1, dinv_ref)
    backward(1, 1, False)
    ghost_grads = vector_grads(1, 1)
    env_ref[...] = jnp.zeros((16, ATOMS), f32)
    for k in range(4):
        for n in range(3):
            env_ref[4 * k + n : 4 * k + n + 1, :] = ghost_grads[n][:, k * ATOMS : (k + 1) * ATOMS]
    s3_ref[0] = env_ref[:, 0:128]
    tail = env_ref[:, 128:256]
    s3_ref[1] = tail + pltpu.roll(tail, 64, 1)
    send(2, lambda o: s3_ref.at[1 if o[2] else 0], r3_ref)

    dinv_ref[...] = dot3(mix0t_ref[0], mix0t_ref[1], back[:, :ATOMS] + dl_ref[...])
    moment_grads(0, dinv_ref)
    backward(0, 0, False)
    grads = [a + b for a, b in zip(vector_grads(0, 0), vector_grads(2, 0))]
    grads = jnp.concatenate(grads + [jnp.zeros((5, SLOTS), f32)], axis=0)

    def returned(inbox):
        tiles = [None] * 8
        for o in OFFSETS:
            g, q = place(o)
            x = jnp.where(quarter == q, inbox[SLOT[o]], 0.0)
            tiles[g] = x if tiles[g] is None else tiles[g] + x
        return scattered(jnp.concatenate(tiles, axis=1), route_ref[...])

    whole(2, r3_ref).wait_recv()
    from_ghosts = returned(r3_ref)
    from_ghosts = jnp.concatenate([from_ghosts[4 * k : 4 * k + 4] for k in range(4)], axis=1)
    grads = grads + jnp.concatenate([from_ghosts, jnp.zeros((4, SLOTS), f32)], axis=0)
    table_grads = scattered(grads, hot_ref[...])
    s4_ref[0] = table_grads[:, 256:384]
    tail = table_grads[:, 384:512]
    s4_ref[1] = tail + pltpu.roll(tail, 64, 1)
    send(3, lambda o: s4_ref.at[1 if o[2] else 0], r4_ref)
    own_grads = table_grads[:, :ATOMS]
    for k in range(4):
        own_grads = own_grads - grads[:, k * ATOMS : (k + 1) * ATOMS]
    whole(3, r4_ref).wait_recv()
    own_grads = own_grads + returned(r4_ref)
    force_ref[...] = -own_grads[0:3]
    whole(0, r1_ref).wait_send()
    whole(1, r2_ref).wait_send()
    whole(2, r3_ref).wait_send()
    whole(3, r4_ref).wait_send()


def body(
    sizes,
    positions,
    species,
    live_count,
    send_lists,
    neighbours,
    embed,
    radial_in,
    radial_out,
    w_up,
    w_skip,
    w_mix,
    readout,
):
    vmem = pl.BlockSpec(memory_space=pltpu.VMEM)
    smem = pl.BlockSpec(memory_space=pltpu.SMEM)
    hbm = pl.BlockSpec(memory_space=pl.ANY)
    energy, forces = pl.pallas_call(
        functools.partial(kernel, sizes),
        out_shape=(
            jax.ShapeDtypeStruct((1, ATOMS), f32),
            jax.ShapeDtypeStruct((3, ATOMS), f32),
        ),
        in_specs=[vmem, vmem, smem, vmem, vmem, vmem, vmem] + [hbm] * 5,
        out_specs=(vmem, vmem),
        scratch_shapes=[
            pltpu.VMEM((2, 64, 8), f32),
            pltpu.VMEM((2, 384, 64), f32),
            pltpu.VMEM((2, 128, 128), f32),
            pltpu.VMEM((2, 128, 128), f32),
            pltpu.VMEM((2, 128, 512), f32),
            pltpu.VMEM((8, ATOMS), f32),
            pltpu.VMEM((26, 8, ATOMS), f32),
            pltpu.VMEM((8, 16, 128), f32),
            pltpu.VMEM((26, 16, 128), f32),
            pltpu.VMEM((2, 16, 128), f32),
            pltpu.VMEM((26, 16, 128), f32),
            pltpu.VMEM((2, 8, 128), f32),
            pltpu.VMEM((26, 8, 128), f32),
            pltpu.VMEM((TABLE, SLOTS), bf16),
            pltpu.VMEM((ATOMS, SLOTS), bf16),
            pltpu.VMEM((2, 64, 32), bf16),
            pltpu.VMEM((2, 384, 192), bf16),
            pltpu.VMEM((2, 128, 512), bf16),
            pltpu.VMEM((2, 512, 128), bf16),
            pltpu.VMEM((2, 128, 128), bf16),
            pltpu.VMEM((2, 128, 128), bf16),
            pltpu.VMEM((512, ATOMS), f32),
            pltpu.VMEM((128, ATOMS), f32),
            pltpu.VMEM((512, ATOMS), f32),
            pltpu.VMEM((3, 768, SLOTS), f32),
            pltpu.VMEM((3, 128, SLOTS), f32),
            pltpu.VMEM((3, 1152, ATOMS), f32),
            pltpu.VMEM((2, 8, 8, SLOTS), f32),
            pltpu.VMEM((512, ATOMS), f32),
            pltpu.VMEM((128, SLOTS), f32),
            pltpu.VMEM((3, 16, SLOTS), f32),
            pltpu.VMEM((2, 8, SLOTS), f32),
            pltpu.VMEM((16, ATOMS), f32),
            pltpu.SemaphoreType.DMA((5,)),
            pltpu.SemaphoreType.DMA((4,)),
            pltpu.SemaphoreType.DMA((4,)),
        ],
        compiler_params=pltpu.CompilerParams(
            collective_id=0, has_side_effects=True, vmem_limit_bytes=48 * 1024 * 1024
        ),
        name="potential",
    )(
        positions,
        species.reshape(1, ATOMS),
        live_count,
        send_lists,
        neighbours.reshape(8, 128),
        embed,
        readout,
        radial_in,
        radial_out,
        w_up,
        w_skip,
        w_mix,
    )
    return energy.reshape(ATOMS), forces


def solution(mesh):
    sizes = {axis: mesh.shape[axis] for axis in AXES}
    split_all = ("gx", "gy", "gz")
    return jax.shard_map(
        functools.partial(body, sizes),
        mesh=mesh,
        in_specs=(
            P(None, split_all),
            P(split_all),
            P(split_all),
            P(None, split_all),
            P(split_all),
            P(),
            P(),
            P(),
            P(),
            P(),
            P(),
            P(),
        ),
        out_specs=(P(split_all), P(None, split_all)),
        check_vma=False,
    )
```

```python
import functools
import itertools
import math

import jax
import jax.numpy as jnp
from jax import lax
from jax.experimental import pallas as pl
from jax.experimental.pallas import tpu as pltpu
from jax.sharding import PartitionSpec as P

AXES = ("gx", "gy", "gz")
MESH = pl.DeviceIdType.MESH
OFFSETS = [o for o in itertools.product((-1, 0, 1), repeat=3) if any(o)]
PLANE = [o for o in OFFSETS if not o[2]]
ABOVE = [o for o in OFFSETS if o[2]]
SLOT = {o: j for j, o in enumerate(PLANE + ABOVE)}
PLANE.sort(key=lambda o: -abs(o[1]))
ABOVE.sort(key=lambda o: -(abs(o[0]) + 2 * abs(o[1])))
f32 = jnp.float32
bf16 = jnp.bfloat16
HIGHEST = lax.Precision.HIGHEST
ATOMS = 256
SLOTS = 1024
CHAN = 128
OWN, NEAR, FAR, NEXT = 0, 1024, 1536, 1792
LANES = 2816
TABLE = 512
VMEM_BYTES = 62 * 1024 * 1024
DEGREE = (0, 1, 1, 1, 2, 2, 2, 2, 2)
ROOT3 = math.sqrt(3.0)
ROOT5 = math.sqrt(5.0)
ROOT15 = math.sqrt(15.0)
X_BRICKS = [(0, 0), (0, -1), (0, 1), (-1, 0), (1, 0), (-1, -1), (1, -1), (-1, 1), (1, 1)]
Y_BRICKS = [-1, 0, 1]


def place(d):
    dx, dy, dz = d
    if dz:
        n = (dx + 1) * 3 + dy + 1
        return 3 + n // 2, (n % 2) * 2 + (0 if dz > 0 else 1)
    if dy:
        return dx + 1, 2 if dy > 0 else 3
    return 0, 0 if dx > 0 else 1


def negated(o):
    return (-o[0], -o[1], -o[2])


def iota(shape, dim):
    return lax.broadcasted_iota(jnp.int32, shape, dim)


def dot(a, b):
    return jnp.dot(a, b, preferred_element_type=f32)


def dot_t(a, b):
    return lax.dot_general(a, b, (((1,), (1,)), ((), ())), preferred_element_type=f32)


def exact_dot(a, b, dim=0):
    return lax.dot_general(
        a, b, (((1,), (dim,)), ((), ())), precision=HIGHEST, preferred_element_type=f32
    )


def split(x):
    hi = x.astype(bf16)
    return hi, (x - hi.astype(f32)).astype(bf16)


def terms(x, count):
    out = []
    for _ in range(count):
        hi = x.astype(bf16).astype(f32)
        out.append(hi)
        x = x - hi
    return jnp.concatenate(out, axis=0).astype(bf16)


def gathered(x, onehot, count):
    rows = x.shape[0]
    wide = dot(terms(x, count), onehot)
    return sum(wide[i * rows : (i + 1) * rows] for i in range(count))


def ones_where(mask):
    return jnp.where(mask, 1.0, 0.0).astype(bf16)


def dot3(a_hi, a_lo, b):
    b_hi, b_lo = split(b)
    return dot(a_hi, b_hi) + (dot(a_hi, b_lo) + dot(a_lo, b_hi))


def column(row):
    eye = iota((128, 128), 0) == iota((128, 128), 1)
    return jnp.sum(jnp.where(eye, row, 0.0), axis=1, keepdims=True)


def kernel(
    sizes,
    count_hbm,
    pos_hbm,
    species_hbm,
    sends_hbm,
    neigh_hbm,
    embed_hbm,
    readout_hbm,
    rin_hbm,
    rout_hbm,
    up_hbm,
    skip_hbm,
    mix_hbm,
    energy_ref,
    force_ref,
    count_ref,
    pos_ref,
    species_ref,
    sends_ref,
    neigh_ref,
    embed_ref,
    readout_ref,
    rin_ref,
    rout_ref,
    up_ref,
    skip_ref,
    mix_ref,
    own_ref,
    r1_ref,
    s2_ref,
    r2_ref,
    s3_ref,
    r3_ref,
    s4_ref,
    r4_ref,
    hot_ref,
    hot_t_ref,
    route_ref,
    route_t_ref,
    win_ref,
    wout_ref,
    mix0_ref,
    mix0t_ref,
    up1_ref,
    up1t_ref,
    tl_ref,
    dl_ref,
    dinv_ref,
    rad_ref,
    m_ref,
    a_ref,
    y_ref,
    inv_ref,
    dm_ref,
    red_ref,
    geo_ref,
    env_ref,
    load_sem,
    send_sem,
    recv_sem,
):
    def device(o):
        out = {}
        for axis, step in zip(AXES, o):
            here = lax.axis_index(axis)
            out[axis] = here if step == 0 else lax.rem(here + (sizes[axis] + step), sizes[axis])
        return out

    loads = [
        pltpu.make_async_copy(src, dst, load_sem.at[i])
        for i, (src, dst) in enumerate(
            (
                (count_hbm, count_ref),
                (pos_hbm, pos_ref),
                (species_hbm, species_ref),
                (sends_hbm, sends_ref),
                (neigh_hbm, neigh_ref),
                (embed_hbm, embed_ref),
                (readout_hbm, readout_ref),
                (rin_hbm, rin_ref),
                (rout_hbm, rout_ref),
                (up_hbm, up_ref),
                (skip_hbm, skip_ref),
                (mix_hbm, mix_ref),
            )
        )
    ]
    for load in loads:
        load.start()
    barrier = pltpu.get_barrier_semaphore()
    for o in ABOVE + PLANE:
        pl.semaphore_signal(barrier, inc=1, device_id=device(o), device_id_type=MESH)

    def send(stage, source, inbox, group):
        for o in group:
            pltpu.make_async_remote_copy(
                src_ref=source(o),
                dst_ref=inbox.at[SLOT[negated(o)]],
                send_sem=send_sem.at[stage],
                recv_sem=recv_sem.at[stage, 1 if o[2] else 0],
                device_id=device(o),
                device_id_type=MESH,
            ).start()

    def copies(stage, inbox, part=0):
        return pltpu.make_async_remote_copy(
            src_ref=inbox,
            dst_ref=inbox,
            send_sem=send_sem.at[stage],
            recv_sem=recv_sem.at[stage, part],
            device_id=device((1, 0, 0)),
            device_id_type=MESH,
        )

    def wait_plane(stage, inbox):
        copies(stage, inbox.at[0:8], 0).wait_recv()

    def wait_above(stage, inbox):
        copies(stage, inbox.at[8:26], 1).wait_recv()

    for load in loads[:5]:
        load.wait()
    own_ref[0:3, :] = pos_ref[...]
    own_ref[3:4, :] = species_ref[...].astype(f32)
    lists = sends_ref[...].astype(f32)
    lists = jnp.concatenate([lists, lists, lists, lists], axis=1)
    own_ref[4:8, 0:128] = lists[0:4]
    own_ref[4:6, 128:256] = lists[4:6]
    own_ref[6:8, 128:256] = jnp.zeros((2, 128), f32)

    lane = iota((1, 128), 1)
    quarter = lane // 32
    live = jnp.where(iota((1, ATOMS), 1) < count_ref[...], 1.0, 0.0)
    live4 = jnp.concatenate([live] * 4, axis=1)

    neigh = neigh_ref[...]
    halves = jnp.concatenate([neigh >> 8, neigh & 255], axis=0).astype(f32).astype(bf16)
    sel_row = iota((128, SLOTS), 0)
    sel_col = iota((128, SLOTS), 1)
    chosen = dot(halves, ones_where(sel_row == 4 * (sel_col & 31) + (sel_col >> 8)))
    chosen = chosen[0:8] * 256.0 + chosen[8:16]
    group = iota((8, SLOTS), 0) == ((iota((8, SLOTS), 1) & 255) >> 5)
    neigh_row = jnp.sum(jnp.where(group, chosen, 0.0), axis=0, keepdims=True).astype(jnp.int32)

    def hot_step(i, carry):
        first = pl.multiple_of(i * 64, 64)
        hot_ref[pl.ds(first, 64), :] = ones_where(iota((64, SLOTS), 0) + i * 64 == neigh_row)
        return carry

    lax.fori_loop(0, TABLE // 64, hot_step, 0)

    def hot_t_step(i, carry):
        first = pl.multiple_of(i * 128, 128)
        slot = iota((128, 128), 0) + i * 128
        sel = ones_where(iota((128, 128), 1) == 4 * (slot & 31) + (slot >> 8))
        mine = dot_t(sel, halves)
        place_at = iota((128, 16), 1)
        mine = mine * jnp.where(place_at < 8, 256.0, 1.0)
        in_group = (place_at & 7) == (((iota((128, 16), 0) + i * 128) & 255) >> 5)
        mine = jnp.sum(jnp.where(in_group, mine, 0.0), axis=1, keepdims=True)
        hot_t_ref[pl.ds(first, 128), :] = ones_where(iota((128, TABLE), 1).astype(f32) == mine)
        return carry

    pl.semaphore_wait(barrier, len(OFFSETS))
    send(0, lambda o: own_ref, r1_ref, ABOVE + PLANE)

    lax.fori_loop(0, SLOTS // 128, hot_t_step, 0)
    for load in loads[5:]:
        load.wait()
    wide_lane = iota((128, 128), 1)

    def stacked(x):
        hi = x.astype(bf16).astype(f32)
        return jnp.concatenate([hi, hi, x - hi, jnp.zeros_like(x)], axis=0)

    for layer in range(2):
        rin = jnp.concatenate([stacked(rin_ref[layer]), jnp.zeros((96, 64), f32)], axis=0)
        rin = jnp.concatenate([rin, jnp.zeros((128, 64), f32)], axis=1).T
        win_ref[layer] = rin[:64, :32].astype(bf16)
        wout_ref[layer] = stacked(rout_ref[layer]).T[:, :192].astype(bf16)
    mix0 = mix_ref[0]
    mix0_ref[0], mix0_ref[1] = split(mix0)
    mix0t_ref[0], mix0t_ref[1] = split(mix0.T)
    up1 = up_ref[1]
    up1_ref[0], up1_ref[1] = split(up1)
    up1t_ref[0], up1t_ref[1] = split(up1.T)
    embed = jnp.concatenate([embed_ref[...], jnp.zeros((2, 128), f32)], axis=0)
    embed3 = jnp.concatenate([embed, embed, embed, jnp.zeros((104, 128), f32)], axis=0)

    def three_terms(x):
        hi = x.astype(bf16).astype(f32)
        mid = (x - hi).astype(bf16).astype(f32)
        lo = x - hi - mid
        x = jnp.where(wide_lane < 8, hi, jnp.where(wide_lane < 16, mid, lo))
        return x[:, :32].astype(bf16)

    up_kinds = three_terms(exact_dot(up_ref[0], embed3, 1))
    skip_kinds = three_terms(exact_dot(skip_ref[0], embed3, 1))
    ro0 = readout_ref[0:1, :]
    ro1 = readout_ref[1:2, :]
    dl_ref[...] = column(ro0 + exact_dot(ro1, skip_ref[1])) * live
    mixed = exact_dot(ro1, mix_ref[1])
    for k in range(4):
        tl_ref[k * 128 : (k + 1) * 128, :] = column(mixed[:, k * 128 : (k + 1) * 128]) * live

    def kind_hot(row):
        width = row.shape[1]
        sub = iota((32, width), 0)
        return ones_where(((sub & 7).astype(f32) == row) & (sub < 24))

    wait_plane(0, r1_ref)
    wait_above(0, r1_ref)

    def table(o):
        return r1_ref[SLOT[o]] if any(o) else own_ref[...]

    def rows(o, which):
        ref = r1_ref.at[SLOT[o]] if any(o) else own_ref
        if which < 4:
            return ref[4 + which : 5 + which, 0:128]
        return ref[which : which + 1, 128:256]

    def by_quarter(parts):
        parts = list(parts) + [parts[-1]] * (4 - len(parts))
        out = parts[3]
        for q in (2, 1, 0):
            out = jnp.where(quarter == q, parts[q], out)
        return out

    def pick(tables, indices, section):
        index = by_quarter(indices).astype(jnp.int32)
        depth = tables[0].shape[1]
        onehot = ones_where(iota((depth, 128), 0) == index)
        stack = jnp.concatenate(tables, axis=0)
        out = gathered(stack, onehot, 3)
        out = by_quarter([out[8 * i : 8 * i + 8] for i in range(len(tables))])
        shift = jnp.where((quarter & 1) == 0, -4.0, 4.0)
        return out + jnp.where(iota((8, 128), 0) == section, shift, 0.0)

    x_tiles = []
    for t in range(0, 9, 2):
        tables, indices = [], []
        for oy, oz in X_BRICKS[t : t + 2]:
            tables += [table((-1, oy, oz)), table((1, oy, oz))]
            indices += [rows((-1, oy, oz), 1), rows((1, oy, oz), 0)]
        x_tiles.append(pick(tables, indices, 0))

    y_tiles = []
    for t in range(0, 3, 2):
        tables, indices = [], []
        for oz in Y_BRICKS[t : t + 2]:
            for oy, which in ((-1, 3), (1, 2)):
                at = X_BRICKS.index((oy, oz))
                tables.append(jnp.concatenate([table((0, oy, oz)), x_tiles[at // 2]], axis=1))
                index = rows((0, oy, oz), which)
                indices.append(index + jnp.where(index < 256.0, 0.0, 64.0 * (at % 2)))
        y_tiles.append(pick(tables, indices, 1))

    tables, indices = [], []
    for oz, which in ((-1, 5), (1, 4)):
        at = X_BRICKS.index((0, oz))
        at_y = Y_BRICKS.index(oz)
        tables.append(
            jnp.concatenate([table((0, 0, oz)), x_tiles[at // 2], y_tiles[at_y // 2]], axis=1)
        )
        index = rows((0, 0, oz), which)
        far = jnp.where(index < 320.0, 64.0 * (at % 2), 64.0 + 64.0 * (at_y % 2))
        indices.append(index + jnp.where(index < 256.0, 0.0, far))
    z_tile = pick(tables, indices, 2)
    ghost0 = jnp.where(lane < 64, x_tiles[0], y_tiles[0])
    ghost1 = jnp.where(lane < 64, z_tile, 0.0)
    full = jnp.concatenate([own_ref[...], ghost0, ghost1], axis=1)

    here = (0, 0, 0)
    direct_lower = rows(here, 1) + 1.0
    direct_upper = rows(here, 0) + 1.0

    def own_only(index):
        return jnp.where(index < 256.0, index + 1.0, 0.0)

    def looked_up(index, lowest, offset):
        inside = (index >= lowest) & (index < lowest + 32.0)
        return jnp.where(inside, index + offset, -1.0)

    def compose(keys, entries):
        depth = entries.shape[1]
        onehot = ones_where(iota((depth, keys.shape[1]), 0) == keys.astype(jnp.int32))
        entries = jnp.broadcast_to(entries, (8, depth)).astype(bf16)
        return dot(entries, onehot)[0:1]

    zero_row = jnp.zeros((1, 128), f32)
    x_entries = by_quarter([direct_lower, direct_upper, zero_row, zero_row])
    keys = []
    for dx, lowest in ((-1, 288.0), (1, 256.0)):
        o = (dx, 0, 0)
        parts = [looked_up(rows(o, which), lowest, -256.0) for which in (3, 2)]
        keys.append(by_quarter([zero_row - 1.0, zero_row - 1.0] + parts))
    found = compose(jnp.concatenate(keys, axis=1), x_entries)
    route = [
        by_quarter([direct_lower, direct_upper, found[:, 0:128], found[:, 0:128]]),
        by_quarter([zero_row, zero_row, own_only(rows(here, 3)), own_only(rows(here, 2))]),
        by_quarter([zero_row, zero_row, found[:, 128:256], found[:, 128:256]]),
    ]
    keys, directs = [], []
    for n in range(0, 10, 2):
        key, direct = [], []
        for at in (n, n + 1):
            dx, dy = at // 3 - 1, at % 3 - 1
            for which in (5, 4):
                if at > 8:
                    key.append(zero_row - 1.0)
                    direct.append(zero_row)
                elif dx == 0 and dy == 0:
                    key.append(zero_row - 1.0)
                    direct.append(own_only(rows(here, which)))
                else:
                    if dy:
                        lowest = 320.0 if dy > 0 else 352.0
                        offset = 128.0 * (dx + 1) - 256.0
                    else:
                        lowest = 256.0 if dx > 0 else 288.0
                        offset = -256.0
                    key.append(looked_up(rows((dx, dy, 0), which), lowest, offset))
                    direct.append(zero_row)
        keys.append(by_quarter(key))
        directs.append(by_quarter(direct))
    found = compose(jnp.concatenate(keys, axis=1), jnp.concatenate(route, axis=1))
    found = found + jnp.concatenate(directs, axis=1)
    route_row = jnp.concatenate(route + [found], axis=1).astype(jnp.int32)

    def route_step(i, carry):
        first = pl.multiple_of(i * 64, 64)
        route_ref[pl.ds(first, 64), :] = ones_where(iota((64, SLOTS), 0) + (i * 64 + 1) == route_row)
        return carry

    lax.fori_loop(0, ATOMS // 64, route_step, 0)

    centres = jnp.concatenate([full[:, :ATOMS]] * 4, axis=1)
    is_coord = iota((8, SLOTS), 0) < 3
    moved = gathered(full, hot_ref[...], 3)
    slots_own = moved - jnp.where(is_coord, centres, 0.0)
    for k in range(4):
        env_ref[4 * k : 4 * k + 4, :] = slots_own[0:4, k * ATOMS : (k + 1) * ATOMS]
    spread_env = gathered(env_ref[...], route_ref[...], 3)
    for g in range(8):
        s2_ref[g] = spread_env[:, g * 128 : (g + 1) * 128]
    send(1, lambda o: s2_ref.at[place(o)[0]], r2_ref, ABOVE + PLANE)

    def geometry(at, slots):
        width = slots.shape[1]
        lanes = slice(at, at + width)
        vx, vy, vz = slots[0:1], slots[1:2], slots[2:3]
        r_sq = vx * vx + vy * vy + vz * vz + 0.04
        inv = lax.rsqrt(r_sq)
        r = r_sq * inv
        ux, uy, uz = vx * inv, vy * inv, vz * inv
        geo_ref[0:1, lanes] = ux
        geo_ref[1:2, lanes] = uy
        geo_ref[2:3, lanes] = uz
        geo_ref[3:4, lanes] = inv
        harm = [
            ROOT3 * ux,
            ROOT3 * uy,
            ROOT3 * uz,
            ROOT15 * ux * uy,
            ROOT15 * uy * uz,
            0.5 * ROOT5 * (3.0 * uz * uz - 1.0),
            ROOT15 * ux * uz,
            0.5 * ROOT15 * (ux * ux - uy * uy),
        ]
        for m in range(8):
            y_ref[m, :, lanes] = jnp.broadcast_to(0.5 * harm[m], (8, width))
        x = r * 0.25
        order = (iota((8, width), 0) + 1).astype(f32)
        phase = order * x
        near = jnp.floor(phase + 0.5)
        part = phase - near
        sign = 1.0 - 2.0 * (near - 2.0 * jnp.floor(near * 0.5))
        angle = part * math.pi
        square = angle * angle
        sin = 1.0
        for k in (14, 12, 10, 8, 6, 4, 2):
            sin = 1.0 - square * sin * (1.0 / (k * (k + 1)))
        sin = sign * angle * sin
        cos = 1.0
        for k in (14, 12, 10, 8, 6, 4, 2):
            cos = 1.0 - square * cos * (1.0 / (k * (k - 1)))
        cos = sign * cos
        gap = 1.0 - x * x
        within = x < 1.0
        env = jnp.where(within, gap * gap, 0.0)
        env_d = jnp.where(within, -x * gap, 0.0)
        scale = math.sqrt(0.5)
        base = scale * sin * inv
        basis = base * env
        basis_d = (scale * (math.pi / 4.0) * order * cos * inv - base * inv) * env + base * env_d
        wide = jnp.concatenate([basis, basis_d], axis=1)
        hi = wide.astype(bf16).astype(f32)
        lo = wide - hi
        return jnp.concatenate([hi, lo, hi, jnp.zeros_like(hi)], axis=0).astype(bf16)

    def radial(at, layer, basis):
        width = basis.shape[1] // 2
        z = dot(win_ref[layer], basis)
        slope, z = z[:, width:], z[:, :width]
        gate = 1.0 / (1.0 + jnp.exp(-z))
        hidden = z * gate
        hidden_d = gate * (1.0 + z * (1.0 - gate)) * slope
        for half, x in enumerate((hidden, hidden_d)):
            hi, lo = split(x)
            rad_ref[half * 384 : (half + 1) * 384, at : at + width] = dot(
                wout_ref[layer], jnp.concatenate([hi, lo, hi], axis=0)
            )

    def tiles_of(at, width, count, tile):
        return [slice(at + k * width + tile * 128, at + k * width + tile * 128 + 128) for k in range(count)]

    def moments(first, lanes, y_shift, folded):
        weighted = []
        for s in lanes:
            m = m_ref[pl.ds(first, 8), s]
            weighted.append([rad_ref[pl.ds(k * 128 + first, 8), s] * m for k in range(3)])
        out = []
        for n in range(9):
            total = None
            for s, w in zip(lanes, weighted):
                y = 0.5 if n == 0 else y_ref[n - 1, :, s.start - y_shift : s.stop - y_shift]
                x = y * w[DEGREE[n]]
                total = x if total is None else total + x
            out.append(total + pltpu.roll(total, 64, 1) if folded else total)
        return out

    def squares_of(a):
        return (
            a[0] * a[0],
            a[1] * a[1] + a[2] * a[2] + a[3] * a[3],
            a[4] * a[4] + a[5] * a[5] + a[6] * a[6] + a[7] * a[7] + a[8] * a[8],
        )

    def forward(parts, folded):
        def step(i, carry):
            first = pl.multiple_of(i * 8, 8)
            for lanes, a_at, inv_at in parts:
                a = moments(first, lanes, 0, folded)
                for n in range(9):
                    a_ref[pl.ds(n * 128 + first, 8), a_at : a_at + 128] = a[n]
                b = squares_of(a)
                cols = slice(inv_at, inv_at + 128)
                inv_ref[pl.ds(first, 8), cols] = a[0]
                inv_ref[pl.ds(128 + first, 8), cols] = b[0]
                inv_ref[pl.ds(256 + first, 8), cols] = b[1] * (1.0 / 3.0)
                inv_ref[pl.ds(384 + first, 8), cols] = b[2] * (1.0 / 5.0)
            return carry

        lax.fori_loop(0, CHAN // 8, step, 0, unroll=2)

    def moment_grads(first, a, grads, g_at):
        cols = slice(g_at, g_at + 128)
        factors = [
            2.0 * grads[pl.ds(128 + first, 8), cols],
            (2.0 / 3.0) * grads[pl.ds(256 + first, 8), cols],
            (2.0 / 5.0) * grads[pl.ds(384 + first, 8), cols],
        ]
        out = [x * factors[DEGREE[n]] for n, x in enumerate(a)]
        out[0] = out[0] + grads[pl.ds(first, 8), cols]
        return out

    def slot_grads(da, s, y_shift):
        y = [None] + [y_ref[n - 1, :, s.start - y_shift : s.stop - y_shift] for n in range(1, 9)]
        return [
            0.5 * da[0],
            da[1] * y[1] + da[2] * y[2] + da[3] * y[3],
            (da[4] * y[4] + da[5] * y[5]) + (da[6] * y[6] + da[7] * y[7]) + da[8] * y[8],
        ]

    def next_layer(parts):
        def step(i, energies):
            first = pl.multiple_of(i * 8, 8)
            out = []
            for (lanes, a_at, t_at), energy in zip(parts, energies):
                a = moments(first, lanes, NEXT, False)
                b = squares_of(a)
                cols = slice(t_at, t_at + 128)
                out.append(
                    energy
                    + a[0] * tl_ref[pl.ds(first, 8), cols]
                    + b[0] * tl_ref[pl.ds(128 + first, 8), cols]
                    + b[1] * ((1.0 / 3.0) * tl_ref[pl.ds(256 + first, 8), cols])
                    + b[2] * ((1.0 / 5.0) * tl_ref[pl.ds(384 + first, 8), cols])
                )
                da = moment_grads(first, a, tl_ref, t_at)
                for n in range(9):
                    a_ref[pl.ds(n * 128 + first, 8), a_at : a_at + 128] = da[n]
                for s in lanes:
                    dw = slot_grads(da, s, NEXT)
                    rad = [rad_ref[pl.ds(j * 128 + first, 8), s] for j in range(3)]
                    dm_ref[pl.ds(first, 8), s.start - NEXT : s.stop - NEXT] = (
                        dw[0] * rad[0] + dw[1] * rad[1] + dw[2] * rad[2]
                    )
            return tuple(out)

        zero = jnp.zeros((8, 128), f32)
        return lax.fori_loop(0, CHAN // 8, step, (zero,) * len(parts), unroll=2)

    def backward(lanes, a_at, y_shift, grads=None, g_at=0):
        def step(i, totals):
            first = pl.multiple_of(i * 8, 8)
            da = [a_ref[pl.ds(n * 128 + first, 8), a_at : a_at + 128] for n in range(9)]
            if grads is not None:
                da = moment_grads(first, da, grads, g_at)
            out = []
            for k, s in enumerate(lanes):
                m = m_ref[pl.ds(first, 8), s]
                weighted = [rad_ref[pl.ds(j * 128 + first, 8), s] * m for j in range(3)]
                for n in range(1, 9):
                    out.append(totals[9 * k + n - 1] + da[n] * weighted[DEGREE[n]])
                dw = slot_grads(da, s, y_shift)
                slope = [rad_ref[pl.ds(384 + j * 128 + first, 8), s] for j in range(3)]
                slope = dw[0] * slope[0] + dw[1] * slope[1] + dw[2] * slope[2]
                out.append(totals[9 * k + 8] + slope * m)
            return tuple(out)

        zero = jnp.zeros((8, 128), f32)
        totals = lax.fori_loop(0, CHAN // 8, step, (zero,) * (9 * len(lanes)))
        for k, s in enumerate(lanes):
            for n in range(9):
                red_ref[n : n + 1, s] = jnp.sum(totals[9 * k + n], axis=0, keepdims=True)

    def vector_grads(at, width, y_shift):
        lanes = slice(at, at + width)
        geo = slice(at - y_shift, at - y_shift + width)
        g = [None] + [0.5 * red_ref[n : n + 1, lanes] for n in range(8)]
        slope = red_ref[8:9, lanes]
        ux, uy, uz, inv = (geo_ref[n : n + 1, geo] for n in range(4))
        gx = ROOT3 * g[1] + ROOT15 * (uy * g[4] + uz * g[7] + ux * g[8])
        gy = ROOT3 * g[2] + ROOT15 * (ux * g[4] + uz * g[5] - uy * g[8])
        gz = ROOT3 * g[3] + ROOT15 * (uy * g[5] + ux * g[7]) + (3.0 * ROOT5) * uz * g[6]
        along = slope - (ux * gx + uy * gy + uz * gz) * inv
        return [gx * inv + ux * along, gy * inv + uy * along, gz * inv + uz * along]

    route_row = route_row.astype(f32)
    for g in range(8):
        mine = column(route_row[:, g * 128 : (g + 1) * 128])
        route_t_ref[g * 128 : (g + 1) * 128, :] = ones_where(
            (iota((128, ATOMS), 1) + 1).astype(f32) == mine
        )
    own_tiles = [tiles_of(OWN, ATOMS, 4, t) for t in range(2)]
    near_tiles = tiles_of(NEAR, 128, 4, 0)
    far_tiles = tiles_of(FAR, 128, 2, 0)
    next_tiles = [tiles_of(NEXT, ATOMS, 4, t) for t in range(2)]
    basis_own = geometry(OWN, slots_own)
    radial(OWN, 0, basis_own)
    m_ref[:, OWN : OWN + SLOTS] = dot(up_kinds, kind_hot(slots_own[3:4])) * live4
    forward([(own_tiles[0], 0, 0), (own_tiles[1], 128, 128)], False)
    skip = dot(skip_kinds, kind_hot(full[3:4, :]))
    first_own = skip[:, :ATOMS] + dot3(mix0_ref[0], mix0_ref[1], inv_ref[...])
    radial(NEXT, 1, basis_own)
    own_part = gathered(dot3(up1_ref[0], up1_ref[1], first_own), hot_ref[0:ATOMS, :], 2)

    wait_plane(1, r2_ref)

    def summed(group):
        total = jnp.zeros((16, 128), f32)
        for o in group:
            total = total + jnp.where(quarter == place(negated(o))[1], r2_ref[SLOT[o]], 0.0)
        return total

    near = summed(PLANE)
    slots_near = jnp.concatenate([near[4 * k : 4 * k + 4] for k in range(4)], axis=1)
    radial(NEAR, 0, geometry(NEAR, slots_near))
    m_ref[:, NEAR:FAR] = dot(up_kinds, kind_hot(slots_near[3:4]))
    forward([(near_tiles, 256, 0)], False)
    mixed_near = dot3(mix0_ref[0], mix0_ref[1], inv_ref[:, 0:128])
    wait_above(1, r2_ref)
    far = summed(ABOVE)
    far = far + pltpu.roll(far, 64, 1)
    slots_far = jnp.concatenate(
        [
            jnp.where(lane < 64, far[0:4], far[4:8]),
            jnp.where(lane < 64, far[8:12], far[12:16]),
        ],
        axis=1,
    )
    radial(FAR, 0, geometry(FAR, slots_far))
    m_ref[:, FAR:NEXT] = dot(up_kinds, kind_hot(slots_far[3:4]))
    forward([(far_tiles, 384, 128)], True)
    mixed_far = dot3(mix0_ref[0], mix0_ref[1], inv_ref[:, 128:256])
    first_ghost = skip[:, ATOMS:] + jnp.concatenate([mixed_near, mixed_far], axis=1)

    projected = dot3(up1_ref[0], up1_ref[1], first_ghost)
    m_ref[:, NEXT:LANES] = (own_part + gathered(projected, hot_ref[ATOMS:TABLE, :], 2)) * live4
    energies = next_layer([(next_tiles[0], 512, 0), (next_tiles[1], 640, 128)])
    energy_ref[...] = jnp.sum(dl_ref[...] * first_own, axis=0, keepdims=True) + jnp.sum(
        jnp.concatenate(energies, axis=1), axis=0, keepdims=True
    )
    back = gathered(dm_ref[...], hot_t_ref[...], 2)
    back = dot3(up1t_ref[0], up1t_ref[1], back)

    back_far = back[:, 384:512]
    back_far = back_far + pltpu.roll(back_far, 64, 1)
    dinv_ref[:, 0:128] = dot3(mix0t_ref[0], mix0t_ref[1], back_far)
    backward(far_tiles, 384, 0, dinv_ref, 0)
    grads_far = vector_grads(FAR, 256, 0)
    s3_ref[...] = jnp.zeros((2, 16, 128), f32)
    for n in range(3):
        for k in range(4):
            x = grads_far[n][:, (k // 2) * 128 : (k // 2) * 128 + 128]
            other = pltpu.roll(x, 64, 1)
            low = lane < 64 if k % 2 == 0 else lane >= 64
            s3_ref[1, 4 * k + n : 4 * k + n + 1, :] = jnp.where(low, x, other)
    send(2, lambda o: s3_ref.at[1], r3_ref, ABOVE)
    dinv_ref[:, 128:256] = dot3(mix0t_ref[0], mix0t_ref[1], back[:, 256:384])
    backward(near_tiles, 256, 0, dinv_ref, 128)
    grads_near = vector_grads(NEAR, 512, 0)
    for n in range(3):
        for k in range(4):
            s3_ref[0, 4 * k + n : 4 * k + n + 1, :] = grads_near[n][:, k * 128 : (k + 1) * 128]
    send(2, lambda o: s3_ref.at[0], r3_ref, PLANE)

    dinv_ref[...] = dot3(mix0t_ref[0], mix0t_ref[1], back[:, :ATOMS] + dl_ref[...])
    for t in range(2):
        backward(own_tiles[t], 128 * t, 0, dinv_ref, 128 * t)
        backward(next_tiles[t], 512 + 128 * t, NEXT)
    grads = [a + b for a, b in zip(vector_grads(OWN, SLOTS, 0), vector_grads(NEXT, SLOTS, NEXT))]
    grads = jnp.concatenate(grads + [jnp.zeros((5, SLOTS), f32)], axis=0)

    def table_grads(x):
        out = gathered(x, hot_t_ref[...], 2)
        own = out[:, :ATOMS]
        for k in range(4):
            own = own - x[:, k * ATOMS : (k + 1) * ATOMS]
        return own, out[:, ATOMS:]

    def merged(inbox, group, tiles):
        tiles = dict.fromkeys(tiles)
        for o in group:
            g, q = place(o)
            x = jnp.where(quarter == q, inbox[SLOT[o]], 0.0)
            tiles[g] = x if tiles[g] is None else tiles[g] + x
        return jnp.concatenate([tiles[g] for g in sorted(tiles)], axis=1)

    def returned(stage, inbox):
        wait_plane(stage, inbox)
        out = gathered(merged(inbox, PLANE, range(3)), route_t_ref[0:384, :], 2)
        wait_above(stage, inbox)
        return out + gathered(merged(inbox, ABOVE, range(3, 8)), route_t_ref[384:SLOTS, :], 2)

    own_grads, ghost_grads = table_grads(grads)
    from_ghosts = returned(2, r3_ref)
    from_ghosts = jnp.concatenate([from_ghosts[4 * k : 4 * k + 4] for k in range(4)], axis=1)
    from_ghosts = jnp.concatenate([from_ghosts, jnp.zeros((4, SLOTS), f32)], axis=0)
    more_own, more_ghost = table_grads(from_ghosts)
    ghost_grads = ghost_grads + more_ghost
    tail = ghost_grads[:, 128:256]
    s4_ref[1] = tail + pltpu.roll(tail, 64, 1)
    s4_ref[0] = ghost_grads[:, 0:128]
    send(3, lambda o: s4_ref.at[1 if o[2] else 0], r4_ref, ABOVE + PLANE)
    own_grads = own_grads + more_own
    force_ref[...] = -(own_grads + returned(3, r4_ref))[0:3]
    for stage, inbox in enumerate((r1_ref, r2_ref, r3_ref, r4_ref)):
        copies(stage, inbox).wait_send()


def body(
    sizes,
    positions,
    species,
    live_count,
    send_lists,
    neighbours,
    embed,
    radial_in,
    radial_out,
    w_up,
    w_skip,
    w_mix,
    readout,
):
    vmem = pl.BlockSpec(memory_space=pltpu.VMEM)
    hbm = pl.BlockSpec(memory_space=pltpu.HBM)
    energy, forces = pl.pallas_call(
        functools.partial(kernel, sizes),
        out_shape=(
            jax.ShapeDtypeStruct((1, ATOMS), f32),
            jax.ShapeDtypeStruct((3, ATOMS), f32),
        ),
        in_specs=[hbm] * 12,
        out_specs=(vmem, vmem),
        scratch_shapes=[
            pltpu.VMEM((1, 1), jnp.int32),
            pltpu.VMEM((3, ATOMS), f32),
            pltpu.VMEM((1, ATOMS), jnp.int32),
            pltpu.VMEM((6, 32), jnp.int32),
            pltpu.VMEM((8, 128), jnp.int32),
            pltpu.VMEM((6, 128), f32),
            pltpu.VMEM((2, 128), f32),
            pltpu.VMEM((2, 8, 64), f32),
            pltpu.VMEM((2, 64, 384), f32),
            pltpu.VMEM((2, 128, 128), f32),
            pltpu.VMEM((2, 128, 128), f32),
            pltpu.VMEM((2, 128, 512), f32),
            pltpu.VMEM((8, ATOMS), f32),
            pltpu.VMEM((26, 8, ATOMS), f32),
            pltpu.VMEM((8, 16, 128), f32),
            pltpu.VMEM((26, 16, 128), f32),
            pltpu.VMEM((2, 16, 128), f32),
            pltpu.VMEM((26, 16, 128), f32),
            pltpu.VMEM((2, 8, 128), f32),
            pltpu.VMEM((26, 8, 128), f32),
            pltpu.VMEM((TABLE, SLOTS), bf16),
            pltpu.VMEM((SLOTS, TABLE), bf16),
            pltpu.VMEM((ATOMS, SLOTS), bf16),
            pltpu.VMEM((SLOTS, ATOMS), bf16),
            pltpu.VMEM((2, 64, 32), bf16),
            pltpu.VMEM((2, 384, 192), bf16),
            pltpu.VMEM((2, 128, 512), bf16),
            pltpu.VMEM((2, 512, 128), bf16),
            pltpu.VMEM((2, 128, 128), bf16),
            pltpu.VMEM((2, 128, 128), bf16),
            pltpu.VMEM((512, ATOMS), f32),
            pltpu.VMEM((128, ATOMS), f32),
            pltpu.VMEM((512, ATOMS), f32),
            pltpu.VMEM((768, LANES), f32),
            pltpu.VMEM((128, LANES), f32),
            pltpu.VMEM((1152, 768), f32),
            pltpu.VMEM((8, 8, NEXT), f32),
            pltpu.VMEM((512, ATOMS), f32),
            pltpu.VMEM((128, SLOTS), f32),
            pltpu.VMEM((16, LANES), f32),
            pltpu.VMEM((8, NEXT), f32),
            pltpu.VMEM((16, ATOMS), f32),
            pltpu.SemaphoreType.DMA((12,)),
            pltpu.SemaphoreType.DMA((4,)),
            pltpu.SemaphoreType.DMA((4, 2)),
        ],
        compiler_params=pltpu.CompilerParams(
            collective_id=0, has_side_effects=True, vmem_limit_bytes=VMEM_BYTES
        ),
        name="potential",
    )(
        live_count.reshape(1, 1),
        positions,
        species.reshape(1, ATOMS),
        send_lists,
        neighbours.reshape(8, 128),
        embed.T,
        readout,
        radial_in.transpose(0, 2, 1),
        radial_out.transpose(0, 2, 1),
        w_up,
        w_skip,
        w_mix,
    )
    return energy.reshape(ATOMS), forces


def solution(mesh):
    sizes = {axis: mesh.shape[axis] for axis in AXES}
    split_all = ("gx", "gy", "gz")
    return jax.shard_map(
        functools.partial(body, sizes),
        mesh=mesh,
        in_specs=(
            P(None, split_all),
            P(split_all),
            P(split_all),
            P(None, split_all),
            P(split_all),
            P(),
            P(),
            P(),
            P(),
            P(),
            P(),
            P(),
        ),
        out_specs=(P(split_all), P(None, split_all)),
        check_vma=False,
    )
```

```python
import functools
import itertools
import math

import jax
import jax.numpy as jnp
from jax import lax
from jax.experimental import pallas as pl
from jax.experimental.pallas import tpu as pltpu
from jax.sharding import PartitionSpec as P

AXES = ("gx", "gy", "gz")
MESH = pl.DeviceIdType.MESH
OFFSETS = [o for o in itertools.product((-1, 0, 1), repeat=3) if any(o)]
PLANE = [o for o in OFFSETS if not o[2]]
ABOVE = [o for o in OFFSETS if o[2]]
SLOT = {o: j for j, o in enumerate(PLANE + ABOVE)}
PLANE.sort(key=lambda o: -abs(o[1]))
ABOVE.sort(key=lambda o: -(abs(o[0]) + 2 * abs(o[1])))
f32 = jnp.float32
bf16 = jnp.bfloat16
HIGHEST = lax.Precision.HIGHEST
ATOMS = 256
SLOTS = 1024
CHAN = 128
OWN, NEAR, FAR, NEXT = 0, 1024, 1536, 1792
LANES = 2816
TABLE = 512
VMEM_BYTES = 48 * 1024 * 1024
DEGREE = (0, 1, 1, 1, 2, 2, 2, 2, 2)
ROOT3 = math.sqrt(3.0)
ROOT5 = math.sqrt(5.0)
ROOT15 = math.sqrt(15.0)
X_BRICKS = [(0, 0), (0, -1), (0, 1), (-1, 0), (1, 0), (-1, -1), (1, -1), (-1, 1), (1, 1)]
Y_BRICKS = [-1, 0, 1]


def place(d):
    dx, dy, dz = d
    if dz:
        n = (dx + 1) * 3 + dy + 1
        return 3 + n // 2, (n % 2) * 2 + (0 if dz > 0 else 1)
    if dy:
        return dx + 1, 2 if dy > 0 else 3
    return 0, 0 if dx > 0 else 1


def negated(o):
    return (-o[0], -o[1], -o[2])


def iota(shape, dim):
    return lax.broadcasted_iota(jnp.int32, shape, dim)


def dot(a, b):
    return jnp.dot(a, b, preferred_element_type=f32)


def dot_t(a, b):
    return lax.dot_general(a, b, (((1,), (1,)), ((), ())), preferred_element_type=f32)


def exact_dot(a, b, dim=0):
    return lax.dot_general(
        a, b, (((1,), (dim,)), ((), ())), precision=HIGHEST, preferred_element_type=f32
    )


def split(x):
    hi = x.astype(bf16)
    return hi, (x - hi.astype(f32)).astype(bf16)


def terms(x, count):
    out = []
    for _ in range(count):
        hi = x.astype(bf16).astype(f32)
        out.append(hi)
        x = x - hi
    return jnp.concatenate(out, axis=0).astype(bf16)


def gathered(x, onehot, count):
    rows = x.shape[0]
    wide = dot(terms(x, count), onehot)
    return sum(wide[i * rows : (i + 1) * rows] for i in range(count))


def ones_where(mask):
    return jnp.where(mask, 1.0, 0.0).astype(bf16)


def dot3(a_hi, a_lo, b):
    b_hi, b_lo = split(b)
    return dot(a_hi, b_hi) + (dot(a_hi, b_lo) + dot(a_lo, b_hi))


def column(row):
    eye = iota((128, 128), 0) == iota((128, 128), 1)
    return jnp.sum(jnp.where(eye, row, 0.0), axis=1, keepdims=True)


def kernel(
    sizes,
    count_ref,
    pos_hbm,
    species_hbm,
    sends_hbm,
    neigh_hbm,
    embed_hbm,
    readout_hbm,
    rin_hbm,
    rout_hbm,
    up_hbm,
    skip_hbm,
    mix_hbm,
    energy_ref,
    force_ref,
    pos_ref,
    species_ref,
    sends_ref,
    neigh_ref,
    embed_ref,
    readout_ref,
    rin_ref,
    rout_ref,
    up_ref,
    skip_ref,
    mix_ref,
    own_ref,
    r1_ref,
    s2_ref,
    r2_ref,
    s3_ref,
    r3_ref,
    s4_ref,
    r4_ref,
    hot_ref,
    hot_t_ref,
    route_ref,
    route_t_ref,
    win_ref,
    wout_ref,
    pass_ref,
    pass_t_ref,
    tl_ref,
    dl_ref,
    dinv_ref,
    rad_ref,
    m_ref,
    a_ref,
    y_ref,
    inv_ref,
    dm_ref,
    dw_ref,
    red_ref,
    geo_ref,
    env_ref,
    load_sem,
    send_sem,
    recv_sem,
):
    def device(o):
        out = {}
        for axis, step in zip(AXES, o):
            here = lax.axis_index(axis)
            out[axis] = here if step == 0 else lax.rem(here + (sizes[axis] + step), sizes[axis])
        return out

    barrier = pltpu.get_barrier_semaphore()
    for o in ABOVE + PLANE:
        pl.semaphore_signal(barrier, inc=1, device_id=device(o), device_id_type=MESH)
    loads = [
        pltpu.make_async_copy(src, dst, load_sem.at[i])
        for i, (src, dst) in enumerate(
            (
                (pos_hbm, pos_ref),
                (species_hbm, species_ref),
                (sends_hbm, sends_ref),
                (neigh_hbm, neigh_ref),
                (mix_hbm, mix_ref),
                (up_hbm, up_ref),
                (rout_hbm, rout_ref),
                (skip_hbm, skip_ref),
                (embed_hbm, embed_ref),
                (readout_hbm, readout_ref),
                (rin_hbm, rin_ref),
            )
        )
    ]
    for load in loads:
        load.start()

    def send(stage, source, inbox, group):
        for o in group:
            pltpu.make_async_remote_copy(
                src_ref=source(o),
                dst_ref=inbox.at[SLOT[negated(o)]],
                send_sem=send_sem.at[stage],
                recv_sem=recv_sem.at[stage, 1 if o[2] else 0],
                device_id=device(o),
                device_id_type=MESH,
            ).start()

    def copies(stage, inbox, part=0):
        return pltpu.make_async_remote_copy(
            src_ref=inbox,
            dst_ref=inbox,
            send_sem=send_sem.at[stage],
            recv_sem=recv_sem.at[stage, part],
            device_id=device((1, 0, 0)),
            device_id_type=MESH,
        )

    def wait_plane(stage, inbox):
        copies(stage, inbox.at[0:8], 0).wait_recv()

    def wait_above(stage, inbox):
        copies(stage, inbox.at[8:26], 1).wait_recv()

    for load in loads[:3]:
        load.wait()
    own_ref[0:3, :] = pos_ref[...]
    own_ref[3:4, :] = species_ref[...].astype(f32)
    lists = sends_ref[...].astype(f32)
    lists = jnp.concatenate([lists, lists, lists, lists], axis=1)
    own_ref[4:8, 0:128] = lists[0:4]
    own_ref[4:6, 128:256] = lists[4:6]
    own_ref[6:8, 128:256] = jnp.zeros((2, 128), f32)

    lane = iota((1, 128), 1)
    quarter = lane // 32
    live = jnp.where(iota((1, ATOMS), 1) < count_ref[0], 1.0, 0.0)
    live4 = jnp.concatenate([live] * 4, axis=1)

    pl.semaphore_wait(barrier, len(OFFSETS))
    send(0, lambda o: own_ref, r1_ref, ABOVE + PLANE)

    loads[3].wait()
    neigh = neigh_ref[...]
    halves = jnp.concatenate([neigh >> 8, neigh & 255], axis=0).astype(f32).astype(bf16)
    sel_row = iota((128, SLOTS), 0)
    sel_col = iota((128, SLOTS), 1)
    chosen = dot(halves, ones_where(sel_row == 4 * (sel_col & 31) + (sel_col >> 8)))
    chosen = chosen[0:8] * 256.0 + chosen[8:16]
    group = iota((8, SLOTS), 0) == ((iota((8, SLOTS), 1) & 255) >> 5)
    neigh_row = jnp.sum(jnp.where(group, chosen, 0.0), axis=0, keepdims=True).astype(jnp.int32)

    def hot_step(i, carry):
        first = pl.multiple_of(i * 64, 64)
        hot_ref[pl.ds(first, 64), :] = ones_where(iota((64, SLOTS), 0) + i * 64 == neigh_row)
        return carry

    lax.fori_loop(0, TABLE // 64, hot_step, 0)

    def hot_t_step(i, carry):
        first = pl.multiple_of(i * 128, 128)
        slot = iota((128, 128), 0) + i * 128
        sel = ones_where(iota((128, 128), 1) == 4 * (slot & 31) + (slot >> 8))
        mine = dot_t(sel, halves)
        place_at = iota((128, 16), 1)
        mine = mine * jnp.where(place_at < 8, 256.0, 1.0)
        in_group = (place_at & 7) == (((iota((128, 16), 0) + i * 128) & 255) >> 5)
        mine = jnp.sum(jnp.where(in_group, mine, 0.0), axis=1, keepdims=True)
        hot_t_ref[pl.ds(first, 128), :] = ones_where(iota((128, TABLE), 1).astype(f32) == mine)
        return carry


    lax.fori_loop(0, SLOTS // 128, hot_t_step, 0)
    for load in loads[4:]:
        load.wait()
    wide_lane = iota((128, 128), 1)

    def stacked(x):
        hi = x.astype(bf16).astype(f32)
        return jnp.concatenate([hi, hi, x - hi, jnp.zeros_like(x)], axis=0)

    for layer in range(2):
        rin = jnp.concatenate([stacked(rin_ref[layer]), jnp.zeros((96, 64), f32)], axis=0)
        rin = jnp.concatenate([rin, jnp.zeros((128, 64), f32)], axis=1).T
        win_ref[layer] = rin[:64, :32].astype(bf16)
        wout_ref[layer] = stacked(rout_ref[layer]).T[:, :192].astype(bf16)
    between = exact_dot(up_ref[1], mix_ref[0])
    pass_ref[0], pass_ref[1] = split(between)
    pass_t_ref[0], pass_t_ref[1] = split(between.T)
    embed = jnp.concatenate([embed_ref[...], jnp.zeros((2, 128), f32)], axis=0)
    embed3 = jnp.concatenate([embed, embed, embed, jnp.zeros((104, 128), f32)], axis=0)

    def three_terms(x):
        hi = x.astype(bf16).astype(f32)
        mid = (x - hi).astype(bf16).astype(f32)
        lo = x - hi - mid
        x = jnp.where(wide_lane < 8, hi, jnp.where(wide_lane < 16, mid, lo))
        return x[:, :32].astype(bf16)

    up_kinds = three_terms(exact_dot(up_ref[0], embed3, 1))
    skip_kinds = exact_dot(skip_ref[0], embed3, 1)
    skip_up_kinds = three_terms(exact_dot(up_ref[1], skip_kinds))
    ro1 = readout_ref[1:2, :]
    direct = readout_ref[0:1, :] + exact_dot(ro1, skip_ref[1])
    kinds_energy = jnp.broadcast_to(exact_dot(direct, skip_kinds), (128, 128))
    kinds_energy = three_terms(kinds_energy)[0:16]
    for ref, mixed in ((dl_ref, exact_dot(direct, mix_ref[0])), (tl_ref, exact_dot(ro1, mix_ref[1]))):
        for k in range(4):
            ref[k * 128 : (k + 1) * 128, :] = column(mixed[:, k * 128 : (k + 1) * 128]) * live

    def kind_hot(row):
        width = row.shape[1]
        sub = iota((32, width), 0)
        return ones_where(((sub & 7).astype(f32) == row) & (sub < 24))

    wait_plane(0, r1_ref)
    wait_above(0, r1_ref)

    def table(o):
        return r1_ref[SLOT[o]] if any(o) else own_ref[...]

    def rows(o, which):
        ref = r1_ref.at[SLOT[o]] if any(o) else own_ref
        if which < 4:
            return ref[4 + which : 5 + which, 0:128]
        return ref[which : which + 1, 128:256]

    def by_quarter(parts):
        parts = list(parts) + [parts[-1]] * (4 - len(parts))
        out = parts[3]
        for q in (2, 1, 0):
            out = jnp.where(quarter == q, parts[q], out)
        return out

    def pick(tables, indices, section):
        index = by_quarter(indices).astype(jnp.int32)
        depth = tables[0].shape[1]
        onehot = ones_where(iota((depth, 128), 0) == index)
        stack = jnp.concatenate(tables, axis=0)
        out = gathered(stack, onehot, 3)
        out = by_quarter([out[8 * i : 8 * i + 8] for i in range(len(tables))])
        shift = jnp.where((quarter & 1) == 0, -4.0, 4.0)
        return out + jnp.where(iota((8, 128), 0) == section, shift, 0.0)

    x_tiles = []
    for t in range(0, 9, 2):
        tables, indices = [], []
        for oy, oz in X_BRICKS[t : t + 2]:
            tables += [table((-1, oy, oz)), table((1, oy, oz))]
            indices += [rows((-1, oy, oz), 1), rows((1, oy, oz), 0)]
        x_tiles.append(pick(tables, indices, 0))

    y_tiles = []
    for t in range(0, 3, 2):
        tables, indices = [], []
        for oz in Y_BRICKS[t : t + 2]:
            for oy, which in ((-1, 3), (1, 2)):
                at = X_BRICKS.index((oy, oz))
                tables.append(jnp.concatenate([table((0, oy, oz)), x_tiles[at // 2]], axis=1))
                index = rows((0, oy, oz), which)
                indices.append(index + jnp.where(index < 256.0, 0.0, 64.0 * (at % 2)))
        y_tiles.append(pick(tables, indices, 1))

    tables, indices = [], []
    for oz, which in ((-1, 5), (1, 4)):
        at = X_BRICKS.index((0, oz))
        at_y = Y_BRICKS.index(oz)
        tables.append(
            jnp.concatenate([table((0, 0, oz)), x_tiles[at // 2], y_tiles[at_y // 2]], axis=1)
        )
        index = rows((0, 0, oz), which)
        far = jnp.where(index < 320.0, 64.0 * (at % 2), 64.0 + 64.0 * (at_y % 2))
        indices.append(index + jnp.where(index < 256.0, 0.0, far))
    z_tile = pick(tables, indices, 2)
    ghost0 = jnp.where(lane < 64, x_tiles[0], y_tiles[0])
    ghost1 = jnp.where(lane < 64, z_tile, 0.0)
    full = jnp.concatenate([own_ref[...], ghost0, ghost1], axis=1)

    here = (0, 0, 0)
    direct_lower = rows(here, 1) + 1.0
    direct_upper = rows(here, 0) + 1.0

    def own_only(index):
        return jnp.where(index < 256.0, index + 1.0, 0.0)

    def looked_up(index, lowest, offset):
        inside = (index >= lowest) & (index < lowest + 32.0)
        return jnp.where(inside, index + offset, -1.0)

    def compose(keys, entries):
        depth = entries.shape[1]
        onehot = ones_where(iota((depth, keys.shape[1]), 0) == keys.astype(jnp.int32))
        entries = jnp.broadcast_to(entries, (8, depth)).astype(bf16)
        return dot(entries, onehot)[0:1]

    zero_row = jnp.zeros((1, 128), f32)
    x_entries = by_quarter([direct_lower, direct_upper, zero_row, zero_row])
    keys = []
    for dx, lowest in ((-1, 288.0), (1, 256.0)):
        o = (dx, 0, 0)
        parts = [looked_up(rows(o, which), lowest, -256.0) for which in (3, 2)]
        keys.append(by_quarter([zero_row - 1.0, zero_row - 1.0] + parts))
    found = compose(jnp.concatenate(keys, axis=1), x_entries)
    route = [
        by_quarter([direct_lower, direct_upper, found[:, 0:128], found[:, 0:128]]),
        by_quarter([zero_row, zero_row, own_only(rows(here, 3)), own_only(rows(here, 2))]),
        by_quarter([zero_row, zero_row, found[:, 128:256], found[:, 128:256]]),
    ]
    keys, directs = [], []
    for n in range(0, 10, 2):
        key, direct = [], []
        for at in (n, n + 1):
            dx, dy = at // 3 - 1, at % 3 - 1
            for which in (5, 4):
                if at > 8:
                    key.append(zero_row - 1.0)
                    direct.append(zero_row)
                elif dx == 0 and dy == 0:
                    key.append(zero_row - 1.0)
                    direct.append(own_only(rows(here, which)))
                else:
                    if dy:
                        lowest = 320.0 if dy > 0 else 352.0
                        offset = 128.0 * (dx + 1) - 256.0
                    else:
                        lowest = 256.0 if dx > 0 else 288.0
                        offset = -256.0
                    key.append(looked_up(rows((dx, dy, 0), which), lowest, offset))
                    direct.append(zero_row)
        keys.append(by_quarter(key))
        directs.append(by_quarter(direct))
    found = compose(jnp.concatenate(keys, axis=1), jnp.concatenate(route, axis=1))
    found = found + jnp.concatenate(directs, axis=1)
    route_row = jnp.concatenate(route + [found], axis=1).astype(jnp.int32)

    def route_step(i, carry):
        first = pl.multiple_of(i * 64, 64)
        route_ref[pl.ds(first, 64), :] = ones_where(iota((64, SLOTS), 0) + (i * 64 + 1) == route_row)
        return carry

    lax.fori_loop(0, ATOMS // 64, route_step, 0)

    centres = jnp.concatenate([full[:, :ATOMS]] * 4, axis=1)
    is_coord = iota((8, SLOTS), 0) < 3
    moved = gathered(full, hot_ref[...], 3)
    slots_own = moved - jnp.where(is_coord, centres, 0.0)
    for k in range(4):
        env_ref[4 * k : 4 * k + 4, :] = slots_own[0:4, k * ATOMS : (k + 1) * ATOMS]
    spread_env = gathered(env_ref[...], route_ref[...], 3)
    for g in range(8):
        s2_ref[g] = spread_env[:, g * 128 : (g + 1) * 128]
    send(1, lambda o: s2_ref.at[place(o)[0]], r2_ref, ABOVE + PLANE)

    def geometry(at, slots):
        width = slots.shape[1]
        lanes = slice(at, at + width)
        vx, vy, vz = slots[0:1], slots[1:2], slots[2:3]
        r_sq = vx * vx + vy * vy + vz * vz + 0.04
        inv = lax.rsqrt(r_sq)
        r = r_sq * inv
        ux, uy, uz = vx * inv, vy * inv, vz * inv
        geo_ref[0:1, lanes] = ux
        geo_ref[1:2, lanes] = uy
        geo_ref[2:3, lanes] = uz
        geo_ref[3:4, lanes] = inv
        harm = [
            ROOT3 * ux,
            ROOT3 * uy,
            ROOT3 * uz,
            ROOT15 * ux * uy,
            ROOT15 * uy * uz,
            0.5 * ROOT5 * (3.0 * uz * uz - 1.0),
            ROOT15 * ux * uz,
            0.5 * ROOT15 * (ux * ux - uy * uy),
        ]
        for m in range(8):
            y_ref[m, :, lanes] = jnp.broadcast_to(0.5 * harm[m], (8, width))
        x = r * 0.25
        order = (iota((8, width), 0) + 1).astype(f32)
        phase = order * x
        near = jnp.floor(phase + 0.5)
        part = phase - near
        sign = 1.0 - 2.0 * (near - 2.0 * jnp.floor(near * 0.5))
        angle = part * math.pi
        square = angle * angle
        sin = 1.0
        for k in (14, 12, 10, 8, 6, 4, 2):
            sin = 1.0 - square * sin * (1.0 / (k * (k + 1)))
        sin = sign * angle * sin
        cos = 1.0
        for k in (14, 12, 10, 8, 6, 4, 2):
            cos = 1.0 - square * cos * (1.0 / (k * (k - 1)))
        cos = sign * cos
        gap = 1.0 - x * x
        within = x < 1.0
        env = jnp.where(within, gap * gap, 0.0)
        env_d = jnp.where(within, -x * gap, 0.0)
        scale = math.sqrt(0.5)
        base = scale * sin * inv
        basis = base * env
        basis_d = (scale * (math.pi / 4.0) * order * cos * inv - base * inv) * env + base * env_d
        wide = jnp.concatenate([basis, basis_d], axis=1)
        hi = wide.astype(bf16).astype(f32)
        lo = wide - hi
        return jnp.concatenate([hi, lo, hi, jnp.zeros_like(hi)], axis=0).astype(bf16)

    def radial(at, layer, basis):
        width = basis.shape[1] // 2
        z = dot(win_ref[layer], basis)
        slope, z = z[:, width:], z[:, :width]
        gate = 1.0 / (1.0 + jnp.exp(-z))
        hidden = z * gate
        hidden_d = gate * (1.0 + z * (1.0 - gate)) * slope
        for half, x in enumerate((hidden, hidden_d)):
            hi, lo = split(x)
            rad_ref[half * 384 : (half + 1) * 384, at : at + width] = dot(
                wout_ref[layer], jnp.concatenate([hi, lo, hi], axis=0)
            )

    def tiles_of(at, width, count, tile):
        return [slice(at + k * width + tile * 128, at + k * width + tile * 128 + 128) for k in range(count)]

    def harmonics_of(s, y_shift):
        return [None] + [y_ref[n, :, s.start - y_shift : s.stop - y_shift] for n in range(8)]

    def moments(firsts, lanes, y_shift, folded):
        out = [[None] * 9 for _ in firsts]
        for s in lanes:
            y = harmonics_of(s, y_shift)
            for c, first in enumerate(firsts):
                m = m_ref[pl.ds(first, 8), s]
                weighted = [rad_ref[pl.ds(k * 128 + first, 8), s] * m for k in range(3)]
                for n in range(9):
                    x = (0.5 if n == 0 else y[n]) * weighted[DEGREE[n]]
                    out[c][n] = x if out[c][n] is None else out[c][n] + x
        if folded:
            out = [[x + pltpu.roll(x, 64, 1) for x in a] for a in out]
        return out

    def squares_of(a):
        return (
            a[0] * a[0],
            a[1] * a[1] + a[2] * a[2] + a[3] * a[3],
            a[4] * a[4] + a[5] * a[5] + a[6] * a[6] + a[7] * a[7] + a[8] * a[8],
        )

    def forward(parts, folded):
        def step(i, carry):
            firsts = [pl.multiple_of(i * 16 + 8 * c, 8) for c in range(2)]
            for lanes, a_at, inv_at in parts:
                cols = slice(inv_at, inv_at + 128)
                for first, a in zip(firsts, moments(firsts, lanes, 0, folded)):
                    for n in range(9):
                        a_ref[pl.ds(n * 128 + first, 8), a_at : a_at + 128] = a[n]
                    b = squares_of(a)
                    inv_ref[pl.ds(first, 8), cols] = a[0]
                    inv_ref[pl.ds(128 + first, 8), cols] = b[0]
                    inv_ref[pl.ds(256 + first, 8), cols] = b[1] * (1.0 / 3.0)
                    inv_ref[pl.ds(384 + first, 8), cols] = b[2] * (1.0 / 5.0)
            return carry

        lax.fori_loop(0, CHAN // 16, step, 0, unroll=2)

    def moment_grads(first, a, grads, g_at):
        cols = slice(g_at, g_at + 128)
        factors = [
            2.0 * grads[pl.ds(128 + first, 8), cols],
            (2.0 / 3.0) * grads[pl.ds(256 + first, 8), cols],
            (2.0 / 5.0) * grads[pl.ds(384 + first, 8), cols],
        ]
        out = [x * factors[DEGREE[n]] for n, x in enumerate(a)]
        out[0] = out[0] + grads[pl.ds(first, 8), cols]
        return out

    def slot_grads(da, y):
        return [
            0.5 * da[0],
            da[1] * y[1] + da[2] * y[2] + da[3] * y[3],
            (da[4] * y[4] + da[5] * y[5]) + (da[6] * y[6] + da[7] * y[7]) + da[8] * y[8],
        ]

    def next_layer(parts):
        def step(i, energies):
            firsts = [pl.multiple_of(i * 16 + 8 * c, 8) for c in range(2)]
            out = []
            for (lanes, a_at, t_at), energy in zip(parts, energies):
                cols = slice(t_at, t_at + 128)
                grads = []
                for first, a in zip(firsts, moments(firsts, lanes, NEXT, False)):
                    b = squares_of(a)
                    energy = (
                        energy
                        + a[0] * tl_ref[pl.ds(first, 8), cols]
                        + b[0] * tl_ref[pl.ds(128 + first, 8), cols]
                        + b[1] * ((1.0 / 3.0) * tl_ref[pl.ds(256 + first, 8), cols])
                        + b[2] * ((1.0 / 5.0) * tl_ref[pl.ds(384 + first, 8), cols])
                    )
                    da = moment_grads(first, a, tl_ref, t_at)
                    for n in range(9):
                        a_ref[pl.ds(n * 128 + first, 8), a_at : a_at + 128] = da[n]
                    grads.append(da)
                out.append(energy)
                for s in lanes:
                    y = harmonics_of(s, NEXT)
                    at = slice(s.start - NEXT, s.stop - NEXT)
                    for first, da in zip(firsts, grads):
                        dw = slot_grads(da, y)
                        rad = [rad_ref[pl.ds(j * 128 + first, 8), s] for j in range(3)]
                        dm_ref[pl.ds(first, 8), at] = dw[0] * rad[0] + dw[1] * rad[1] + dw[2] * rad[2]
                        for j in range(3):
                            dw_ref[pl.ds(j * 128 + first, 8), at] = dw[j]
            return tuple(out)

        zero = jnp.zeros((8, 128), f32)
        return lax.fori_loop(0, CHAN // 16, step, (zero,) * len(parts))

    def backward(lanes, a_at, y_shift, grads=None, g_at=0):
        def step(i, totals):
            first = pl.multiple_of(i * 8, 8)
            da = [a_ref[pl.ds(n * 128 + first, 8), a_at : a_at + 128] for n in range(9)]
            if grads is not None:
                da = moment_grads(first, da, grads, g_at)
            out = []
            for k, s in enumerate(lanes):
                m = m_ref[pl.ds(first, 8), s]
                weighted = [rad_ref[pl.ds(j * 128 + first, 8), s] * m for j in range(3)]
                for n in range(1, 9):
                    out.append(totals[9 * k + n - 1] + da[n] * weighted[DEGREE[n]])
                if grads is None:
                    at = slice(s.start - y_shift, s.stop - y_shift)
                    dw = [dw_ref[pl.ds(j * 128 + first, 8), at] for j in range(3)]
                else:
                    dw = slot_grads(da, harmonics_of(s, y_shift))
                slope = [rad_ref[pl.ds(384 + j * 128 + first, 8), s] for j in range(3)]
                slope = dw[0] * slope[0] + dw[1] * slope[1] + dw[2] * slope[2]
                out.append(totals[9 * k + 8] + slope * m)
            return tuple(out)

        zero = jnp.zeros((8, 128), f32)
        totals = lax.fori_loop(0, CHAN // 8, step, (zero,) * (9 * len(lanes)), unroll=4)
        for k, s in enumerate(lanes):
            for n in range(9):
                red_ref[n : n + 1, s] = jnp.sum(totals[9 * k + n], axis=0, keepdims=True)

    def vector_grads(at, width, y_shift):
        lanes = slice(at, at + width)
        geo = slice(at - y_shift, at - y_shift + width)
        g = [None] + [0.5 * red_ref[n : n + 1, lanes] for n in range(8)]
        slope = red_ref[8:9, lanes]
        ux, uy, uz, inv = (geo_ref[n : n + 1, geo] for n in range(4))
        gx = ROOT3 * g[1] + ROOT15 * (uy * g[4] + uz * g[7] + ux * g[8])
        gy = ROOT3 * g[2] + ROOT15 * (ux * g[4] + uz * g[5] - uy * g[8])
        gz = ROOT3 * g[3] + ROOT15 * (uy * g[5] + ux * g[7]) + (3.0 * ROOT5) * uz * g[6]
        along = slope - (ux * gx + uy * gy + uz * gz) * inv
        return [gx * inv + ux * along, gy * inv + uy * along, gz * inv + uz * along]

    route_row = route_row.astype(f32)
    for g in range(8):
        mine = column(route_row[:, g * 128 : (g + 1) * 128])
        route_t_ref[g * 128 : (g + 1) * 128, :] = ones_where(
            (iota((128, ATOMS), 1) + 1).astype(f32) == mine
        )
    own_tiles = [tiles_of(OWN, ATOMS, 4, t) for t in range(2)]
    near_tiles = tiles_of(NEAR, 128, 4, 0)
    far_tiles = tiles_of(FAR, 128, 2, 0)
    next_tiles = [tiles_of(NEXT, ATOMS, 4, t) for t in range(2)]
    basis_own = geometry(OWN, slots_own)
    radial(OWN, 0, basis_own)
    m_ref[:, OWN : OWN + SLOTS] = dot(up_kinds, kind_hot(slots_own[3:4])) * live4
    forward([(own_tiles[0], 0, 0), (own_tiles[1], 128, 128)], False)
    kinds = kind_hot(full[3:4, :])
    skip = dot(skip_up_kinds, kinds)
    energy = jnp.sum(dl_ref[...] * inv_ref[...], axis=0, keepdims=True)
    energy = energy + live * dot(kinds_energy, kinds[:, :ATOMS])[0:1]
    projected = skip[:, :ATOMS] + dot3(pass_ref[0], pass_ref[1], inv_ref[...])
    radial(NEXT, 1, basis_own)
    own_part = gathered(projected, hot_ref[0:ATOMS, :], 2)

    wait_plane(1, r2_ref)

    def summed(group):
        total = jnp.zeros((16, 128), f32)
        for o in group:
            total = total + jnp.where(quarter == place(negated(o))[1], r2_ref[SLOT[o]], 0.0)
        return total

    near = summed(PLANE)
    slots_near = jnp.concatenate([near[4 * k : 4 * k + 4] for k in range(4)], axis=1)
    radial(NEAR, 0, geometry(NEAR, slots_near))
    m_ref[:, NEAR:FAR] = dot(up_kinds, kind_hot(slots_near[3:4]))
    forward([(near_tiles, 256, 0)], False)
    mixed_near = dot3(pass_ref[0], pass_ref[1], inv_ref[:, 0:128])
    wait_above(1, r2_ref)
    far = summed(ABOVE)
    far = far + pltpu.roll(far, 64, 1)
    slots_far = jnp.concatenate(
        [
            jnp.where(lane < 64, far[0:4], far[4:8]),
            jnp.where(lane < 64, far[8:12], far[12:16]),
        ],
        axis=1,
    )
    radial(FAR, 0, geometry(FAR, slots_far))
    m_ref[:, FAR:NEXT] = dot(up_kinds, kind_hot(slots_far[3:4]))
    forward([(far_tiles, 384, 128)], True)
    mixed_far = dot3(pass_ref[0], pass_ref[1], inv_ref[:, 128:256])
    projected = skip[:, ATOMS:] + jnp.concatenate([mixed_near, mixed_far], axis=1)

    m_ref[:, NEXT:LANES] = (own_part + gathered(projected, hot_ref[ATOMS:TABLE, :], 2)) * live4
    energies = next_layer([(next_tiles[0], 512, 0), (next_tiles[1], 640, 128)])
    energy_ref[...] = energy + jnp.sum(jnp.concatenate(energies, axis=1), axis=0, keepdims=True)
    back = gathered(dm_ref[...], hot_t_ref[...], 2)

    back_far = back[:, 384:512]
    back_far = back_far + pltpu.roll(back_far, 64, 1)
    dinv_ref[:, 0:128] = dot3(pass_t_ref[0], pass_t_ref[1], back_far)
    backward(far_tiles, 384, 0, dinv_ref, 0)
    grads_far = vector_grads(FAR, 256, 0)
    s3_ref[...] = jnp.zeros((2, 16, 128), f32)
    for n in range(3):
        for k in range(4):
            x = grads_far[n][:, (k // 2) * 128 : (k // 2) * 128 + 128]
            other = pltpu.roll(x, 64, 1)
            low = lane < 64 if k % 2 == 0 else lane >= 64
            s3_ref[1, 4 * k + n : 4 * k + n + 1, :] = jnp.where(low, x, other)
    send(2, lambda o: s3_ref.at[1], r3_ref, ABOVE)
    dinv_ref[:, 128:256] = dot3(pass_t_ref[0], pass_t_ref[1], back[:, 256:384])
    backward(near_tiles, 256, 0, dinv_ref, 128)
    grads_near = vector_grads(NEAR, 512, 0)
    for n in range(3):
        for k in range(4):
            s3_ref[0, 4 * k + n : 4 * k + n + 1, :] = grads_near[n][:, k * 128 : (k + 1) * 128]
    send(2, lambda o: s3_ref.at[0], r3_ref, PLANE)

    dinv_ref[...] = dot3(pass_t_ref[0], pass_t_ref[1], back[:, :ATOMS]) + dl_ref[...]
    for t in range(2):
        backward(own_tiles[t], 128 * t, 0, dinv_ref, 128 * t)
        backward(next_tiles[t], 512 + 128 * t, NEXT)
    grads = [a + b for a, b in zip(vector_grads(OWN, SLOTS, 0), vector_grads(NEXT, SLOTS, NEXT))]
    grads = jnp.concatenate(grads + [jnp.zeros((5, SLOTS), f32)], axis=0)

    def table_grads(x):
        out = gathered(x, hot_t_ref[...], 2)
        own = out[:, :ATOMS]
        for k in range(4):
            own = own - x[:, k * ATOMS : (k + 1) * ATOMS]
        return own, out[:, ATOMS:]

    def merged(inbox, group, tiles):
        tiles = dict.fromkeys(tiles)
        for o in group:
            g, q = place(o)
            x = jnp.where(quarter == q, inbox[SLOT[o]], 0.0)
            tiles[g] = x if tiles[g] is None else tiles[g] + x
        return jnp.concatenate([tiles[g] for g in sorted(tiles)], axis=1)

    def returned(stage, inbox):
        wait_plane(stage, inbox)
        out = gathered(merged(inbox, PLANE, range(3)), route_t_ref[0:384, :], 2)
        wait_above(stage, inbox)
        return out + gathered(merged(inbox, ABOVE, range(3, 8)), route_t_ref[384:SLOTS, :], 2)

    own_grads, ghost_grads = table_grads(grads)
    from_ghosts = returned(2, r3_ref)
    from_ghosts = jnp.concatenate([from_ghosts[4 * k : 4 * k + 4] for k in range(4)], axis=1)
    from_ghosts = jnp.concatenate([from_ghosts, jnp.zeros((4, SLOTS), f32)], axis=0)
    more_own, more_ghost = table_grads(from_ghosts)
    ghost_grads = ghost_grads + more_ghost
    tail = ghost_grads[:, 128:256]
    s4_ref[1] = tail + pltpu.roll(tail, 64, 1)
    s4_ref[0] = ghost_grads[:, 0:128]
    send(3, lambda o: s4_ref.at[1 if o[2] else 0], r4_ref, ABOVE + PLANE)
    own_grads = own_grads + more_own
    force_ref[...] = -(own_grads + returned(3, r4_ref))[0:3]
    for stage, inbox in enumerate((r1_ref, r2_ref, r3_ref, r4_ref)):
        copies(stage, inbox).wait_send()


def hand_over(energy_ref, force_ref, energy_out, force_out, sem):
    copies = [
        pltpu.make_async_copy(energy_ref, energy_out, sem.at[0]),
        pltpu.make_async_copy(force_ref, force_out, sem.at[1]),
    ]
    for copy in copies:
        copy.start()
    for copy in copies:
        copy.wait()


def body(
    sizes,
    positions,
    species,
    live_count,
    send_lists,
    neighbours,
    embed,
    radial_in,
    radial_out,
    w_up,
    w_skip,
    w_mix,
    readout,
):
    vmem = pl.BlockSpec(memory_space=pltpu.VMEM)
    hbm = pl.BlockSpec(memory_space=pltpu.HBM)
    energy, forces = pl.pallas_call(
        functools.partial(kernel, sizes),
        out_shape=(pltpu.VMEM((1, ATOMS), f32), pltpu.VMEM((3, ATOMS), f32)),
        in_specs=[pl.BlockSpec(memory_space=pltpu.SMEM)] + [hbm] * 11,
        out_specs=(vmem, vmem),
        scratch_shapes=[
            pltpu.VMEM((3, ATOMS), f32),
            pltpu.VMEM((1, ATOMS), jnp.int32),
            pltpu.VMEM((6, 32), jnp.int32),
            pltpu.VMEM((8, 128), jnp.int32),
            pltpu.VMEM((6, 128), f32),
            pltpu.VMEM((2, 128), f32),
            pltpu.VMEM((2, 8, 64), f32),
            pltpu.VMEM((2, 64, 384), f32),
            pltpu.VMEM((2, 128, 128), f32),
            pltpu.VMEM((2, 128, 128), f32),
            pltpu.VMEM((2, 128, 512), f32),
            pltpu.VMEM((8, ATOMS), f32),
            pltpu.VMEM((26, 8, ATOMS), f32),
            pltpu.VMEM((8, 16, 128), f32),
            pltpu.VMEM((26, 16, 128), f32),
            pltpu.VMEM((2, 16, 128), f32),
            pltpu.VMEM((26, 16, 128), f32),
            pltpu.VMEM((2, 8, 128), f32),
            pltpu.VMEM((26, 8, 128), f32),
            pltpu.VMEM((TABLE, SLOTS), bf16),
            pltpu.VMEM((SLOTS, TABLE), bf16),
            pltpu.VMEM((ATOMS, SLOTS), bf16),
            pltpu.VMEM((SLOTS, ATOMS), bf16),
            pltpu.VMEM((2, 64, 32), bf16),
            pltpu.VMEM((2, 384, 192), bf16),
            pltpu.VMEM((2, 128, 512), bf16),
            pltpu.VMEM((2, 512, 128), bf16),
            pltpu.VMEM((512, ATOMS), f32),
            pltpu.VMEM((512, ATOMS), f32),
            pltpu.VMEM((512, ATOMS), f32),
            pltpu.VMEM((768, LANES), f32),
            pltpu.VMEM((128, LANES), f32),
            pltpu.VMEM((1152, 768), f32),
            pltpu.VMEM((8, 8, NEXT), f32),
            pltpu.VMEM((512, ATOMS), f32),
            pltpu.VMEM((128, SLOTS), f32),
            pltpu.VMEM((384, SLOTS), f32),
            pltpu.VMEM((16, LANES), f32),
            pltpu.VMEM((8, NEXT), f32),
            pltpu.VMEM((16, ATOMS), f32),
            pltpu.SemaphoreType.DMA((11,)),
            pltpu.SemaphoreType.DMA((4,)),
            pltpu.SemaphoreType.DMA((4, 2)),
        ],
        compiler_params=pltpu.CompilerParams(
            collective_id=0, has_side_effects=True, vmem_limit_bytes=VMEM_BYTES
        ),
        name="potential",
    )(
        live_count,
        *(
            pltpu.with_memory_space_constraint(x, pltpu.HBM)
            for x in (
                positions,
                species.reshape(1, ATOMS),
                send_lists,
                neighbours.reshape(8, 128),
                embed.T,
                readout,
                radial_in.transpose(0, 2, 1),
                radial_out.transpose(0, 2, 1),
                w_up,
                w_skip,
                w_mix,
            )
        ),
    )
    energy, forces = pl.pallas_call(
        hand_over,
        out_shape=(
            jax.ShapeDtypeStruct((1, ATOMS), f32),
            jax.ShapeDtypeStruct((3, ATOMS), f32),
        ),
        in_specs=[vmem, vmem],
        out_specs=(hbm, hbm),
        scratch_shapes=[pltpu.SemaphoreType.DMA((2,))],
        name="hand_over",
    )(*(pltpu.with_memory_space_constraint(x, pltpu.VMEM) for x in (energy, forces)))
    return energy.reshape(ATOMS), forces


def solution(mesh):
    sizes = {axis: mesh.shape[axis] for axis in AXES}
    split_all = ("gx", "gy", "gz")
    return jax.shard_map(
        functools.partial(body, sizes),
        mesh=mesh,
        in_specs=(
            P(None, split_all),
            P(split_all),
            P(split_all),
            P(None, split_all),
            P(split_all),
            P(),
            P(),
            P(),
            P(),
            P(),
            P(),
            P(),
        ),
        out_specs=(P(split_all), P(None, split_all)),
        check_vma=False,
    )
```

```python
import functools
import itertools
import math

import jax
import jax.numpy as jnp
from jax import lax
from jax.experimental import pallas as pl
from jax.experimental.pallas import tpu as pltpu
from jax.sharding import PartitionSpec as P

AXES = ("gx", "gy", "gz")
MESH = pl.DeviceIdType.MESH
OFFSETS = [o for o in itertools.product((-1, 0, 1), repeat=3) if any(o)]
PLANE = [o for o in OFFSETS if not o[2]]
ABOVE = [o for o in OFFSETS if o[2]]
SLOT = {o: j for j, o in enumerate(PLANE)} | {o: j for j, o in enumerate(ABOVE)}
PLANE.sort(key=lambda o: -abs(o[1]))
ABOVE.sort(key=lambda o: -(abs(o[0]) + 2 * abs(o[1])))
f32 = jnp.float32
bf16 = jnp.bfloat16
HIGHEST = lax.Precision.HIGHEST
ATOMS = 256
SLOTS = 1024
CHAN = 128
OWN, NEAR, FAR, NEXT = 0, 1024, 1536, 1792
LANES = 2816
TABLE = 512
VMEM_BYTES = 48 * 1024 * 1024
DEGREE = (0, 1, 1, 1, 2, 2, 2, 2, 2)
ROOT3 = math.sqrt(3.0)
ROOT5 = math.sqrt(5.0)
ROOT15 = math.sqrt(15.0)


def place(d):
    dx, dy, dz = d
    if dz:
        n = (dx + 1) * 3 + dy + 1
        return 3 + n // 2, (n % 2) * 2 + (0 if dz > 0 else 1)
    if dy:
        return dx + 1, 2 if dy > 0 else 3
    return 0, 0 if dx > 0 else 1


def env_row(k):
    return 4 * (k // 2) + 8 * (k % 2)


def negated(o):
    return (-o[0], -o[1], -o[2])


def iota(shape, dim):
    return lax.broadcasted_iota(jnp.int32, shape, dim)


def dot(a, b):
    return jnp.dot(a, b, preferred_element_type=f32)


def dot_t(a, b):
    return lax.dot_general(a, b, (((1,), (1,)), ((), ())), preferred_element_type=f32)


def exact_dot(a, b, dim=0):
    return lax.dot_general(
        a, b, (((1,), (dim,)), ((), ())), precision=HIGHEST, preferred_element_type=f32
    )


def split(x):
    hi = x.astype(bf16)
    return hi, (x - hi.astype(f32)).astype(bf16)


def terms(x, count):
    out = []
    for _ in range(count):
        hi = x.astype(bf16).astype(f32)
        out.append(hi)
        x = x - hi
    return jnp.concatenate(out, axis=0).astype(bf16)


def gathered(x, onehot, count):
    rows = x.shape[0]
    wide = dot(terms(x, count), onehot)
    return sum(wide[i * rows : (i + 1) * rows] for i in range(count))


def ones_where(mask):
    return jnp.where(mask, 1.0, 0.0).astype(bf16)


def dot3(a_hi, a_lo, b):
    b_hi, b_lo = split(b)
    return dot(a_hi, b_hi) + (dot(a_hi, b_lo) + dot(a_lo, b_hi))


def column(row):
    eye = iota((128, 128), 0) == iota((128, 128), 1)
    return jnp.sum(jnp.where(eye, row, 0.0), axis=1, keepdims=True)


def kernel(
    sizes,
    count_ref,
    pos_hbm,
    species_hbm,
    sends_hbm,
    neigh_hbm,
    embed_hbm,
    readout_hbm,
    rin_hbm,
    rout_hbm,
    up_hbm,
    skip_hbm,
    mix_hbm,
    energy_ref,
    force_ref,
    pos_ref,
    species_ref,
    sends_ref,
    neigh_ref,
    embed_ref,
    readout_ref,
    rin_ref,
    rout_ref,
    up_ref,
    skip_ref,
    mix_ref,
    own_ref,
    s1_ref,
    r1_plane,
    r1_above,
    s2_plane,
    s2_above,
    r2_plane,
    r2_above,
    s3_plane,
    s3_above,
    r3_plane,
    r3_above,
    s4_ref,
    r4_plane,
    r4_above,
    hot_ref,
    hot_t_ref,
    route_ref,
    route_t_ref,
    win_ref,
    wout_ref,
    pass_ref,
    pass_t_ref,
    tl_ref,
    dl_ref,
    dinv_ref,
    rad_ref,
    m_ref,
    a_ref,
    y_ref,
    inv_ref,
    dm_ref,
    dw_ref,
    red_ref,
    geo_ref,
    env_ref,
    load_sem,
    send_sem,
    recv_sem,
):
    r1, r2 = (r1_plane, r1_above), (r2_plane, r2_above)
    r3, r4 = (r3_plane, r3_above), (r4_plane, r4_above)

    def device(o):
        out = {}
        for axis, step in zip(AXES, o):
            here = lax.axis_index(axis)
            out[axis] = here if step == 0 else lax.rem(here + (sizes[axis] + step), sizes[axis])
        return out

    barrier = pltpu.get_barrier_semaphore()
    for o in ABOVE + PLANE:
        pl.semaphore_signal(barrier, inc=1, device_id=device(o), device_id_type=MESH)
    loads = [
        pltpu.make_async_copy(src, dst, load_sem.at[i])
        for i, (src, dst) in enumerate(
            (
                (pos_hbm, pos_ref),
                (species_hbm, species_ref),
                (sends_hbm, sends_ref),
                (neigh_hbm, neigh_ref),
                (mix_hbm, mix_ref),
                (up_hbm, up_ref),
                (rout_hbm, rout_ref),
                (skip_hbm, skip_ref),
                (embed_hbm, embed_ref),
                (readout_hbm, readout_ref),
                (rin_hbm, rin_ref),
            )
        )
    ]
    for load in loads:
        load.start()

    def send(stage, source, inboxes, group):
        for o in group:
            part = 1 if o[2] else 0
            pltpu.make_async_remote_copy(
                src_ref=source(o),
                dst_ref=inboxes[part].at[SLOT[negated(o)]],
                send_sem=send_sem.at[stage, part],
                recv_sem=recv_sem.at[stage, part],
                device_id=device(o),
                device_id_type=MESH,
            ).start()

    def copies(stage, inboxes, part):
        return pltpu.make_async_remote_copy(
            src_ref=inboxes[part],
            dst_ref=inboxes[part],
            send_sem=send_sem.at[stage, part],
            recv_sem=recv_sem.at[stage, part],
            device_id=device((1, 0, 0)),
            device_id_type=MESH,
        )

    def wait_plane(stage, inboxes):
        copies(stage, inboxes, 0).wait_recv()

    def wait_above(stage, inboxes):
        copies(stage, inboxes, 1).wait_recv()

    for load in loads[:3]:
        load.wait()
    own_ref[0:3, :] = pos_ref[...]
    own_ref[3:4, :] = species_ref[...].astype(f32)
    lists = sends_ref[...].astype(f32)
    own_ref[4:8, :] = jnp.zeros((4, ATOMS), f32)
    own_index = jnp.concatenate([lists[n : n + 1] for n in (1, 0, 3, 2)], axis=1)
    own_index_z = jnp.concatenate([lists[n : n + 1] for n in (5, 4, 5, 4)], axis=1)
    wanted = jnp.concatenate([own_index, own_index_z], axis=1).astype(jnp.int32)
    chosen = gathered(own_ref[...], ones_where(iota((ATOMS, 256), 0) == wanted), 3)
    s1_ref[0:4, :] = chosen[0:4, 0:128]
    s1_ref[4:5, :] = own_index
    low = iota((1, 128), 1) < 64
    s1_ref[5:6, :] = jnp.where(low, chosen[0:1, 128:256], chosen[1:2, 128:256])
    s1_ref[6:7, :] = jnp.where(low, chosen[2:3, 128:256], chosen[3:4, 128:256])
    s1_ref[7:8, :] = own_index_z

    lane = iota((1, 128), 1)
    quarter = lane // 32
    live = jnp.where(iota((1, ATOMS), 1) < count_ref[0], 1.0, 0.0)
    live4 = jnp.concatenate([live] * 4, axis=1)

    pl.semaphore_wait(barrier, len(OFFSETS))
    send(0, lambda o: s1_ref, r1, ABOVE + PLANE)

    loads[3].wait()
    neigh = neigh_ref[...]
    halves = jnp.concatenate([neigh >> 8, neigh & 255], axis=0).astype(f32).astype(bf16)
    sel_row = iota((128, SLOTS), 0)
    sel_col = iota((128, SLOTS), 1)
    chosen = dot(halves, ones_where(sel_row == 4 * (sel_col & 31) + (sel_col >> 8)))
    chosen = chosen[0:8] * 256.0 + chosen[8:16]
    group = iota((8, SLOTS), 0) == ((iota((8, SLOTS), 1) & 255) >> 5)
    neigh_row = jnp.sum(jnp.where(group, chosen, 0.0), axis=0, keepdims=True).astype(jnp.int32)

    def hot_step(i, carry):
        first = pl.multiple_of(i * 64, 64)
        hot_ref[pl.ds(first, 64), :] = ones_where(iota((64, SLOTS), 0) + i * 64 == neigh_row)
        return carry

    lax.fori_loop(0, TABLE // 64, hot_step, 0)

    def hot_t_step(i, carry):
        first = pl.multiple_of(i * 128, 128)
        slot = iota((128, 128), 0) + i * 128
        sel = ones_where(iota((128, 128), 1) == 4 * (slot & 31) + (slot >> 8))
        mine = dot_t(sel, halves)
        place_at = iota((128, 16), 1)
        mine = mine * jnp.where(place_at < 8, 256.0, 1.0)
        in_group = (place_at & 7) == (((iota((128, 16), 0) + i * 128) & 255) >> 5)
        mine = jnp.sum(jnp.where(in_group, mine, 0.0), axis=1, keepdims=True)
        hot_t_ref[pl.ds(first, 128), :] = ones_where(iota((128, TABLE), 1).astype(f32) == mine)
        return carry


    lax.fori_loop(0, SLOTS // 128, hot_t_step, 0)
    for load in loads[4:]:
        load.wait()
    wide_lane = iota((128, 128), 1)

    def stacked(x):
        hi = x.astype(bf16).astype(f32)
        return jnp.concatenate([hi, hi, x - hi, jnp.zeros_like(x)], axis=0)

    for layer in range(2):
        rin = jnp.concatenate([stacked(rin_ref[layer]), jnp.zeros((96, 64), f32)], axis=0)
        rin = jnp.concatenate([rin, jnp.zeros((128, 64), f32)], axis=1).T
        win_ref[layer] = rin[:64, :32].astype(bf16)
        wout_ref[layer] = stacked(rout_ref[layer]).T[:, :192].astype(bf16)
    between = exact_dot(up_ref[1], mix_ref[0])
    pass_ref[0], pass_ref[1] = split(between)
    pass_t_ref[0], pass_t_ref[1] = split(between.T)
    embed = jnp.concatenate([embed_ref[...], jnp.zeros((2, 128), f32)], axis=0)
    embed3 = jnp.concatenate([embed, embed, embed, jnp.zeros((104, 128), f32)], axis=0)

    def three_terms(x):
        hi = x.astype(bf16).astype(f32)
        mid = (x - hi).astype(bf16).astype(f32)
        lo = x - hi - mid
        x = jnp.where(wide_lane < 8, hi, jnp.where(wide_lane < 16, mid, lo))
        return x[:, :32].astype(bf16)

    up_kinds = three_terms(exact_dot(up_ref[0], embed3, 1))
    skip_kinds = exact_dot(skip_ref[0], embed3, 1)
    skip_up_kinds = three_terms(exact_dot(up_ref[1], skip_kinds))
    ro1 = readout_ref[1:2, :]
    direct = readout_ref[0:1, :] + exact_dot(ro1, skip_ref[1])
    kinds_energy = jnp.broadcast_to(exact_dot(direct, skip_kinds), (128, 128))
    kinds_energy = three_terms(kinds_energy)[0:16]
    for ref, mixed in ((dl_ref, exact_dot(direct, mix_ref[0])), (tl_ref, exact_dot(ro1, mix_ref[1]))):
        for k in range(4):
            ref[k * 128 : (k + 1) * 128, :] = column(mixed[:, k * 128 : (k + 1) * 128]) * live

    def kind_hot(row):
        width = row.shape[1]
        sub = iota((32, width), 0)
        return ones_where(((sub & 7).astype(f32) == row) & (sub < 24))

    wait_plane(0, r1)

    def message(o):
        return r1[1 if o[2] else 0][SLOT[o]]

    def shift(section):
        step = jnp.where((quarter & 1) == 0, -4.0, 4.0)
        return jnp.where(iota((8, 128), 0) == section, step, 0.0)

    def picked(index, valid, lower, upper, edge):
        index = jnp.where(valid, index, -1.0).astype(jnp.int32)
        onehot = ones_where(iota((128, 128), 0) == index)
        out = gathered(jnp.concatenate([lower, upper], axis=0), onehot, 3)
        return jnp.where(lane < edge, out[0:8], out[8:16])

    def x_tile(oy, oz):
        return jnp.where(lane < 32, message((-1, oy, oz)), message((1, oy, oz))) + shift(0)

    def xy_tile(oz):
        lower, upper = message((0, -1, oz)), message((0, 1, oz))
        own_rows = jnp.where(lane < 96, lower, upper)
        ghosts = picked(own_rows[4:5] - 256.0, lane >= 64, x_tile(-1, oz), x_tile(1, oz), 96)
        return jnp.where(lane < 64, x_tile(0, oz), own_rows + ghosts + shift(1))

    ghost0 = xy_tile(0)
    moved = gathered(own_ref[...], hot_ref[0:ATOMS, :], 3)
    moved = moved + gathered(ghost0, hot_ref[ATOMS : ATOMS + 128, :], 3)

    def own_only(index):
        return jnp.where(index < 256.0, index + 1.0, 0.0)

    def looked_up(index, lowest, offset):
        inside = (index >= lowest) & (index < lowest + 32.0)
        return jnp.where(inside, index + offset, -1.0)

    def compose(keys, entries):
        depth = entries.shape[1]
        onehot = ones_where(iota((depth, keys.shape[1]), 0) == keys.astype(jnp.int32))
        entries = jnp.broadcast_to(entries, (8, depth)).astype(bf16)
        return dot(entries, onehot)[0:1]

    zero_row = jnp.zeros((1, 128), f32)
    x_entries = jnp.where(lane < 64, own_index + 1.0, 0.0)
    keys = []
    for dx, lowest in ((-1, 288.0), (1, 256.0)):
        key = looked_up(message((dx, 0, 0))[4:5], lowest, -256.0)
        keys.append(jnp.where(lane < 64, -1.0, key))
    found = compose(jnp.concatenate(keys, axis=1), x_entries)
    route = [
        jnp.where(lane < 64, own_index + 1.0, found[:, 0:128]),
        jnp.where(lane < 64, 0.0, own_only(own_index)),
        jnp.where(lane < 64, 0.0, found[:, 128:256]),
    ]
    keys, directs = [], []
    for n in range(10):
        dx, dy = n // 3 - 1, n % 3 - 1
        key, direct = zero_row - 1.0, zero_row
        if n == 4:
            direct = own_only(own_index_z)
        elif n < 9:
            if dy:
                lowest = 320.0 if dy > 0 else 352.0
                offset = 128.0 * (dx + 1) - 256.0
            else:
                lowest = 256.0 if dx > 0 else 288.0
                offset = -256.0
            key = looked_up(message((dx, dy, 0))[7:8], lowest, offset)
        keys.append(key)
        directs.append(direct)
    keys = [jnp.where(lane < 64, keys[n], keys[n + 1]) for n in range(0, 10, 2)]
    directs = [jnp.where(lane < 64, directs[n], directs[n + 1]) for n in range(0, 10, 2)]
    found = compose(jnp.concatenate(keys, axis=1), jnp.concatenate(route, axis=1))
    found = found + jnp.concatenate(directs, axis=1)
    route_row = jnp.concatenate(route + [found], axis=1).astype(jnp.int32)

    def route_step(i, carry):
        first = pl.multiple_of(i * 64, 64)
        route_ref[pl.ds(first, 64), :] = ones_where(iota((64, SLOTS), 0) + (i * 64 + 1) == route_row)
        return carry

    lax.fori_loop(0, ATOMS // 64, route_step, 0)

    wait_above(0, r1)
    lower, upper = message((0, 0, -1)), message((0, 0, 1))
    own_rows = jnp.where((quarter & 1) == 0, lower, upper)
    turned = pltpu.roll(own_rows, 64, 1)
    ghosts = picked(own_rows[7:8] - 256.0, lane < 64, xy_tile(-1), xy_tile(1), 32)
    own_rows = [own_rows[5:6], turned[5:6], own_rows[6:7], turned[6:7], jnp.zeros((4, 128), f32)]
    ghost1 = jnp.concatenate(own_rows, axis=0) + ghosts + shift(2)
    ghost1 = jnp.where(lane < 64, ghost1, 0.0)

    centres = jnp.concatenate([own_ref[...]] * 4, axis=1)
    is_coord = iota((8, SLOTS), 0) < 3
    moved = moved + gathered(ghost1, hot_ref[ATOMS + 128 : TABLE, :], 3)
    slots_own = moved - jnp.where(is_coord, centres, 0.0)
    for k in range(4):
        env_ref[env_row(k) : env_row(k) + 4, :] = slots_own[0:4, k * ATOMS : (k + 1) * ATOMS]
    spread_env = gathered(env_ref[...], route_ref[...], 3)
    for g in range(3, 8):
        even, odd = (spread_env[n : n + 8, g * 128 : (g + 1) * 128] for n in (0, 8))
        s2_above[2 * g - 6] = jnp.where(lane < 64, even, pltpu.roll(odd, 64, 1))
        s2_above[2 * g - 5] = jnp.where(lane < 64, pltpu.roll(even, 64, 1), odd)
    send(1, lambda o: s2_above.at[2 * place(o)[0] - 6 + place(o)[1] // 2], r2, ABOVE)
    for g in range(3):
        s2_plane[g] = spread_env[:, g * 128 : (g + 1) * 128]
    send(1, lambda o: s2_plane.at[place(o)[0]], r2, PLANE)

    def geometry(at, slots):
        width = slots.shape[1]
        lanes = slice(at, at + width)
        vx, vy, vz = slots[0:1], slots[1:2], slots[2:3]
        r_sq = vx * vx + vy * vy + vz * vz + 0.04
        inv = lax.rsqrt(r_sq)
        r = r_sq * inv
        ux, uy, uz = vx * inv, vy * inv, vz * inv
        geo_ref[0:1, lanes] = ux
        geo_ref[1:2, lanes] = uy
        geo_ref[2:3, lanes] = uz
        geo_ref[3:4, lanes] = inv
        harm = [
            ROOT3 * ux,
            ROOT3 * uy,
            ROOT3 * uz,
            ROOT15 * ux * uy,
            ROOT15 * uy * uz,
            0.5 * ROOT5 * (3.0 * uz * uz - 1.0),
            ROOT15 * ux * uz,
            0.5 * ROOT15 * (ux * ux - uy * uy),
        ]
        for m in range(8):
            y_ref[m, :, lanes] = jnp.broadcast_to(0.5 * harm[m], (8, width))
        x = r * 0.25
        order = (iota((8, width), 0) + 1).astype(f32)
        phase = order * x
        near = jnp.floor(phase + 0.5)
        part = phase - near
        sign = 1.0 - 2.0 * (near - 2.0 * jnp.floor(near * 0.5))
        angle = part * math.pi
        square = angle * angle
        sin = 1.0
        for k in (14, 12, 10, 8, 6, 4, 2):
            sin = 1.0 - square * sin * (1.0 / (k * (k + 1)))
        sin = sign * angle * sin
        cos = 1.0
        for k in (14, 12, 10, 8, 6, 4, 2):
            cos = 1.0 - square * cos * (1.0 / (k * (k - 1)))
        cos = sign * cos
        gap = 1.0 - x * x
        within = x < 1.0
        env = jnp.where(within, gap * gap, 0.0)
        env_d = jnp.where(within, -x * gap, 0.0)
        scale = math.sqrt(0.5)
        base = scale * sin * inv
        basis = base * env
        basis_d = (scale * (math.pi / 4.0) * order * cos * inv - base * inv) * env + base * env_d
        wide = jnp.concatenate([basis, basis_d], axis=1)
        hi = wide.astype(bf16).astype(f32)
        lo = wide - hi
        return jnp.concatenate([hi, lo, hi, jnp.zeros_like(hi)], axis=0).astype(bf16)

    def radial(at, layer, basis):
        width = basis.shape[1] // 2
        z = dot(win_ref[layer], basis)
        slope, z = z[:, width:], z[:, :width]
        gate = 1.0 / (1.0 + jnp.exp(-z))
        hidden = z * gate
        hidden_d = gate * (1.0 + z * (1.0 - gate)) * slope
        for half, x in enumerate((hidden, hidden_d)):
            hi, lo = split(x)
            rad_ref[half * 384 : (half + 1) * 384, at : at + width] = dot(
                wout_ref[layer], jnp.concatenate([hi, lo, hi], axis=0)
            )

    def tiles_of(at, width, count, tile):
        return [slice(at + k * width + tile * 128, at + k * width + tile * 128 + 128) for k in range(count)]

    def harmonics_of(s, y_shift):
        return [None] + [y_ref[n, :, s.start - y_shift : s.stop - y_shift] for n in range(8)]

    def moments(firsts, lanes, y_shift, folded):
        out = [[None] * 9 for _ in firsts]
        for s in lanes:
            y = harmonics_of(s, y_shift)
            for c, first in enumerate(firsts):
                m = m_ref[pl.ds(first, 8), s]
                weighted = [rad_ref[pl.ds(k * 128 + first, 8), s] * m for k in range(3)]
                for n in range(9):
                    x = (0.5 if n == 0 else y[n]) * weighted[DEGREE[n]]
                    out[c][n] = x if out[c][n] is None else out[c][n] + x
        if folded:
            out = [[x + pltpu.roll(x, 64, 1) for x in a] for a in out]
        return out

    def squares_of(a):
        return (
            a[0] * a[0],
            a[1] * a[1] + a[2] * a[2] + a[3] * a[3],
            a[4] * a[4] + a[5] * a[5] + a[6] * a[6] + a[7] * a[7] + a[8] * a[8],
        )

    def forward(parts, folded):
        def step(i, carry):
            firsts = [pl.multiple_of(i * 16 + 8 * c, 8) for c in range(2)]
            for lanes, a_at, inv_at in parts:
                cols = slice(inv_at, inv_at + 128)
                for first, a in zip(firsts, moments(firsts, lanes, 0, folded)):
                    for n in range(9):
                        a_ref[pl.ds(n * 128 + first, 8), a_at : a_at + 128] = a[n]
                    b = squares_of(a)
                    inv_ref[pl.ds(first, 8), cols] = a[0]
                    inv_ref[pl.ds(128 + first, 8), cols] = b[0]
                    inv_ref[pl.ds(256 + first, 8), cols] = b[1] * (1.0 / 3.0)
                    inv_ref[pl.ds(384 + first, 8), cols] = b[2] * (1.0 / 5.0)
            return carry

        lax.fori_loop(0, CHAN // 16, step, 0, unroll=8 if folded else 2)

    def moment_grads(first, a, grads, g_at):
        cols = slice(g_at, g_at + 128)
        factors = [
            2.0 * grads[pl.ds(128 + first, 8), cols],
            (2.0 / 3.0) * grads[pl.ds(256 + first, 8), cols],
            (2.0 / 5.0) * grads[pl.ds(384 + first, 8), cols],
        ]
        out = [x * factors[DEGREE[n]] for n, x in enumerate(a)]
        out[0] = out[0] + grads[pl.ds(first, 8), cols]
        return out

    def slot_grads(da, y):
        return [
            0.5 * da[0],
            da[1] * y[1] + da[2] * y[2] + da[3] * y[3],
            (da[4] * y[4] + da[5] * y[5]) + (da[6] * y[6] + da[7] * y[7]) + da[8] * y[8],
        ]

    def next_layer(parts):
        def step(i, energies):
            firsts = [pl.multiple_of(i * 16 + 8 * c, 8) for c in range(2)]
            out = []
            for (lanes, a_at, t_at), energy in zip(parts, energies):
                cols = slice(t_at, t_at + 128)
                grads = []
                for first, a in zip(firsts, moments(firsts, lanes, NEXT, False)):
                    b = squares_of(a)
                    energy = (
                        energy
                        + a[0] * tl_ref[pl.ds(first, 8), cols]
                        + b[0] * tl_ref[pl.ds(128 + first, 8), cols]
                        + b[1] * ((1.0 / 3.0) * tl_ref[pl.ds(256 + first, 8), cols])
                        + b[2] * ((1.0 / 5.0) * tl_ref[pl.ds(384 + first, 8), cols])
                    )
                    da = moment_grads(first, a, tl_ref, t_at)
                    for n in range(9):
                        a_ref[pl.ds(n * 128 + first, 8), a_at : a_at + 128] = da[n]
                    grads.append(da)
                out.append(energy)
                for s in lanes:
                    y = harmonics_of(s, NEXT)
                    at = slice(s.start - NEXT, s.stop - NEXT)
                    dm = []
                    for first, da in zip(firsts, grads):
                        dw = slot_grads(da, y)
                        rad = [rad_ref[pl.ds(j * 128 + first, 8), s] for j in range(3)]
                        dm.append(dw[0] * rad[0] + dw[1] * rad[1] + dw[2] * rad[2])
                        for j in range(3):
                            dw_ref[pl.ds(j * 128 + first, 8), at] = dw[j]
                    hi, lo = split(jnp.concatenate(dm, axis=0))
                    both = pl.multiple_of(i * 16, 16)
                    dm_ref[pl.ds(both, 16), at] = hi
                    dm_ref[pl.ds(CHAN + both, 16), at] = lo
            return tuple(out)

        zero = jnp.zeros((8, 128), f32)
        return lax.fori_loop(0, CHAN // 16, step, (zero,) * len(parts), unroll=2)

    def backward(lanes, a_at, y_shift, grads=None, g_at=0):
        def step(i, totals):
            first = pl.multiple_of(i * 8, 8)
            da = [a_ref[pl.ds(n * 128 + first, 8), a_at : a_at + 128] for n in range(9)]
            if grads is not None:
                da = moment_grads(first, da, grads, g_at)
            out = []
            for k, s in enumerate(lanes):
                m = m_ref[pl.ds(first, 8), s]
                weighted = [rad_ref[pl.ds(j * 128 + first, 8), s] * m for j in range(3)]
                for n in range(1, 9):
                    out.append(totals[9 * k + n - 1] + da[n] * weighted[DEGREE[n]])
                if grads is None:
                    at = slice(s.start - y_shift, s.stop - y_shift)
                    dw = [dw_ref[pl.ds(j * 128 + first, 8), at] for j in range(3)]
                else:
                    dw = slot_grads(da, harmonics_of(s, y_shift))
                slope = [rad_ref[pl.ds(384 + j * 128 + first, 8), s] for j in range(3)]
                slope = dw[0] * slope[0] + dw[1] * slope[1] + dw[2] * slope[2]
                out.append(totals[9 * k + 8] + slope * m)
            return tuple(out)

        zero = jnp.zeros((8, 128), f32)
        totals = lax.fori_loop(0, CHAN // 8, step, (zero,) * (9 * len(lanes)), unroll=4 if len(lanes) == 4 else 8)
        for k, s in enumerate(lanes):
            for n in range(9):
                red_ref[n : n + 1, s] = jnp.sum(totals[9 * k + n], axis=0, keepdims=True)

    def vector_grads(at, width, y_shift):
        lanes = slice(at, at + width)
        geo = slice(at - y_shift, at - y_shift + width)
        g = [None] + [0.5 * red_ref[n : n + 1, lanes] for n in range(8)]
        slope = red_ref[8:9, lanes]
        ux, uy, uz, inv = (geo_ref[n : n + 1, geo] for n in range(4))
        gx = ROOT3 * g[1] + ROOT15 * (uy * g[4] + uz * g[7] + ux * g[8])
        gy = ROOT3 * g[2] + ROOT15 * (ux * g[4] + uz * g[5] - uy * g[8])
        gz = ROOT3 * g[3] + ROOT15 * (uy * g[5] + ux * g[7]) + (3.0 * ROOT5) * uz * g[6]
        along = slope - (ux * gx + uy * gy + uz * gz) * inv
        return [gx * inv + ux * along, gy * inv + uy * along, gz * inv + uz * along]

    route_row = route_row.astype(f32)
    for g in range(8):
        mine = column(route_row[:, g * 128 : (g + 1) * 128])
        route_t_ref[g * 128 : (g + 1) * 128, :] = ones_where(
            (iota((128, ATOMS), 1) + 1).astype(f32) == mine
        )
    own_tiles = [tiles_of(OWN, ATOMS, 4, t) for t in range(2)]
    near_tiles = tiles_of(NEAR, 128, 4, 0)
    far_tiles = tiles_of(FAR, 128, 2, 0)
    next_tiles = [tiles_of(NEXT, ATOMS, 4, t) for t in range(2)]
    basis_own = geometry(OWN, slots_own)
    radial(OWN, 0, basis_own)
    m_ref[:, OWN : OWN + SLOTS] = dot(up_kinds, kind_hot(slots_own[3:4])) * live4
    forward([(own_tiles[0], 0, 0), (own_tiles[1], 128, 128)], False)
    kinds = kind_hot(jnp.concatenate([own_ref[3:4, :], ghost0[3:4], ghost1[3:4]], axis=1))
    skip = dot(skip_up_kinds, kinds)
    energy = jnp.sum(dl_ref[...] * inv_ref[...], axis=0, keepdims=True)
    energy = energy + live * dot(kinds_energy, kinds[:, :ATOMS])[0:1]
    projected = skip[:, :ATOMS] + dot3(pass_ref[0], pass_ref[1], inv_ref[...])
    radial(NEXT, 1, basis_own)
    own_part = gathered(projected, hot_ref[0:ATOMS, :], 2)

    wait_plane(1, r2)

    near = jnp.zeros((16, 128), f32)
    for o in PLANE:
        near = near + jnp.where(quarter == place(negated(o))[1], r2_plane[SLOT[o]], 0.0)
    slots_near = jnp.concatenate([near[env_row(k) : env_row(k) + 4] for k in range(4)], axis=1)
    radial(NEAR, 0, geometry(NEAR, slots_near))
    m_ref[:, NEAR:FAR] = dot(up_kinds, kind_hot(slots_near[3:4]))
    forward([(near_tiles, 256, 0)], False)
    mixed_near = dot3(pass_ref[0], pass_ref[1], inv_ref[:, 0:128])
    wait_above(1, r2)
    far = jnp.zeros((8, 128), f32)
    for o in ABOVE:
        far = far + jnp.where((quarter & 1) == place(negated(o))[1] % 2, r2_above[SLOT[o]], 0.0)
    slots_far = jnp.concatenate([far[0:4], far[4:8]], axis=1)
    radial(FAR, 0, geometry(FAR, slots_far))
    m_ref[:, FAR:NEXT] = dot(up_kinds, kind_hot(slots_far[3:4]))
    forward([(far_tiles, 384, 128)], True)
    mixed_far = dot3(pass_ref[0], pass_ref[1], inv_ref[:, 128:256])
    projected = skip[:, ATOMS:] + jnp.concatenate([mixed_near, mixed_far], axis=1)

    m_ref[:, NEXT:LANES] = (own_part + gathered(projected, hot_ref[ATOMS:TABLE, :], 2)) * live4
    energies = next_layer([(next_tiles[0], 512, 0), (next_tiles[1], 640, 128)])
    energy_ref[...] = energy + jnp.sum(jnp.concatenate(energies, axis=1), axis=0, keepdims=True)

    def feature_grads(cols):
        wide = dot(dm_ref[...], hot_t_ref[:, cols])
        return wide[:CHAN] + wide[CHAN:]


    back_far = feature_grads(slice(384, TABLE))
    back_far = back_far + pltpu.roll(back_far, 64, 1)
    dinv_ref[:, 0:128] = dot3(pass_t_ref[0], pass_t_ref[1], back_far)
    backward(far_tiles, 384, 0, dinv_ref, 0)
    grads_far = vector_grads(FAR, 256, 0)
    s3_plane[...] = jnp.zeros((16, 128), f32)
    s3_above[...] = jnp.zeros((8, 128), f32)
    for n in range(3):
        for t in range(2):
            s3_above[4 * t + n : 4 * t + n + 1, :] = grads_far[n][:, t * 128 : (t + 1) * 128]
    send(2, lambda o: s3_above, r3, ABOVE)
    back = feature_grads(slice(0, 384))
    dinv_ref[:, 128:256] = dot3(pass_t_ref[0], pass_t_ref[1], back[:, 256:384])
    backward(near_tiles, 256, 0, dinv_ref, 128)
    grads_near = vector_grads(NEAR, 512, 0)
    for n in range(3):
        for k in range(4):
            at = env_row(k) + n
            s3_plane[at : at + 1, :] = grads_near[n][:, k * 128 : (k + 1) * 128]
    send(2, lambda o: s3_plane, r3, PLANE)

    dinv_ref[...] = dot3(pass_t_ref[0], pass_t_ref[1], back[:, :ATOMS]) + dl_ref[...]
    for t in range(2):
        backward(own_tiles[t], 128 * t, 0, dinv_ref, 128 * t)
        backward(next_tiles[t], 512 + 128 * t, NEXT)
    grads = [a + b for a, b in zip(vector_grads(OWN, SLOTS, 0), vector_grads(NEXT, SLOTS, NEXT))]
    grads = jnp.concatenate(grads + [jnp.zeros((5, SLOTS), f32)], axis=0)

    def own_table_grads(x):
        own = gathered(x, hot_t_ref[:, 0:ATOMS], 2)
        for k in range(4):
            own = own - x[:, k * ATOMS : (k + 1) * ATOMS]
        return own

    def ghost_table_grads(x):
        return gathered(x, hot_t_ref[:, ATOMS:TABLE], 2)

    def merged(inbox, group, tiles):
        tiles = dict.fromkeys(tiles)
        for o in group:
            g, q = place(o)
            x = jnp.where(quarter == q, inbox[SLOT[o]], 0.0)
            tiles[g] = x if tiles[g] is None else tiles[g] + x
        return jnp.concatenate([tiles[g] for g in sorted(tiles)], axis=1)

    def unpacked(inbox):
        at = {place(o): inbox[SLOT[o]] for o in ABOVE}
        zero = jnp.zeros((8, 128), f32)
        tiles = []
        for g in range(3, 8):
            first = jnp.where((quarter & 1) == 0, at[g, 0], at[g, 1])
            second = jnp.where((quarter & 1) == 0, at.get((g, 2), zero), at.get((g, 3), zero))
            even = jnp.where(lane < 64, first, pltpu.roll(second, 64, 1))
            odd = jnp.where(lane < 64, pltpu.roll(first, 64, 1), second)
            tiles.append(jnp.concatenate([even, odd], axis=0))
        return jnp.concatenate(tiles, axis=1)

    def returned(stage, inboxes, above):
        wait_plane(stage, inboxes)
        plane = merged(inboxes[0], PLANE, range(3))
        rows = max(8, plane.shape[0])
        fill = jnp.zeros((rows - plane.shape[0], 384), f32)
        plane = jnp.concatenate([plane, fill], axis=0) if rows > plane.shape[0] else plane
        out = gathered(plane, route_t_ref[0:384, :], 2)
        wait_above(stage, inboxes)
        far = above(inboxes[1])
        fill = jnp.zeros((rows - far.shape[0], 640), f32)
        far = jnp.concatenate([far, fill], axis=0) if rows > far.shape[0] else far
        return out + gathered(far, route_t_ref[384:SLOTS, :], 2)

    own_grads = own_table_grads(grads)
    ghost_grads = ghost_table_grads(grads)
    from_ghosts = returned(2, r3, unpacked)
    from_ghosts = jnp.concatenate(
        [from_ghosts[env_row(k) : env_row(k) + 4] for k in range(4)], axis=1
    )
    from_ghosts = jnp.concatenate([from_ghosts, jnp.zeros((4, SLOTS), f32)], axis=0)
    ghost_grads = (ghost_grads + ghost_table_grads(from_ghosts))[0:4]
    tail = ghost_grads[:, 128:256]
    s4_ref[1] = tail + pltpu.roll(tail, 64, 1)
    s4_ref[0] = ghost_grads[:, 0:128]
    send(3, lambda o: s4_ref.at[1 if o[2] else 0], r4, ABOVE + PLANE)
    own_grads = own_grads + own_table_grads(from_ghosts)
    last = returned(3, r4, lambda inbox: merged(inbox, ABOVE, range(3, 8)))
    force_ref[...] = -(own_grads + last)[0:3]
    for stage, inboxes in enumerate((r1, r2, r3, r4)):
        for part in range(2):
            copies(stage, inboxes, part).wait_send()


def hand_over(energy_ref, force_ref, energy_out, force_out, sem):
    copies = [
        pltpu.make_async_copy(energy_ref, energy_out, sem.at[0]),
        pltpu.make_async_copy(force_ref, force_out, sem.at[1]),
    ]
    for copy in copies:
        copy.start()
    for copy in copies:
        copy.wait()


def body(
    sizes,
    positions,
    species,
    live_count,
    send_lists,
    neighbours,
    embed,
    radial_in,
    radial_out,
    w_up,
    w_skip,
    w_mix,
    readout,
):
    vmem = pl.BlockSpec(memory_space=pltpu.VMEM)
    hbm = pl.BlockSpec(memory_space=pltpu.HBM)
    energy, forces = pl.pallas_call(
        functools.partial(kernel, sizes),
        out_shape=(pltpu.VMEM((1, ATOMS), f32), pltpu.VMEM((3, ATOMS), f32)),
        in_specs=[pl.BlockSpec(memory_space=pltpu.SMEM)] + [hbm] * 11,
        out_specs=(vmem, vmem),
        scratch_shapes=[
            pltpu.VMEM((3, ATOMS), f32),
            pltpu.VMEM((1, ATOMS), jnp.int32),
            pltpu.VMEM((6, 32), jnp.int32),
            pltpu.VMEM((8, 128), jnp.int32),
            pltpu.VMEM((6, 128), f32),
            pltpu.VMEM((2, 128), f32),
            pltpu.VMEM((2, 8, 64), f32),
            pltpu.VMEM((2, 64, 384), f32),
            pltpu.VMEM((2, 128, 128), f32),
            pltpu.VMEM((2, 128, 128), f32),
            pltpu.VMEM((2, 128, 512), f32),
            pltpu.VMEM((8, ATOMS), f32),
            pltpu.VMEM((8, 128), f32),
            pltpu.VMEM((8, 8, 128), f32),
            pltpu.VMEM((18, 8, 128), f32),
            pltpu.VMEM((3, 16, 128), f32),
            pltpu.VMEM((10, 8, 128), f32),
            pltpu.VMEM((8, 16, 128), f32),
            pltpu.VMEM((18, 8, 128), f32),
            pltpu.VMEM((16, 128), f32),
            pltpu.VMEM((8, 128), f32),
            pltpu.VMEM((8, 16, 128), f32),
            pltpu.VMEM((18, 8, 128), f32),
            pltpu.VMEM((2, 4, 128), f32),
            pltpu.VMEM((8, 4, 128), f32),
            pltpu.VMEM((18, 4, 128), f32),
            pltpu.VMEM((TABLE, SLOTS), bf16),
            pltpu.VMEM((SLOTS, TABLE), bf16),
            pltpu.VMEM((ATOMS, SLOTS), bf16),
            pltpu.VMEM((SLOTS, ATOMS), bf16),
            pltpu.VMEM((2, 64, 32), bf16),
            pltpu.VMEM((2, 384, 192), bf16),
            pltpu.VMEM((2, 128, 512), bf16),
            pltpu.VMEM((2, 512, 128), bf16),
            pltpu.VMEM((512, ATOMS), f32),
            pltpu.VMEM((512, ATOMS), f32),
            pltpu.VMEM((512, ATOMS), f32),
            pltpu.VMEM((768, LANES), f32),
            pltpu.VMEM((128, LANES), f32),
            pltpu.VMEM((1152, 768), f32),
            pltpu.VMEM((8, 8, NEXT), f32),
            pltpu.VMEM((512, ATOMS), f32),
            pltpu.VMEM((256, SLOTS), bf16),
            pltpu.VMEM((384, SLOTS), f32),
            pltpu.VMEM((16, LANES), f32),
            pltpu.VMEM((8, NEXT), f32),
            pltpu.VMEM((16, ATOMS), f32),
            pltpu.SemaphoreType.DMA((11,)),
            pltpu.SemaphoreType.DMA((4, 2)),
            pltpu.SemaphoreType.DMA((4, 2)),
        ],
        compiler_params=pltpu.CompilerParams(
            collective_id=0, has_side_effects=True, vmem_limit_bytes=VMEM_BYTES
        ),
        name="potential",
    )(
        live_count,
        *(
            pltpu.with_memory_space_constraint(x, pltpu.HBM)
            for x in (
                positions,
                species.reshape(1, ATOMS),
                send_lists,
                neighbours.reshape(8, 128),
                embed.T,
                readout,
                radial_in.transpose(0, 2, 1),
                radial_out.transpose(0, 2, 1),
                w_up,
                w_skip,
                w_mix,
            )
        ),
    )
    energy, forces = pl.pallas_call(
        hand_over,
        out_shape=(
            jax.ShapeDtypeStruct((1, ATOMS), f32),
            jax.ShapeDtypeStruct((3, ATOMS), f32),
        ),
        in_specs=[vmem, vmem],
        out_specs=(hbm, hbm),
        scratch_shapes=[pltpu.SemaphoreType.DMA((2,))],
        name="hand_over",
    )(*(pltpu.with_memory_space_constraint(x, pltpu.VMEM) for x in (energy, forces)))
    return energy.reshape(ATOMS), forces


def solution(mesh):
    sizes = {axis: mesh.shape[axis] for axis in AXES}
    split_all = ("gx", "gy", "gz")
    return jax.shard_map(
        functools.partial(body, sizes),
        mesh=mesh,
        in_specs=(
            P(None, split_all),
            P(split_all),
            P(split_all),
            P(None, split_all),
            P(split_all),
            P(),
            P(),
            P(),
            P(),
            P(),
            P(),
            P(),
        ),
        out_specs=(P(split_all), P(None, split_all)),
        check_vma=False,
    )
```

```python
import functools
import itertools
import math

import jax
import jax.numpy as jnp
from jax import lax
from jax.experimental import pallas as pl
from jax.experimental.pallas import tpu as pltpu
from jax.sharding import PartitionSpec as P

AXES = ("gx", "gy", "gz")
MESH = pl.DeviceIdType.MESH
OFFSETS = [o for o in itertools.product((-1, 0, 1), repeat=3) if any(o)]
PLANE = [o for o in OFFSETS if not o[2]]
ABOVE = [o for o in OFFSETS if o[2]]
SLOT = {o: j for j, o in enumerate(PLANE)} | {o: j for j, o in enumerate(ABOVE)}
SLOWEST_FIRST = sorted(OFFSETS, key=lambda o: (-sum(map(abs, o)), -abs(o[1]), -abs(o[0])))
PLANE.sort(key=SLOWEST_FIRST.index)
ABOVE.sort(key=SLOWEST_FIRST.index)
f32 = jnp.float32
bf16 = jnp.bfloat16
HIGHEST = lax.Precision.HIGHEST
ATOMS = 256
SLOTS = 1024
CHAN = 128
OWN, NEAR, FAR, NEXT = 0, 1024, 1536, 1792
LANES = 2816
TABLE = 512
VMEM_BYTES = 48 * 1024 * 1024
DEGREE = (0, 1, 1, 1, 2, 2, 2, 2, 2)
ROOT3 = math.sqrt(3.0)
ROOT5 = math.sqrt(5.0)
ROOT15 = math.sqrt(15.0)


def place(d):
    dx, dy, dz = d
    if dz:
        n = (dx + 1) * 3 + dy + 1
        return 3 + n // 2, (n % 2) * 2 + (0 if dz > 0 else 1)
    if dy:
        return dx + 1, 2 if dy > 0 else 3
    return 0, 0 if dx > 0 else 1


def env_row(k):
    return 4 * (k // 2) + 8 * (k % 2)


def negated(o):
    return (-o[0], -o[1], -o[2])


def iota(shape, dim):
    return lax.broadcasted_iota(jnp.int32, shape, dim)


def dot(a, b):
    return jnp.dot(a, b, preferred_element_type=f32)


def dot_t(a, b):
    return lax.dot_general(a, b, (((1,), (1,)), ((), ())), preferred_element_type=f32)


def exact_dot(a, b, dim=0):
    return lax.dot_general(
        a, b, (((1,), (dim,)), ((), ())), precision=HIGHEST, preferred_element_type=f32
    )


def split(x):
    hi = x.astype(bf16)
    return hi, (x - hi.astype(f32)).astype(bf16)


def terms(x, count):
    out = []
    for _ in range(count):
        hi = x.astype(bf16).astype(f32)
        out.append(hi)
        x = x - hi
    return jnp.concatenate(out, axis=0).astype(bf16)


def gathered(x, onehot, count):
    rows = x.shape[0]
    wide = dot(terms(x, count), onehot)
    return sum(wide[i * rows : (i + 1) * rows] for i in range(count))


def ones_where(mask):
    return jnp.where(mask, 1.0, 0.0).astype(bf16)


def dot3(a_hi, a_lo, b):
    b_hi, b_lo = split(b)
    return dot(a_hi, b_hi) + (dot(a_hi, b_lo) + dot(a_lo, b_hi))


def column(row):
    eye = iota((128, 128), 0) == iota((128, 128), 1)
    return jnp.sum(jnp.where(eye, row, 0.0), axis=1, keepdims=True)


def kernel(
    sizes,
    count_ref,
    pos_hbm,
    species_hbm,
    sends_hbm,
    neigh_hbm,
    embed_hbm,
    readout_hbm,
    rin_hbm,
    rout_hbm,
    up_hbm,
    skip_hbm,
    mix_hbm,
    energy_ref,
    force_ref,
    pos_ref,
    species_ref,
    sends_ref,
    neigh_ref,
    embed_ref,
    readout_ref,
    rin_ref,
    rout_ref,
    up_ref,
    skip_ref,
    mix_ref,
    own_ref,
    s1_ref,
    r1_plane,
    r1_above,
    s2_ref,
    r2_plane,
    r2_above,
    s3_plane,
    s3_above,
    r3_plane,
    r3_above,
    s4_ref,
    r4_plane,
    r4_above,
    hot_ref,
    hot_t_ref,
    route_ref,
    route_t_ref,
    win_ref,
    wout_ref,
    pass_ref,
    pass_t_ref,
    tl_ref,
    dl_ref,
    dinv_ref,
    rad_ref,
    m_ref,
    a_ref,
    y_ref,
    inv_ref,
    dm_ref,
    dw_ref,
    red_ref,
    geo_ref,
    env_ref,
    load_sem,
    send_sem,
    recv_sem,
):
    r1, r2 = (r1_plane, r1_above), (r2_plane, r2_above)
    r3, r4 = (r3_plane, r3_above), (r4_plane, r4_above)

    def device(o):
        out = {}
        for axis, step in zip(AXES, o):
            here = lax.axis_index(axis)
            out[axis] = here if step == 0 else lax.rem(here + (sizes[axis] + step), sizes[axis])
        return out

    barrier = pltpu.get_barrier_semaphore()
    for o in SLOWEST_FIRST:
        pl.semaphore_signal(barrier, inc=1, device_id=device(o), device_id_type=MESH)
    loads = [
        pltpu.make_async_copy(src, dst, load_sem.at[i])
        for i, (src, dst) in enumerate(
            (
                (pos_hbm, pos_ref),
                (species_hbm, species_ref),
                (sends_hbm, sends_ref),
                (neigh_hbm, neigh_ref),
                (mix_hbm, mix_ref),
                (up_hbm, up_ref),
                (rout_hbm, rout_ref),
                (skip_hbm, skip_ref),
                (embed_hbm, embed_ref),
                (readout_hbm, readout_ref),
                (rin_hbm, rin_ref),
            )
        )
    ]
    for load in loads:
        load.start()

    def send(stage, source, inboxes, group):
        for o in group:
            part = 1 if o[2] else 0
            pltpu.make_async_remote_copy(
                src_ref=source(o),
                dst_ref=inboxes[part].at[SLOT[negated(o)]],
                send_sem=send_sem.at[stage, part],
                recv_sem=recv_sem.at[stage, part],
                device_id=device(o),
                device_id_type=MESH,
            ).start()

    def copies(stage, inboxes, part):
        return pltpu.make_async_remote_copy(
            src_ref=inboxes[part],
            dst_ref=inboxes[part],
            send_sem=send_sem.at[stage, part],
            recv_sem=recv_sem.at[stage, part],
            device_id=device((1, 0, 0)),
            device_id_type=MESH,
        )

    def wait_plane(stage, inboxes):
        copies(stage, inboxes, 0).wait_recv()

    def wait_above(stage, inboxes):
        copies(stage, inboxes, 1).wait_recv()

    for load in loads[:3]:
        load.wait()
    own_ref[0:3, :] = pos_ref[...]
    own_ref[3:4, :] = species_ref[...].astype(f32)
    lists = sends_ref[...].astype(f32)
    own_ref[4:8, :] = jnp.zeros((4, ATOMS), f32)
    own_index = jnp.concatenate([lists[n : n + 1] for n in (1, 0, 3, 2)], axis=1)
    own_index_z = jnp.concatenate([lists[n : n + 1] for n in (5, 4, 5, 4)], axis=1)
    wanted = jnp.concatenate([own_index, own_index_z], axis=1).astype(jnp.int32)
    chosen = gathered(own_ref[...], ones_where(iota((ATOMS, 256), 0) == wanted), 3)
    s1_ref[0:4, :] = chosen[0:4, 0:128]
    s1_ref[4:5, :] = own_index
    low = iota((1, 128), 1) < 64
    s1_ref[5:6, :] = jnp.where(low, chosen[0:1, 128:256], chosen[1:2, 128:256])
    s1_ref[6:7, :] = jnp.where(low, chosen[2:3, 128:256], chosen[3:4, 128:256])
    s1_ref[7:8, :] = own_index_z

    lane = iota((1, 128), 1)
    quarter = lane // 32
    live = jnp.where(iota((1, ATOMS), 1) < count_ref[0], 1.0, 0.0)
    live4 = jnp.concatenate([live] * 4, axis=1)

    pl.semaphore_wait(barrier, len(OFFSETS))
    send(0, lambda o: s1_ref, r1, SLOWEST_FIRST)

    loads[3].wait()
    neigh = neigh_ref[...]
    halves = jnp.concatenate([neigh >> 8, neigh & 255], axis=0).astype(f32).astype(bf16)
    sel_row = iota((128, SLOTS), 0)
    sel_col = iota((128, SLOTS), 1)
    chosen = dot(halves, ones_where(sel_row == 4 * (sel_col & 31) + (sel_col >> 8)))
    chosen = chosen[0:8] * 256.0 + chosen[8:16]
    group = iota((8, SLOTS), 0) == ((iota((8, SLOTS), 1) & 255) >> 5)
    neigh_row = jnp.sum(jnp.where(group, chosen, 0.0), axis=0, keepdims=True).astype(jnp.int32)

    def hot_step(i, carry):
        first = pl.multiple_of(i * 64, 64)
        hot_ref[pl.ds(first, 64), :] = ones_where(iota((64, SLOTS), 0) + i * 64 == neigh_row)
        return carry

    lax.fori_loop(0, TABLE // 64, hot_step, 0)

    def hot_t_step(i, carry):
        first = pl.multiple_of(i * 128, 128)
        slot = iota((128, 128), 0) + i * 128
        sel = ones_where(iota((128, 128), 1) == 4 * (slot & 31) + (slot >> 8))
        mine = dot_t(sel, halves)
        place_at = iota((128, 16), 1)
        mine = mine * jnp.where(place_at < 8, 256.0, 1.0)
        in_group = (place_at & 7) == (((iota((128, 16), 0) + i * 128) & 255) >> 5)
        mine = jnp.sum(jnp.where(in_group, mine, 0.0), axis=1, keepdims=True)
        hot_t_ref[pl.ds(first, 128), :] = ones_where(iota((128, TABLE), 1).astype(f32) == mine)
        return carry


    lax.fori_loop(0, SLOTS // 128, hot_t_step, 0)
    for load in loads[4:]:
        load.wait()
    wide_lane = iota((128, 128), 1)

    def stacked(x):
        hi = x.astype(bf16).astype(f32)
        return jnp.concatenate([hi, hi, x - hi, jnp.zeros_like(x)], axis=0)

    for layer in range(2):
        rin = jnp.concatenate([stacked(rin_ref[layer]), jnp.zeros((96, 64), f32)], axis=0)
        rin = jnp.concatenate([rin, jnp.zeros((128, 64), f32)], axis=1).T
        win_ref[layer] = rin[:64, :32].astype(bf16)
        halved = jnp.where(iota((64, 384), 1) < CHAN, 0.5, 1.0) * rout_ref[layer]
        wout_ref[layer] = stacked(halved).T[:, :192].astype(bf16)
    between = exact_dot(up_ref[1], mix_ref[0])
    pass_ref[0], pass_ref[1] = split(between)
    pass_t_ref[0], pass_t_ref[1] = split(between.T)
    embed = jnp.concatenate([embed_ref[...], jnp.zeros((2, 128), f32)], axis=0)
    embed3 = jnp.concatenate([embed, embed, embed, jnp.zeros((104, 128), f32)], axis=0)

    def three_terms(x):
        hi = x.astype(bf16).astype(f32)
        mid = (x - hi).astype(bf16).astype(f32)
        lo = x - hi - mid
        x = jnp.where(wide_lane < 8, hi, jnp.where(wide_lane < 16, mid, lo))
        return x[:, :32].astype(bf16)

    up_kinds = three_terms(exact_dot(up_ref[0], embed3, 1))
    skip_kinds = exact_dot(skip_ref[0], embed3, 1)
    skip_up_kinds = three_terms(exact_dot(up_ref[1], skip_kinds))
    ro1 = readout_ref[1:2, :]
    direct = readout_ref[0:1, :] + exact_dot(ro1, skip_ref[1])
    kinds_energy = jnp.broadcast_to(exact_dot(direct, skip_kinds), (128, 128))
    kinds_energy = three_terms(kinds_energy)[0:16]
    for ref, mixed in ((dl_ref, exact_dot(direct, mix_ref[0])), (tl_ref, exact_dot(ro1, mix_ref[1]))):
        for k in range(4):
            ref[k * 128 : (k + 1) * 128, :] = column(mixed[:, k * 128 : (k + 1) * 128]) * live

    def kind_hot(row):
        width = row.shape[1]
        sub = iota((32, width), 0)
        return ones_where(((sub & 7).astype(f32) == row) & (sub < 24))

    wait_plane(0, r1)

    def message(o):
        return r1[1 if o[2] else 0][SLOT[o]]

    def shift(section):
        step = jnp.where((quarter & 1) == 0, -4.0, 4.0)
        return jnp.where(iota((8, 128), 0) == section, step, 0.0)

    def picked(index, valid, lower, upper, edge):
        index = jnp.where(valid, index, -1.0).astype(jnp.int32)
        onehot = ones_where(iota((128, 128), 0) == index)
        out = gathered(jnp.concatenate([lower, upper], axis=0), onehot, 3)
        return jnp.where(lane < edge, out[0:8], out[8:16])

    def x_tile(oy, oz):
        return jnp.where(lane < 32, message((-1, oy, oz)), message((1, oy, oz))) + shift(0)

    def xy_tile(oz):
        lower, upper = message((0, -1, oz)), message((0, 1, oz))
        own_rows = jnp.where(lane < 96, lower, upper)
        ghosts = picked(own_rows[4:5] - 256.0, lane >= 64, x_tile(-1, oz), x_tile(1, oz), 96)
        return jnp.where(lane < 64, x_tile(0, oz), own_rows + ghosts + shift(1))

    ghost0 = xy_tile(0)
    moved = gathered(own_ref[...], hot_ref[0:ATOMS, :], 3)
    moved = moved + gathered(ghost0, hot_ref[ATOMS : ATOMS + 128, :], 3)

    def own_only(index):
        return jnp.where(index < 256.0, index + 1.0, 0.0)

    def looked_up(index, lowest, offset):
        inside = (index >= lowest) & (index < lowest + 32.0)
        return jnp.where(inside, index + offset, -1.0)

    def compose(keys, entries):
        depth = entries.shape[1]
        onehot = ones_where(iota((depth, keys.shape[1]), 0) == keys.astype(jnp.int32))
        entries = jnp.broadcast_to(entries, (8, depth)).astype(bf16)
        return dot(entries, onehot)[0:1]

    zero_row = jnp.zeros((1, 128), f32)
    x_entries = jnp.where(lane < 64, own_index + 1.0, 0.0)
    keys = []
    for dx, lowest in ((-1, 288.0), (1, 256.0)):
        key = looked_up(message((dx, 0, 0))[4:5], lowest, -256.0)
        keys.append(jnp.where(lane < 64, -1.0, key))
    found = compose(jnp.concatenate(keys, axis=1), x_entries)
    route = [
        jnp.where(lane < 64, own_index + 1.0, found[:, 0:128]),
        jnp.where(lane < 64, 0.0, own_only(own_index)),
        jnp.where(lane < 64, 0.0, found[:, 128:256]),
    ]
    keys, directs = [], []
    for n in range(10):
        dx, dy = n // 3 - 1, n % 3 - 1
        key, direct = zero_row - 1.0, zero_row
        if n == 4:
            direct = own_only(own_index_z)
        elif n < 9:
            if dy:
                lowest = 320.0 if dy > 0 else 352.0
                offset = 128.0 * (dx + 1) - 256.0
            else:
                lowest = 256.0 if dx > 0 else 288.0
                offset = -256.0
            key = looked_up(message((dx, dy, 0))[7:8], lowest, offset)
        keys.append(key)
        directs.append(direct)
    keys = [jnp.where(lane < 64, keys[n], keys[n + 1]) for n in range(0, 10, 2)]
    directs = [jnp.where(lane < 64, directs[n], directs[n + 1]) for n in range(0, 10, 2)]
    found = compose(jnp.concatenate(keys, axis=1), jnp.concatenate(route, axis=1))
    found = found + jnp.concatenate(directs, axis=1)
    route_row = jnp.concatenate(route + [found], axis=1).astype(jnp.int32)

    def route_step(i, carry):
        first = pl.multiple_of(i * 64, 64)
        route_ref[pl.ds(first, 64), :] = ones_where(iota((64, SLOTS), 0) + (i * 64 + 1) == route_row)
        return carry

    lax.fori_loop(0, ATOMS // 64, route_step, 0)

    wait_above(0, r1)
    lower, upper = message((0, 0, -1)), message((0, 0, 1))
    own_rows = jnp.where((quarter & 1) == 0, lower, upper)
    turned = pltpu.roll(own_rows, 64, 1)
    ghosts = picked(own_rows[7:8] - 256.0, lane < 64, xy_tile(-1), xy_tile(1), 32)
    own_rows = [own_rows[5:6], turned[5:6], own_rows[6:7], turned[6:7], jnp.zeros((4, 128), f32)]
    ghost1 = jnp.concatenate(own_rows, axis=0) + ghosts + shift(2)
    ghost1 = jnp.where(lane < 64, ghost1, 0.0)

    centres = jnp.concatenate([own_ref[...]] * 4, axis=1)
    is_coord = iota((8, SLOTS), 0) < 3
    moved = moved + gathered(ghost1, hot_ref[ATOMS + 128 : TABLE, :], 3)
    slots_own = moved - jnp.where(is_coord, centres, 0.0)
    for k in range(4):
        env_ref[env_row(k) : env_row(k) + 4, :] = slots_own[0:4, k * ATOMS : (k + 1) * ATOMS]
    spread_env = gathered(env_ref[...], route_ref[...], 3)
    in_first = (quarter & 1) == 0

    def packed(even, odd):
        out = []
        for half in range(2):
            if half == 0:
                both = jnp.where(lane < 64, even, pltpu.roll(odd, 64, 1))
            else:
                both = jnp.where(lane < 64, pltpu.roll(even, 64, 1), odd)
            out += packed_pair(both)
        return out

    def packed_pair(both):
        ahead, behind = pltpu.roll(both, 32, 1), pltpu.roll(both, 96, 1)
        return [
            jnp.where(in_first, both[0:4], ahead[4:8]),
            jnp.where(in_first, behind[0:4], both[4:8]),
        ]

    def unpacked_pair(first, second):
        ahead, behind = pltpu.roll(second, 32, 1), pltpu.roll(first, 96, 1)
        return jnp.concatenate(
            [jnp.where(in_first, first, ahead), jnp.where(in_first, behind, second)], axis=0
        )

    def unpacked(parts):
        low, high = unpacked_pair(parts[0], parts[1]), unpacked_pair(parts[2], parts[3])
        even = jnp.where(lane < 64, low, pltpu.roll(high, 64, 1))
        odd = jnp.where(lane < 64, pltpu.roll(low, 64, 1), high)
        return jnp.concatenate([even, odd], axis=0)

    def summed(inbox, group, count):
        parts = [None] * count
        for o in group:
            q = place(negated(o))[1] % count
            parts[q] = inbox[SLOT[o]] if parts[q] is None else parts[q] + inbox[SLOT[o]]
        return parts

    for g in range(8):
        even, odd = (spread_env[n : n + 8, g * 128 : (g + 1) * 128] for n in (0, 8))
        for q, x in enumerate(packed(even, odd)):
            s2_ref[4 * g + q] = x
    send(1, lambda o: s2_ref.at[4 * place(o)[0] + place(o)[1]], r2, SLOWEST_FIRST)

    def geometry(at, slots):
        width = slots.shape[1]
        lanes = slice(at, at + width)
        vx, vy, vz = slots[0:1], slots[1:2], slots[2:3]
        r_sq = vx * vx + vy * vy + vz * vz + 0.04
        inv = lax.rsqrt(r_sq)
        r = r_sq * inv
        ux, uy, uz = vx * inv, vy * inv, vz * inv
        geo_ref[0:1, lanes] = ux
        geo_ref[1:2, lanes] = uy
        geo_ref[2:3, lanes] = uz
        geo_ref[3:4, lanes] = inv
        harm = [
            ROOT3 * ux,
            ROOT3 * uy,
            ROOT3 * uz,
            ROOT15 * ux * uy,
            ROOT15 * uy * uz,
            0.5 * ROOT5 * (3.0 * uz * uz - 1.0),
            ROOT15 * ux * uz,
            0.5 * ROOT15 * (ux * ux - uy * uy),
        ]
        for m in range(8):
            y_ref[m, :, lanes] = jnp.broadcast_to(0.5 * harm[m], (8, width))
        x = r * 0.25
        order = (iota((8, width), 0) + 1).astype(f32)
        phase = order * x
        near = jnp.floor(phase + 0.5)
        part = phase - near
        sign = 1.0 - 2.0 * (near - 2.0 * jnp.floor(near * 0.5))
        angle = part * math.pi
        square = angle * angle
        sin = 1.0
        for k in (14, 12, 10, 8, 6, 4, 2):
            sin = 1.0 - square * sin * (1.0 / (k * (k + 1)))
        sin = sign * angle * sin
        cos = 1.0
        for k in (14, 12, 10, 8, 6, 4, 2):
            cos = 1.0 - square * cos * (1.0 / (k * (k - 1)))
        cos = sign * cos
        gap = 1.0 - x * x
        within = x < 1.0
        env = jnp.where(within, gap * gap, 0.0)
        env_d = jnp.where(within, -x * gap, 0.0)
        scale = math.sqrt(0.5)
        base = scale * sin * inv
        basis = base * env
        basis_d = (scale * (math.pi / 4.0) * order * cos * inv - base * inv) * env + base * env_d
        wide = jnp.concatenate([basis, basis_d], axis=1)
        hi = wide.astype(bf16).astype(f32)
        lo = wide - hi
        return jnp.concatenate([hi, lo, hi, jnp.zeros_like(hi)], axis=0).astype(bf16)

    def radial(at, layer, basis):
        width = basis.shape[1] // 2
        z = dot(win_ref[layer], basis)
        slope, z = z[:, width:], z[:, :width]
        gate = 1.0 / (1.0 + jnp.exp(-z))
        hidden = z * gate
        hidden_d = gate * (1.0 + z * (1.0 - gate)) * slope
        for half, x in enumerate((hidden, hidden_d)):
            hi, lo = split(x)
            rad_ref[half * 384 : (half + 1) * 384, at : at + width] = dot(
                wout_ref[layer], jnp.concatenate([hi, lo, hi], axis=0)
            )

    def tiles_of(at, width, count, tile):
        return [slice(at + k * width + tile * 128, at + k * width + tile * 128 + 128) for k in range(count)]

    def harmonics_of(s, y_shift):
        return [None] + [y_ref[n, :, s.start - y_shift : s.stop - y_shift] for n in range(8)]

    def moments(firsts, lanes, y_shift, folded):
        out = [[None] * 9 for _ in firsts]
        for s in lanes:
            y = harmonics_of(s, y_shift)
            for c, first in enumerate(firsts):
                m = m_ref[pl.ds(first, 8), s]
                weighted = [rad_ref[pl.ds(k * 128 + first, 8), s] * m for k in range(3)]
                for n in range(9):
                    x = weighted[0] if n == 0 else y[n] * weighted[DEGREE[n]]
                    out[c][n] = x if out[c][n] is None else out[c][n] + x
        if folded:
            out = [[x + pltpu.roll(x, 64, 1) for x in a] for a in out]
        return out

    def squares_of(a):
        return (
            a[0] * a[0],
            a[1] * a[1] + a[2] * a[2] + a[3] * a[3],
            a[4] * a[4] + a[5] * a[5] + a[6] * a[6] + a[7] * a[7] + a[8] * a[8],
        )

    def forward(parts, folded):
        def step(i, carry):
            firsts = [pl.multiple_of(i * 16 + 8 * c, 8) for c in range(2)]
            for lanes, a_at, inv_at in parts:
                cols = slice(inv_at, inv_at + 128)
                for first, a in zip(firsts, moments(firsts, lanes, 0, folded)):
                    for n in range(9):
                        a_ref[pl.ds(n * 128 + first, 8), a_at : a_at + 128] = a[n]
                    b = squares_of(a)
                    inv_ref[pl.ds(first, 8), cols] = a[0]
                    inv_ref[pl.ds(128 + first, 8), cols] = b[0]
                    inv_ref[pl.ds(256 + first, 8), cols] = b[1] * (1.0 / 3.0)
                    inv_ref[pl.ds(384 + first, 8), cols] = b[2] * (1.0 / 5.0)
            return carry

        lax.fori_loop(0, CHAN // 16, step, 0, unroll=8 if folded else 2)

    def moment_grads(first, a, grads, g_at):
        cols = slice(g_at, g_at + 128)
        factors = [
            2.0 * grads[pl.ds(128 + first, 8), cols],
            (2.0 / 3.0) * grads[pl.ds(256 + first, 8), cols],
            (2.0 / 5.0) * grads[pl.ds(384 + first, 8), cols],
        ]
        out = [x * factors[DEGREE[n]] for n, x in enumerate(a)]
        out[0] = out[0] + grads[pl.ds(first, 8), cols]
        return out

    def slot_grads(da, y):
        return [
            da[0],
            da[1] * y[1] + da[2] * y[2] + da[3] * y[3],
            (da[4] * y[4] + da[5] * y[5]) + (da[6] * y[6] + da[7] * y[7]) + da[8] * y[8],
        ]

    def next_layer(parts):
        def step(i, energies):
            firsts = [pl.multiple_of(i * 16 + 8 * c, 8) for c in range(2)]
            out = []
            for (lanes, a_at, t_at), energy in zip(parts, energies):
                cols = slice(t_at, t_at + 128)
                grads = []
                for first, a in zip(firsts, moments(firsts, lanes, NEXT, False)):
                    b = squares_of(a)
                    energy = (
                        energy
                        + a[0] * tl_ref[pl.ds(first, 8), cols]
                        + b[0] * tl_ref[pl.ds(128 + first, 8), cols]
                        + b[1] * ((1.0 / 3.0) * tl_ref[pl.ds(256 + first, 8), cols])
                        + b[2] * ((1.0 / 5.0) * tl_ref[pl.ds(384 + first, 8), cols])
                    )
                    da = moment_grads(first, a, tl_ref, t_at)
                    for n in range(9):
                        a_ref[pl.ds(n * 128 + first, 8), a_at : a_at + 128] = da[n]
                    grads.append(da)
                out.append(energy)
                for s in lanes:
                    y = harmonics_of(s, NEXT)
                    at = slice(s.start - NEXT, s.stop - NEXT)
                    dm = []
                    for first, da in zip(firsts, grads):
                        dw = slot_grads(da, y)
                        rad = [rad_ref[pl.ds(j * 128 + first, 8), s] for j in range(3)]
                        dm.append(dw[0] * rad[0] + dw[1] * rad[1] + dw[2] * rad[2])
                        for j in range(3):
                            dw_ref[pl.ds(j * 128 + first, 8), at] = dw[j]
                    hi, lo = split(jnp.concatenate(dm, axis=0))
                    both = pl.multiple_of(i * 16, 16)
                    dm_ref[pl.ds(both, 16), at] = hi
                    dm_ref[pl.ds(CHAN + both, 16), at] = lo
            return tuple(out)

        zero = jnp.zeros((8, 128), f32)
        return lax.fori_loop(0, CHAN // 16, step, (zero,) * len(parts))

    def backward(lanes, a_at, y_shift, grads=None, g_at=0):
        def step(i, totals):
            first = pl.multiple_of(i * 8, 8)
            da = [a_ref[pl.ds(n * 128 + first, 8), a_at : a_at + 128] for n in range(9)]
            if grads is not None:
                da = moment_grads(first, da, grads, g_at)
            out = []
            for k, s in enumerate(lanes):
                m = m_ref[pl.ds(first, 8), s]
                weighted = [rad_ref[pl.ds(j * 128 + first, 8), s] * m for j in range(3)]
                for n in range(1, 9):
                    out.append(totals[9 * k + n - 1] + da[n] * weighted[DEGREE[n]])
                if grads is None:
                    at = slice(s.start - y_shift, s.stop - y_shift)
                    dw = [dw_ref[pl.ds(j * 128 + first, 8), at] for j in range(3)]
                else:
                    dw = slot_grads(da, harmonics_of(s, y_shift))
                slope = [rad_ref[pl.ds(384 + j * 128 + first, 8), s] for j in range(3)]
                slope = dw[0] * slope[0] + dw[1] * slope[1] + dw[2] * slope[2]
                out.append(totals[9 * k + 8] + slope * m)
            return tuple(out)

        zero = jnp.zeros((8, 128), f32)
        totals = lax.fori_loop(0, CHAN // 8, step, (zero,) * (9 * len(lanes)), unroll=4 if len(lanes) == 4 else 8)
        for k, s in enumerate(lanes):
            for n in range(9):
                red_ref[n : n + 1, s] = jnp.sum(totals[9 * k + n], axis=0, keepdims=True)

    def vector_grads(at, width, y_shift):
        lanes = slice(at, at + width)
        geo = slice(at - y_shift, at - y_shift + width)
        g = [None] + [0.5 * red_ref[n : n + 1, lanes] for n in range(8)]
        slope = red_ref[8:9, lanes]
        ux, uy, uz, inv = (geo_ref[n : n + 1, geo] for n in range(4))
        gx = ROOT3 * g[1] + ROOT15 * (uy * g[4] + uz * g[7] + ux * g[8])
        gy = ROOT3 * g[2] + ROOT15 * (ux * g[4] + uz * g[5] - uy * g[8])
        gz = ROOT3 * g[3] + ROOT15 * (uy * g[5] + ux * g[7]) + (3.0 * ROOT5) * uz * g[6]
        along = slope - (ux * gx + uy * gy + uz * gz) * inv
        return [gx * inv + ux * along, gy * inv + uy * along, gz * inv + uz * along]

    route_row = route_row.astype(f32)
    for g in range(8):
        mine = column(route_row[:, g * 128 : (g + 1) * 128])
        route_t_ref[g * 128 : (g + 1) * 128, :] = ones_where(
            (iota((128, ATOMS), 1) + 1).astype(f32) == mine
        )
    own_tiles = [tiles_of(OWN, ATOMS, 4, t) for t in range(2)]
    near_tiles = tiles_of(NEAR, 128, 4, 0)
    far_tiles = tiles_of(FAR, 128, 2, 0)
    next_tiles = [tiles_of(NEXT, ATOMS, 4, t) for t in range(2)]
    basis_own = geometry(OWN, slots_own)
    radial(OWN, 0, basis_own)
    m_ref[:, OWN : OWN + SLOTS] = dot(up_kinds, kind_hot(slots_own[3:4])) * live4
    forward([(own_tiles[0], 0, 0), (own_tiles[1], 128, 128)], False)
    kinds = kind_hot(jnp.concatenate([own_ref[3:4, :], ghost0[3:4], ghost1[3:4]], axis=1))
    skip = dot(skip_up_kinds, kinds)
    energy = jnp.sum(dl_ref[...] * inv_ref[...], axis=0, keepdims=True)
    energy = energy + live * dot(kinds_energy, kinds[:, :ATOMS])[0:1]
    projected = skip[:, :ATOMS] + dot3(pass_ref[0], pass_ref[1], inv_ref[...])
    radial(NEXT, 1, basis_own)
    own_part = gathered(projected, hot_ref[0:ATOMS, :], 2)

    wait_plane(1, r2)

    near = unpacked(summed(r2_plane, PLANE, 4))
    slots_near = jnp.concatenate([near[env_row(k) : env_row(k) + 4] for k in range(4)], axis=1)
    radial(NEAR, 0, geometry(NEAR, slots_near))
    m_ref[:, NEAR:FAR] = dot(up_kinds, kind_hot(slots_near[3:4]))
    forward([(near_tiles, 256, 0)], False)
    mixed_near = dot3(pass_ref[0], pass_ref[1], inv_ref[:, 0:128])
    wait_above(1, r2)
    far = unpacked_pair(*summed(r2_above, ABOVE, 2))
    slots_far = jnp.concatenate([far[0:4], far[4:8]], axis=1)
    radial(FAR, 0, geometry(FAR, slots_far))
    m_ref[:, FAR:NEXT] = dot(up_kinds, kind_hot(slots_far[3:4]))
    forward([(far_tiles, 384, 128)], True)
    mixed_far = dot3(pass_ref[0], pass_ref[1], inv_ref[:, 128:256])
    projected = skip[:, ATOMS:] + jnp.concatenate([mixed_near, mixed_far], axis=1)

    m_ref[:, NEXT:LANES] = (own_part + gathered(projected, hot_ref[ATOMS:TABLE, :], 2)) * live4
    energies = next_layer([(next_tiles[0], 512, 0), (next_tiles[1], 640, 128)])
    energy_ref[...] = energy + jnp.sum(jnp.concatenate(energies, axis=1), axis=0, keepdims=True)

    def feature_grads(cols):
        wide = dot(dm_ref[...], hot_t_ref[:, cols])
        return wide[:CHAN] + wide[CHAN:]


    back_far = feature_grads(slice(384, TABLE))
    back_far = back_far + pltpu.roll(back_far, 64, 1)
    dinv_ref[:, 0:128] = dot3(pass_t_ref[0], pass_t_ref[1], back_far)
    backward(far_tiles, 384, 0, dinv_ref, 0)
    grads_far = vector_grads(FAR, 256, 0)
    zero_row = jnp.zeros((1, 128), f32)
    both = [x[:, t * 128 : (t + 1) * 128] if x is not None else zero_row for t in range(2) for x in grads_far + [None]]
    s3_above[0], s3_above[1] = packed_pair(jnp.concatenate(both, axis=0))
    send(2, lambda o: s3_above.at[place(negated(o))[1] % 2], r3, ABOVE)
    back = feature_grads(slice(0, 384))
    dinv_ref[:, 128:256] = dot3(pass_t_ref[0], pass_t_ref[1], back[:, 256:384])
    backward(near_tiles, 256, 0, dinv_ref, 128)
    grads_near = vector_grads(NEAR, 512, 0)
    halves = []
    for parity in range(2):
        both = [x[:, k * 128 : (k + 1) * 128] if x is not None else zero_row for k in (parity, parity + 2) for x in grads_near + [None]]
        halves.append(jnp.concatenate(both, axis=0))
    for q, x in enumerate(packed(*halves)):
        s3_plane[q] = x
    send(2, lambda o: s3_plane.at[place(negated(o))[1]], r3, PLANE)

    dinv_ref[...] = dot3(pass_t_ref[0], pass_t_ref[1], back[:, :ATOMS]) + dl_ref[...]
    for t in range(2):
        backward(own_tiles[t], 128 * t, 0, dinv_ref, 128 * t)
        backward(next_tiles[t], 512 + 128 * t, NEXT)
    grads = [a + b for a, b in zip(vector_grads(OWN, SLOTS, 0), vector_grads(NEXT, SLOTS, NEXT))]
    grads = jnp.concatenate(grads + [jnp.zeros((5, SLOTS), f32)], axis=0)

    def own_table_grads(x):
        own = gathered(x, hot_t_ref[:, 0:ATOMS], 2)
        for k in range(4):
            own = own - x[:, k * ATOMS : (k + 1) * ATOMS]
        return own

    def ghost_table_grads(x):
        return gathered(x, hot_t_ref[:, ATOMS:TABLE], 2)

    def merged(inbox, group, tiles):
        tiles = dict.fromkeys(tiles)
        for o in group:
            g, q = place(o)
            x = jnp.where(quarter == q, inbox[SLOT[o]], 0.0)
            tiles[g] = x if tiles[g] is None else tiles[g] + x
        return jnp.concatenate([tiles[g] for g in sorted(tiles)], axis=1)

    def merged_vectors(inbox, group, tiles):
        at = {place(o): inbox[SLOT[o]] for o in group}
        zero = jnp.zeros((4, 128), f32)
        return jnp.concatenate(
            [unpacked([at.get((g, q), zero) for q in range(4)]) for g in tiles], axis=1
        )

    def merged_rows(inbox, group, tiles):
        out = merged(inbox, group, tiles)
        return jnp.concatenate([out, jnp.zeros_like(out)], axis=0)

    def returned(stage, inboxes, merge):
        wait_plane(stage, inboxes)
        out = gathered(merge(inboxes[0], PLANE, range(3)), route_t_ref[0:384, :], 2)
        wait_above(stage, inboxes)
        return out + gathered(merge(inboxes[1], ABOVE, range(3, 8)), route_t_ref[384:SLOTS, :], 2)

    own_grads = own_table_grads(grads)
    ghost_grads = ghost_table_grads(grads)
    from_ghosts = returned(2, r3, merged_vectors)
    from_ghosts = jnp.concatenate(
        [from_ghosts[env_row(k) : env_row(k) + 4] for k in range(4)], axis=1
    )
    from_ghosts = jnp.concatenate([from_ghosts, jnp.zeros((4, SLOTS), f32)], axis=0)
    ghost_grads = (ghost_grads + ghost_table_grads(from_ghosts))[0:4]
    tail = ghost_grads[:, 128:256]
    s4_ref[1] = tail + pltpu.roll(tail, 64, 1)
    s4_ref[0] = ghost_grads[:, 0:128]
    send(3, lambda o: s4_ref.at[1 if o[2] else 0], r4, SLOWEST_FIRST)
    own_grads = own_grads + own_table_grads(from_ghosts)
    last = returned(3, r4, merged_rows)
    force_ref[...] = -(own_grads + last)[0:3]
    for stage, inboxes in enumerate((r1, r2, r3, r4)):
        for part in range(2):
            copies(stage, inboxes, part).wait_send()


def hand_over(energy_ref, force_ref, energy_out, force_out, sem):
    copies = [
        pltpu.make_async_copy(energy_ref, energy_out, sem.at[0]),
        pltpu.make_async_copy(force_ref, force_out, sem.at[1]),
    ]
    for copy in copies:
        copy.start()
    for copy in copies:
        copy.wait()


def body(
    sizes,
    positions,
    species,
    live_count,
    send_lists,
    neighbours,
    embed,
    radial_in,
    radial_out,
    w_up,
    w_skip,
    w_mix,
    readout,
):
    vmem = pl.BlockSpec(memory_space=pltpu.VMEM)
    hbm = pl.BlockSpec(memory_space=pltpu.HBM)
    energy, forces = pl.pallas_call(
        functools.partial(kernel, sizes),
        out_shape=(pltpu.VMEM((1, ATOMS), f32), pltpu.VMEM((3, ATOMS), f32)),
        in_specs=[pl.BlockSpec(memory_space=pltpu.SMEM)] + [hbm] * 11,
        out_specs=(vmem, vmem),
        scratch_shapes=[
            pltpu.VMEM((3, ATOMS), f32),
            pltpu.VMEM((1, ATOMS), jnp.int32),
            pltpu.VMEM((6, 32), jnp.int32),
            pltpu.VMEM((8, 128), jnp.int32),
            pltpu.VMEM((6, 128), f32),
            pltpu.VMEM((2, 128), f32),
            pltpu.VMEM((2, 8, 64), f32),
            pltpu.VMEM((2, 64, 384), f32),
            pltpu.VMEM((2, 128, 128), f32),
            pltpu.VMEM((2, 128, 128), f32),
            pltpu.VMEM((2, 128, 512), f32),
            pltpu.VMEM((8, ATOMS), f32),
            pltpu.VMEM((8, 128), f32),
            pltpu.VMEM((8, 8, 128), f32),
            pltpu.VMEM((18, 8, 128), f32),
            pltpu.VMEM((32, 4, 128), f32),
            pltpu.VMEM((8, 4, 128), f32),
            pltpu.VMEM((18, 4, 128), f32),
            pltpu.VMEM((4, 4, 128), f32),
            pltpu.VMEM((2, 4, 128), f32),
            pltpu.VMEM((8, 4, 128), f32),
            pltpu.VMEM((18, 4, 128), f32),
            pltpu.VMEM((2, 4, 128), f32),
            pltpu.VMEM((8, 4, 128), f32),
            pltpu.VMEM((18, 4, 128), f32),
            pltpu.VMEM((TABLE, SLOTS), bf16),
            pltpu.VMEM((SLOTS, TABLE), bf16),
            pltpu.VMEM((ATOMS, SLOTS), bf16),
            pltpu.VMEM((SLOTS, ATOMS), bf16),
            pltpu.VMEM((2, 64, 32), bf16),
            pltpu.VMEM((2, 384, 192), bf16),
            pltpu.VMEM((2, 128, 512), bf16),
            pltpu.VMEM((2, 512, 128), bf16),
            pltpu.VMEM((512, ATOMS), f32),
            pltpu.VMEM((512, ATOMS), f32),
            pltpu.VMEM((512, ATOMS), f32),
            pltpu.VMEM((768, LANES), f32),
            pltpu.VMEM((128, LANES), f32),
            pltpu.VMEM((1152, 768), f32),
            pltpu.VMEM((8, 8, NEXT), f32),
            pltpu.VMEM((512, ATOMS), f32),
            pltpu.VMEM((256, SLOTS), bf16),
            pltpu.VMEM((384, SLOTS), f32),
            pltpu.VMEM((16, LANES), f32),
            pltpu.VMEM((8, NEXT), f32),
            pltpu.VMEM((16, ATOMS), f32),
            pltpu.SemaphoreType.DMA((11,)),
            pltpu.SemaphoreType.DMA((4, 2)),
            pltpu.SemaphoreType.DMA((4, 2)),
        ],
        compiler_params=pltpu.CompilerParams(
            collective_id=0, has_side_effects=True, vmem_limit_bytes=VMEM_BYTES
        ),
        name="potential",
    )(
        live_count,
        *(
            pltpu.with_memory_space_constraint(x, pltpu.HBM)
            for x in (
                positions,
                species.reshape(1, ATOMS),
                send_lists,
                neighbours.reshape(8, 128),
                embed.T,
                readout,
                radial_in.transpose(0, 2, 1),
                radial_out.transpose(0, 2, 1),
                w_up,
                w_skip,
                w_mix,
            )
        ),
    )
    energy, forces = pl.pallas_call(
        hand_over,
        out_shape=(
            jax.ShapeDtypeStruct((1, ATOMS), f32),
            jax.ShapeDtypeStruct((3, ATOMS), f32),
        ),
        in_specs=[vmem, vmem],
        out_specs=(hbm, hbm),
        scratch_shapes=[pltpu.SemaphoreType.DMA((2,))],
        name="hand_over",
    )(*(pltpu.with_memory_space_constraint(x, pltpu.VMEM) for x in (energy, forces)))
    return energy.reshape(ATOMS), forces


def solution(mesh):
    sizes = {axis: mesh.shape[axis] for axis in AXES}
    split_all = ("gx", "gy", "gz")
    return jax.shard_map(
        functools.partial(body, sizes),
        mesh=mesh,
        in_specs=(
            P(None, split_all),
            P(split_all),
            P(split_all),
            P(None, split_all),
            P(split_all),
            P(),
            P(),
            P(),
            P(),
            P(),
            P(),
            P(),
        ),
        out_specs=(P(split_all), P(None, split_all)),
        check_vma=False,
    )
```

```python
import functools
import itertools
import math

import jax
import jax.numpy as jnp
from jax import lax
from jax.experimental import pallas as pl
from jax.experimental.pallas import tpu as pltpu
from jax.sharding import PartitionSpec as P

AXES = ("gx", "gy", "gz")
MESH = pl.DeviceIdType.MESH
OFFSETS = [o for o in itertools.product((-1, 0, 1), repeat=3) if any(o)]
PLANE = [o for o in OFFSETS if not o[2]]
ABOVE = [o for o in OFFSETS if o[2]]
SLOT = {o: j for j, o in enumerate(PLANE)} | {o: j for j, o in enumerate(ABOVE)}
SLOWEST_FIRST = sorted(OFFSETS, key=lambda o: (-sum(map(abs, o)), -abs(o[1]), -abs(o[0])))
PLANE.sort(key=SLOWEST_FIRST.index)
ABOVE.sort(key=SLOWEST_FIRST.index)
f32 = jnp.float32
bf16 = jnp.bfloat16
HIGHEST = lax.Precision.HIGHEST
ATOMS = 256
SLOTS = 1024
CHAN = 128
OWN, NEAR, FAR, NEXT = 0, 1024, 1536, 1792
LANES = 2816
TABLE = 512
VMEM_BYTES = 48 * 1024 * 1024
DEGREE = (0, 1, 1, 1, 2, 2, 2, 2, 2)
ROOT3 = math.sqrt(3.0)
ROOT5 = math.sqrt(5.0)
ROOT15 = math.sqrt(15.0)


def place(d):
    dx, dy, dz = d
    if dz:
        n = (dx + 1) * 3 + dy + 1
        return 3 + n // 2, (n % 2) * 2 + (0 if dz > 0 else 1)
    if dy:
        return dx + 1, 2 if dy > 0 else 3
    return 0, 0 if dx > 0 else 1


def env_row(k):
    return 4 * (k // 2) + 8 * (k % 2)


def negated(o):
    return (-o[0], -o[1], -o[2])


def iota(shape, dim):
    return lax.broadcasted_iota(jnp.int32, shape, dim)


def dot(a, b):
    return jnp.dot(a, b, preferred_element_type=f32)


def dot_t(a, b):
    return lax.dot_general(a, b, (((1,), (1,)), ((), ())), preferred_element_type=f32)


def exact_dot(a, b, dim=0):
    return lax.dot_general(
        a, b, (((1,), (dim,)), ((), ())), precision=HIGHEST, preferred_element_type=f32
    )


def split(x):
    hi = x.astype(bf16)
    return hi, (x - hi.astype(f32)).astype(bf16)


def terms(x, count):
    out = []
    for _ in range(count):
        hi = x.astype(bf16).astype(f32)
        out.append(hi)
        x = x - hi
    return jnp.concatenate(out, axis=0).astype(bf16)


def gathered(x, onehot, count):
    rows = x.shape[0]
    wide = dot(terms(x, count), onehot)
    return sum(wide[i * rows : (i + 1) * rows] for i in range(count))


def ones_where(mask):
    return jnp.where(mask, 1.0, 0.0).astype(bf16)


def dot3(a_hi, a_lo, b):
    b_hi, b_lo = split(b)
    return dot(a_hi, b_hi) + (dot(a_hi, b_lo) + dot(a_lo, b_hi))


def column(row):
    eye = iota((128, 128), 0) == iota((128, 128), 1)
    return jnp.sum(jnp.where(eye, row, 0.0), axis=1, keepdims=True)


def kernel(
    sizes,
    count_ref,
    pos_hbm,
    species_hbm,
    sends_hbm,
    neigh_hbm,
    embed_hbm,
    readout_hbm,
    rin_hbm,
    rout_hbm,
    up_hbm,
    skip_hbm,
    mix_hbm,
    energy_ref,
    force_ref,
    pos_ref,
    species_ref,
    sends_ref,
    neigh_ref,
    embed_ref,
    readout_ref,
    rin_ref,
    rout_ref,
    up_ref,
    skip_ref,
    mix_ref,
    own_ref,
    s1_ref,
    r1_plane,
    r1_above,
    s2_ref,
    r2_plane,
    r2_above,
    s3_plane,
    s3_above,
    r3_plane,
    r3_above,
    s4_ref,
    r4_plane,
    r4_above,
    hot_ref,
    hot_t_ref,
    route_ref,
    route_t_ref,
    win_ref,
    wout_ref,
    pass_ref,
    pass_t_ref,
    tl_ref,
    dl_ref,
    dinv_ref,
    rad_ref,
    m_ref,
    a_ref,
    y_ref,
    inv_ref,
    dm_ref,
    dw_ref,
    red_ref,
    geo_ref,
    env_ref,
    load_sem,
    send_sem,
    recv_sem,
):
    r1, r2 = (r1_plane, r1_above), (r2_plane, r2_above)
    r3, r4 = (r3_plane, r3_above), (r4_plane, r4_above)

    def device(o):
        out = {}
        for axis, step in zip(AXES, o):
            here = lax.axis_index(axis)
            out[axis] = here if step == 0 else lax.rem(here + (sizes[axis] + step), sizes[axis])
        return out

    barrier = pltpu.get_barrier_semaphore()
    for o in SLOWEST_FIRST:
        pl.semaphore_signal(barrier, inc=1, device_id=device(o), device_id_type=MESH)
    loads = [
        pltpu.make_async_copy(src, dst, load_sem.at[i])
        for i, (src, dst) in enumerate(
            (
                (pos_hbm, pos_ref),
                (species_hbm, species_ref),
                (sends_hbm, sends_ref),
                (neigh_hbm, neigh_ref),
                (mix_hbm, mix_ref),
                (up_hbm, up_ref),
                (rout_hbm, rout_ref),
                (skip_hbm, skip_ref),
                (embed_hbm, embed_ref),
                (readout_hbm, readout_ref),
                (rin_hbm, rin_ref),
            )
        )
    ]
    for load in loads:
        load.start()

    def send(stage, source, inboxes, group):
        for o in group:
            part = 1 if o[2] else 0
            pltpu.make_async_remote_copy(
                src_ref=source(o),
                dst_ref=inboxes[part].at[SLOT[negated(o)]],
                send_sem=send_sem.at[stage, part],
                recv_sem=recv_sem.at[stage, part],
                device_id=device(o),
                device_id_type=MESH,
            ).start()

    def copies(stage, inboxes, part):
        return pltpu.make_async_remote_copy(
            src_ref=inboxes[part],
            dst_ref=inboxes[part],
            send_sem=send_sem.at[stage, part],
            recv_sem=recv_sem.at[stage, part],
            device_id=device((1, 0, 0)),
            device_id_type=MESH,
        )

    def wait_plane(stage, inboxes):
        copies(stage, inboxes, 0).wait_recv()

    def wait_above(stage, inboxes):
        copies(stage, inboxes, 1).wait_recv()

    for load in loads[:3]:
        load.wait()
    own_ref[0:3, :] = pos_ref[...]
    own_ref[3:4, :] = species_ref[...].astype(f32)
    lists = sends_ref[...].astype(f32)
    own_ref[4:8, :] = jnp.zeros((4, ATOMS), f32)
    own_index = jnp.concatenate([lists[n : n + 1] for n in (1, 0, 3, 2)], axis=1)
    own_index_z = jnp.concatenate([lists[n : n + 1] for n in (5, 4, 5, 4)], axis=1)
    wanted = jnp.concatenate([own_index, own_index_z], axis=1).astype(jnp.int32)
    chosen = gathered(own_ref[...], ones_where(iota((ATOMS, 256), 0) == wanted), 3)
    s1_ref[0:4, :] = chosen[0:4, 0:128]
    s1_ref[4:5, :] = own_index
    low = iota((1, 128), 1) < 64
    s1_ref[5:6, :] = jnp.where(low, chosen[0:1, 128:256], chosen[1:2, 128:256])
    s1_ref[6:7, :] = jnp.where(low, chosen[2:3, 128:256], chosen[3:4, 128:256])
    s1_ref[7:8, :] = own_index_z

    lane = iota((1, 128), 1)
    quarter = lane // 32
    live = jnp.where(iota((1, ATOMS), 1) < count_ref[0], 1.0, 0.0)
    live4 = jnp.concatenate([live] * 4, axis=1)

    pl.semaphore_wait(barrier, len(OFFSETS))
    send(0, lambda o: s1_ref, r1, SLOWEST_FIRST)

    loads[3].wait()
    neigh = neigh_ref[...]
    halves = jnp.concatenate([neigh >> 8, neigh & 255], axis=0).astype(f32).astype(bf16)
    sel_row = iota((128, SLOTS), 0)
    sel_col = iota((128, SLOTS), 1)
    chosen = dot(halves, ones_where(sel_row == 4 * (sel_col & 31) + (sel_col >> 8)))
    chosen = chosen[0:8] * 256.0 + chosen[8:16]
    group = iota((8, SLOTS), 0) == ((iota((8, SLOTS), 1) & 255) >> 5)
    neigh_row = jnp.sum(jnp.where(group, chosen, 0.0), axis=0, keepdims=True).astype(jnp.int32)

    def hot_step(i, carry):
        first = pl.multiple_of(i * 64, 64)
        hot_ref[pl.ds(first, 64), :] = ones_where(iota((64, SLOTS), 0) + i * 64 == neigh_row)
        return carry

    lax.fori_loop(0, TABLE // 64, hot_step, 0)

    def hot_t_step(i, carry):
        first = pl.multiple_of(i * 128, 128)
        slot = iota((128, 128), 0) + i * 128
        sel = ones_where(iota((128, 128), 1) == 4 * (slot & 31) + (slot >> 8))
        mine = dot_t(sel, halves)
        place_at = iota((128, 16), 1)
        mine = mine * jnp.where(place_at < 8, 256.0, 1.0)
        in_group = (place_at & 7) == (((iota((128, 16), 0) + i * 128) & 255) >> 5)
        mine = jnp.sum(jnp.where(in_group, mine, 0.0), axis=1, keepdims=True)
        hot_t_ref[pl.ds(first, 128), :] = ones_where(iota((128, TABLE), 1).astype(f32) == mine)
        return carry


    lax.fori_loop(0, SLOTS // 128, hot_t_step, 0)
    for load in loads[4:]:
        load.wait()
    wide_lane = iota((128, 128), 1)

    def stacked(x):
        hi = x.astype(bf16).astype(f32)
        return jnp.concatenate([hi, hi, x - hi, jnp.zeros_like(x)], axis=0)

    for layer in range(2):
        rin = jnp.concatenate([stacked(rin_ref[layer]), jnp.zeros((96, 64), f32)], axis=0)
        rin = jnp.concatenate([rin, jnp.zeros((128, 64), f32)], axis=1).T
        win_ref[layer] = rin[:64, :32].astype(bf16)
        halved = jnp.where(iota((64, 384), 1) < CHAN, 0.5, 1.0) * rout_ref[layer]
        wout_ref[layer] = stacked(halved).T[:, :192].astype(bf16)
    between = exact_dot(up_ref[1], mix_ref[0])
    pass_ref[0], pass_ref[1] = split(between)
    pass_t_ref[0], pass_t_ref[1] = split(between.T)
    embed = jnp.concatenate([embed_ref[...], jnp.zeros((2, 128), f32)], axis=0)
    embed3 = jnp.concatenate([embed, embed, embed, jnp.zeros((104, 128), f32)], axis=0)

    def three_terms(x):
        hi = x.astype(bf16).astype(f32)
        mid = (x - hi).astype(bf16).astype(f32)
        lo = x - hi - mid
        x = jnp.where(wide_lane < 8, hi, jnp.where(wide_lane < 16, mid, lo))
        return x[:, :32].astype(bf16)

    up_kinds = three_terms(exact_dot(up_ref[0], embed3, 1))
    skip_kinds = exact_dot(skip_ref[0], embed3, 1)
    skip_up_kinds = three_terms(exact_dot(up_ref[1], skip_kinds))
    ro1 = readout_ref[1:2, :]
    direct = readout_ref[0:1, :] + exact_dot(ro1, skip_ref[1])
    kinds_energy = jnp.broadcast_to(exact_dot(direct, skip_kinds), (128, 128))
    kinds_energy = three_terms(kinds_energy)[0:16]
    for ref, mixed in ((dl_ref, exact_dot(direct, mix_ref[0])), (tl_ref, exact_dot(ro1, mix_ref[1]))):
        for k in range(4):
            ref[k * 128 : (k + 1) * 128, :] = column(mixed[:, k * 128 : (k + 1) * 128]) * live

    def kind_hot(row):
        width = row.shape[1]
        sub = iota((32, width), 0)
        return ones_where(((sub & 7).astype(f32) == row) & (sub < 24))

    wait_plane(0, r1)

    def message(o):
        return r1[1 if o[2] else 0][SLOT[o]]

    def shift(section):
        step = jnp.where((quarter & 1) == 0, -4.0, 4.0)
        return jnp.where(iota((8, 128), 0) == section, step, 0.0)

    def picked(index, valid, lower, upper, edge):
        index = jnp.where(valid, index, -1.0).astype(jnp.int32)
        onehot = ones_where(iota((128, 128), 0) == index)
        out = gathered(jnp.concatenate([lower, upper], axis=0), onehot, 3)
        return jnp.where(lane < edge, out[0:8], out[8:16])

    def x_tile(oy, oz):
        return jnp.where(lane < 32, message((-1, oy, oz)), message((1, oy, oz))) + shift(0)

    def xy_tile(oz):
        lower, upper = message((0, -1, oz)), message((0, 1, oz))
        own_rows = jnp.where(lane < 96, lower, upper)
        ghosts = picked(own_rows[4:5] - 256.0, lane >= 64, x_tile(-1, oz), x_tile(1, oz), 96)
        return jnp.where(lane < 64, x_tile(0, oz), own_rows + ghosts + shift(1))

    ghost0 = xy_tile(0)
    moved = gathered(own_ref[...], hot_ref[0:ATOMS, :], 3)
    moved = moved + gathered(ghost0, hot_ref[ATOMS : ATOMS + 128, :], 3)

    def own_only(index):
        return jnp.where(index < 256.0, index + 1.0, 0.0)

    def looked_up(index, lowest, offset):
        inside = (index >= lowest) & (index < lowest + 32.0)
        return jnp.where(inside, index + offset, -1.0)

    def compose(keys, entries):
        depth = entries.shape[1]
        onehot = ones_where(iota((depth, keys.shape[1]), 0) == keys.astype(jnp.int32))
        entries = jnp.broadcast_to(entries, (8, depth)).astype(bf16)
        return dot(entries, onehot)[0:1]

    zero_row = jnp.zeros((1, 128), f32)
    x_entries = jnp.where(lane < 64, own_index + 1.0, 0.0)
    keys = []
    for dx, lowest in ((-1, 288.0), (1, 256.0)):
        key = looked_up(message((dx, 0, 0))[4:5], lowest, -256.0)
        keys.append(jnp.where(lane < 64, -1.0, key))
    found = compose(jnp.concatenate(keys, axis=1), x_entries)
    route = [
        jnp.where(lane < 64, own_index + 1.0, found[:, 0:128]),
        jnp.where(lane < 64, 0.0, own_only(own_index)),
        jnp.where(lane < 64, 0.0, found[:, 128:256]),
    ]
    keys, directs = [], []
    for n in range(10):
        dx, dy = n // 3 - 1, n % 3 - 1
        key, direct = zero_row - 1.0, zero_row
        if n == 4:
            direct = own_only(own_index_z)
        elif n < 9:
            if dy:
                lowest = 320.0 if dy > 0 else 352.0
                offset = 128.0 * (dx + 1) - 256.0
            else:
                lowest = 256.0 if dx > 0 else 288.0
                offset = -256.0
            key = looked_up(message((dx, dy, 0))[7:8], lowest, offset)
        keys.append(key)
        directs.append(direct)
    keys = [jnp.where(lane < 64, keys[n], keys[n + 1]) for n in range(0, 10, 2)]
    directs = [jnp.where(lane < 64, directs[n], directs[n + 1]) for n in range(0, 10, 2)]
    found = compose(jnp.concatenate(keys, axis=1), jnp.concatenate(route, axis=1))
    found = found + jnp.concatenate(directs, axis=1)
    route_row = jnp.concatenate(route + [found], axis=1).astype(jnp.int32)

    def route_step(i, carry):
        first = pl.multiple_of(i * 64, 64)
        route_ref[pl.ds(first, 64), :] = ones_where(iota((64, SLOTS), 0) + (i * 64 + 1) == route_row)
        return carry

    lax.fori_loop(0, ATOMS // 64, route_step, 0)

    wait_above(0, r1)
    lower, upper = message((0, 0, -1)), message((0, 0, 1))
    own_rows = jnp.where((quarter & 1) == 0, lower, upper)
    turned = pltpu.roll(own_rows, 64, 1)
    ghosts = picked(own_rows[7:8] - 256.0, lane < 64, xy_tile(-1), xy_tile(1), 32)
    own_rows = [own_rows[5:6], turned[5:6], own_rows[6:7], turned[6:7], jnp.zeros((4, 128), f32)]
    ghost1 = jnp.concatenate(own_rows, axis=0) + ghosts + shift(2)
    ghost1 = jnp.where(lane < 64, ghost1, 0.0)

    centres = jnp.concatenate([own_ref[...]] * 4, axis=1)
    is_coord = iota((8, SLOTS), 0) < 3
    moved = moved + gathered(ghost1, hot_ref[ATOMS + 128 : TABLE, :], 3)
    slots_own = moved - jnp.where(is_coord, centres, 0.0)
    for k in range(4):
        env_ref[env_row(k) : env_row(k) + 4, :] = slots_own[0:4, k * ATOMS : (k + 1) * ATOMS]
    spread_env = gathered(env_ref[...], route_ref[...], 3)
    in_first = (quarter & 1) == 0

    def packed(even, odd):
        out = []
        for half in range(2):
            if half == 0:
                both = jnp.where(lane < 64, even, pltpu.roll(odd, 64, 1))
            else:
                both = jnp.where(lane < 64, pltpu.roll(even, 64, 1), odd)
            out += packed_pair(both)
        return out

    def packed_pair(both):
        ahead, behind = pltpu.roll(both, 32, 1), pltpu.roll(both, 96, 1)
        return [
            jnp.where(in_first, both[0:4], ahead[4:8]),
            jnp.where(in_first, behind[0:4], both[4:8]),
        ]

    def unpacked_pair(first, second):
        ahead, behind = pltpu.roll(second, 32, 1), pltpu.roll(first, 96, 1)
        return jnp.concatenate(
            [jnp.where(in_first, first, ahead), jnp.where(in_first, behind, second)], axis=0
        )

    def unpacked(parts):
        low, high = unpacked_pair(parts[0], parts[1]), unpacked_pair(parts[2], parts[3])
        even = jnp.where(lane < 64, low, pltpu.roll(high, 64, 1))
        odd = jnp.where(lane < 64, pltpu.roll(low, 64, 1), high)
        return jnp.concatenate([even, odd], axis=0)

    def summed(inbox, group, count):
        parts = [None] * count
        for o in group:
            q = place(negated(o))[1] % count
            parts[q] = inbox[SLOT[o]] if parts[q] is None else parts[q] + inbox[SLOT[o]]
        return parts

    for g in range(8):
        even, odd = (spread_env[n : n + 8, g * 128 : (g + 1) * 128] for n in (0, 8))
        for q, x in enumerate(packed(even, odd)):
            s2_ref[4 * g + q] = x
    send(1, lambda o: s2_ref.at[4 * place(o)[0] + place(o)[1]], r2, SLOWEST_FIRST)

    def geometry(at, slots):
        width = slots.shape[1]
        lanes = slice(at, at + width)
        vx, vy, vz = slots[0:1], slots[1:2], slots[2:3]
        r_sq = vx * vx + vy * vy + vz * vz + 0.04
        inv = lax.rsqrt(r_sq)
        r = r_sq * inv
        ux, uy, uz = vx * inv, vy * inv, vz * inv
        geo_ref[0:1, lanes] = ux
        geo_ref[1:2, lanes] = uy
        geo_ref[2:3, lanes] = uz
        geo_ref[3:4, lanes] = inv
        harm = [
            ROOT3 * ux,
            ROOT3 * uy,
            ROOT3 * uz,
            ROOT15 * ux * uy,
            ROOT15 * uy * uz,
            0.5 * ROOT5 * (3.0 * uz * uz - 1.0),
            ROOT15 * ux * uz,
            0.5 * ROOT15 * (ux * ux - uy * uy),
        ]
        for m in range(8):
            y_ref[m, :, lanes] = jnp.broadcast_to(0.5 * harm[m], (8, width))
        x = r * 0.25
        order = (iota((8, width), 0) + 1).astype(f32)
        phase = order * x
        near = jnp.floor(phase + 0.5)
        part = phase - near
        sign = 1.0 - 2.0 * (near - 2.0 * jnp.floor(near * 0.5))
        angle = part * math.pi
        square = angle * angle
        sin = 1.0
        for k in (14, 12, 10, 8, 6, 4, 2):
            sin = 1.0 - square * sin * (1.0 / (k * (k + 1)))
        sin = sign * angle * sin
        cos = 1.0
        for k in (14, 12, 10, 8, 6, 4, 2):
            cos = 1.0 - square * cos * (1.0 / (k * (k - 1)))
        cos = sign * cos
        gap = 1.0 - x * x
        within = x < 1.0
        env = jnp.where(within, gap * gap, 0.0)
        env_d = jnp.where(within, -x * gap, 0.0)
        scale = math.sqrt(0.5)
        base = scale * sin * inv
        basis = base * env
        basis_d = (scale * (math.pi / 4.0) * order * cos * inv - base * inv) * env + base * env_d
        wide = jnp.concatenate([basis, basis_d], axis=1)
        hi = wide.astype(bf16).astype(f32)
        lo = wide - hi
        return jnp.concatenate([hi, lo, hi, jnp.zeros_like(hi)], axis=0).astype(bf16)

    def radial(at, layer, basis):
        width = basis.shape[1] // 2
        z = dot(win_ref[layer], basis)
        slope, z = z[:, width:], z[:, :width]
        gate = 1.0 / (1.0 + jnp.exp(-z))
        hidden = z * gate
        hidden_d = gate * (1.0 + z * (1.0 - gate)) * slope
        for half, x in enumerate((hidden, hidden_d)):
            hi, lo = split(x)
            rad_ref[half * 384 : (half + 1) * 384, at : at + width] = dot(
                wout_ref[layer], jnp.concatenate([hi, lo, hi], axis=0)
            )

    def tiles_of(at, width, count, tile):
        return [slice(at + k * width + tile * 128, at + k * width + tile * 128 + 128) for k in range(count)]

    def harmonics_of(s, y_shift):
        return [None] + [y_ref[n, :, s.start - y_shift : s.stop - y_shift] for n in range(8)]

    def moments(firsts, lanes, y_shift, folded):
        out = [[None] * 9 for _ in firsts]
        for s in lanes:
            y = harmonics_of(s, y_shift)
            for c, first in enumerate(firsts):
                m = m_ref[pl.ds(first, 8), s]
                weighted = [rad_ref[pl.ds(k * 128 + first, 8), s] * m for k in range(3)]
                for n in range(9):
                    x = weighted[0] if n == 0 else y[n] * weighted[DEGREE[n]]
                    out[c][n] = x if out[c][n] is None else out[c][n] + x
        if folded:
            out = [[x + pltpu.roll(x, 64, 1) for x in a] for a in out]
        return out

    def squares_of(a):
        return (
            a[0] * a[0],
            a[1] * a[1] + a[2] * a[2] + a[3] * a[3],
            a[4] * a[4] + a[5] * a[5] + a[6] * a[6] + a[7] * a[7] + a[8] * a[8],
        )

    def forward(parts, folded):
        def step(i, carry):
            firsts = [pl.multiple_of(i * 16 + 8 * c, 8) for c in range(2)]
            for lanes, a_at, inv_at in parts:
                cols = slice(inv_at, inv_at + 128)
                for first, a in zip(firsts, moments(firsts, lanes, 0, folded)):
                    for n in range(9):
                        a_ref[pl.ds(n * 128 + first, 8), a_at : a_at + 128] = a[n]
                    b = squares_of(a)
                    inv_ref[pl.ds(first, 8), cols] = a[0]
                    inv_ref[pl.ds(128 + first, 8), cols] = b[0]
                    inv_ref[pl.ds(256 + first, 8), cols] = b[1] * (1.0 / 3.0)
                    inv_ref[pl.ds(384 + first, 8), cols] = b[2] * (1.0 / 5.0)
            return carry

        lax.fori_loop(0, CHAN // 16, step, 0, unroll=8 if folded else 2)

    def moment_grads(first, a, grads, g_at):
        cols = slice(g_at, g_at + 128)
        factors = [
            2.0 * grads[pl.ds(128 + first, 8), cols],
            (2.0 / 3.0) * grads[pl.ds(256 + first, 8), cols],
            (2.0 / 5.0) * grads[pl.ds(384 + first, 8), cols],
        ]
        out = [x * factors[DEGREE[n]] for n, x in enumerate(a)]
        out[0] = out[0] + grads[pl.ds(first, 8), cols]
        return out

    def slot_grads(da, y):
        return [
            da[0],
            da[1] * y[1] + da[2] * y[2] + da[3] * y[3],
            (da[4] * y[4] + da[5] * y[5]) + (da[6] * y[6] + da[7] * y[7]) + da[8] * y[8],
        ]

    def next_layer(parts):
        def step(i, energies):
            firsts = [pl.multiple_of(i * 16 + 8 * c, 8) for c in range(2)]
            out = []
            for (lanes, a_at, t_at), energy in zip(parts, energies):
                cols = slice(t_at, t_at + 128)
                grads = []
                for first, a in zip(firsts, moments(firsts, lanes, NEXT, False)):
                    b = squares_of(a)
                    energy = (
                        energy
                        + a[0] * tl_ref[pl.ds(first, 8), cols]
                        + b[0] * tl_ref[pl.ds(128 + first, 8), cols]
                        + b[1] * ((1.0 / 3.0) * tl_ref[pl.ds(256 + first, 8), cols])
                        + b[2] * ((1.0 / 5.0) * tl_ref[pl.ds(384 + first, 8), cols])
                    )
                    da = moment_grads(first, a, tl_ref, t_at)
                    for n in range(9):
                        a_ref[pl.ds(n * 128 + first, 8), a_at : a_at + 128] = da[n]
                    grads.append(da)
                out.append(energy)
                for s in lanes:
                    y = harmonics_of(s, NEXT)
                    at = slice(s.start - NEXT, s.stop - NEXT)
                    dm = []
                    for first, da in zip(firsts, grads):
                        dw = slot_grads(da, y)
                        rad = [rad_ref[pl.ds(j * 128 + first, 8), s] for j in range(3)]
                        dm.append(dw[0] * rad[0] + dw[1] * rad[1] + dw[2] * rad[2])
                        for j in range(3):
                            dw_ref[pl.ds(j * 128 + first, 8), at] = dw[j]
                    hi, lo = split(jnp.concatenate(dm, axis=0))
                    both = pl.multiple_of(i * 16, 16)
                    dm_ref[pl.ds(both, 16), at] = hi
                    dm_ref[pl.ds(CHAN + both, 16), at] = lo
            return tuple(out)

        zero = jnp.zeros((8, 128), f32)
        return lax.fori_loop(0, CHAN // 16, step, (zero,) * len(parts))

    def backward(lanes, a_at, y_shift, grads=None, g_at=0):
        def step(i, totals):
            first = pl.multiple_of(i * 8, 8)
            da = [a_ref[pl.ds(n * 128 + first, 8), a_at : a_at + 128] for n in range(9)]
            if grads is not None:
                da = moment_grads(first, da, grads, g_at)
            out = []
            for k, s in enumerate(lanes):
                m = m_ref[pl.ds(first, 8), s]
                weighted = [rad_ref[pl.ds(j * 128 + first, 8), s] * m for j in range(3)]
                for n in range(1, 9):
                    out.append(totals[9 * k + n - 1] + da[n] * weighted[DEGREE[n]])
                if grads is None:
                    at = slice(s.start - y_shift, s.stop - y_shift)
                    dw = [dw_ref[pl.ds(j * 128 + first, 8), at] for j in range(3)]
                else:
                    dw = slot_grads(da, harmonics_of(s, y_shift))
                slope = [rad_ref[pl.ds(384 + j * 128 + first, 8), s] for j in range(3)]
                slope = dw[0] * slope[0] + dw[1] * slope[1] + dw[2] * slope[2]
                out.append(totals[9 * k + 8] + slope * m)
            return tuple(out)

        zero = jnp.zeros((8, 128), f32)
        totals = lax.fori_loop(0, CHAN // 8, step, (zero,) * (9 * len(lanes)), unroll=4 if len(lanes) == 4 else 8)
        for k, s in enumerate(lanes):
            for n in range(9):
                red_ref[n : n + 1, s] = jnp.sum(totals[9 * k + n], axis=0, keepdims=True)

    def vector_grads(at, width, y_shift):
        lanes = slice(at, at + width)
        geo = slice(at - y_shift, at - y_shift + width)
        g = [None] + [0.5 * red_ref[n : n + 1, lanes] for n in range(8)]
        slope = red_ref[8:9, lanes]
        ux, uy, uz, inv = (geo_ref[n : n + 1, geo] for n in range(4))
        gx = ROOT3 * g[1] + ROOT15 * (uy * g[4] + uz * g[7] + ux * g[8])
        gy = ROOT3 * g[2] + ROOT15 * (ux * g[4] + uz * g[5] - uy * g[8])
        gz = ROOT3 * g[3] + ROOT15 * (uy * g[5] + ux * g[7]) + (3.0 * ROOT5) * uz * g[6]
        along = slope - (ux * gx + uy * gy + uz * gz) * inv
        return [gx * inv + ux * along, gy * inv + uy * along, gz * inv + uz * along]

    route_row = route_row.astype(f32)
    for g in range(8):
        mine = column(route_row[:, g * 128 : (g + 1) * 128])
        route_t_ref[g * 128 : (g + 1) * 128, :] = ones_where(
            (iota((128, ATOMS), 1) + 1).astype(f32) == mine
        )
    own_tiles = [tiles_of(OWN, ATOMS, 4, t) for t in range(2)]
    near_tiles = tiles_of(NEAR, 128, 4, 0)
    far_tiles = tiles_of(FAR, 128, 2, 0)
    next_tiles = [tiles_of(NEXT, ATOMS, 4, t) for t in range(2)]
    basis_own = geometry(OWN, slots_own)
    radial(OWN, 0, basis_own)
    m_ref[:, OWN : OWN + SLOTS] = dot(up_kinds, kind_hot(slots_own[3:4])) * live4
    forward([(own_tiles[0], 0, 0), (own_tiles[1], 128, 128)], False)
    kinds = kind_hot(jnp.concatenate([own_ref[3:4, :], ghost0[3:4], ghost1[3:4]], axis=1))
    skip = dot(skip_up_kinds, kinds)
    energy = jnp.sum(dl_ref[...] * inv_ref[...], axis=0, keepdims=True)
    energy = energy + live * dot(kinds_energy, kinds[:, :ATOMS])[0:1]
    projected = skip[:, :ATOMS] + dot3(pass_ref[0], pass_ref[1], inv_ref[...])
    radial(NEXT, 1, basis_own)
    own_part = gathered(projected, hot_ref[0:ATOMS, :], 2)

    wait_plane(1, r2)

    near = unpacked(summed(r2_plane, PLANE, 4))
    slots_near = jnp.concatenate([near[env_row(k) : env_row(k) + 4] for k in range(4)], axis=1)
    radial(NEAR, 0, geometry(NEAR, slots_near))
    m_ref[:, NEAR:FAR] = dot(up_kinds, kind_hot(slots_near[3:4]))
    forward([(near_tiles, 256, 0)], False)
    mixed_near = dot3(pass_ref[0], pass_ref[1], inv_ref[:, 0:128])
    wait_above(1, r2)
    far = unpacked_pair(*summed(r2_above, ABOVE, 2))
    slots_far = jnp.concatenate([far[0:4], far[4:8]], axis=1)
    radial(FAR, 0, geometry(FAR, slots_far))
    m_ref[:, FAR:NEXT] = dot(up_kinds, kind_hot(slots_far[3:4]))
    forward([(far_tiles, 384, 128)], True)
    mixed_far = dot3(pass_ref[0], pass_ref[1], inv_ref[:, 128:256])
    projected = skip[:, ATOMS:] + jnp.concatenate([mixed_near, mixed_far], axis=1)

    m_ref[:, NEXT:LANES] = (own_part + gathered(projected, hot_ref[ATOMS:TABLE, :], 2)) * live4
    energies = next_layer([(next_tiles[0], 512, 0), (next_tiles[1], 640, 128)])
    energy_ref[...] = energy + jnp.sum(jnp.concatenate(energies, axis=1), axis=0, keepdims=True)

    def feature_grads(cols):
        wide = dot(dm_ref[...], hot_t_ref[:, cols])
        return wide[:CHAN] + wide[CHAN:]


    back_far = feature_grads(slice(384, TABLE))
    back_far = back_far + pltpu.roll(back_far, 64, 1)
    dinv_ref[:, 0:128] = dot3(pass_t_ref[0], pass_t_ref[1], back_far)
    backward(far_tiles, 384, 0, dinv_ref, 0)
    grads_far = vector_grads(FAR, 256, 0)
    zero_row = jnp.zeros((1, 128), f32)
    both = [x[:, t * 128 : (t + 1) * 128] if x is not None else zero_row for t in range(2) for x in grads_far + [None]]
    s3_above[0], s3_above[1] = packed_pair(jnp.concatenate(both, axis=0))
    send(2, lambda o: s3_above.at[place(negated(o))[1] % 2], r3, ABOVE)
    back_near = feature_grads(slice(ATOMS, 384))
    dinv_ref[:, 128:256] = dot3(pass_t_ref[0], pass_t_ref[1], back_near)
    backward(near_tiles, 256, 0, dinv_ref, 128)
    grads_near = vector_grads(NEAR, 512, 0)
    halves = []
    for parity in range(2):
        both = [x[:, k * 128 : (k + 1) * 128] if x is not None else zero_row for k in (parity, parity + 2) for x in grads_near + [None]]
        halves.append(jnp.concatenate(both, axis=0))
    for q, x in enumerate(packed(*halves)):
        s3_plane[q] = x
    send(2, lambda o: s3_plane.at[place(negated(o))[1]], r3, PLANE)

    dinv_ref[...] = dot3(pass_t_ref[0], pass_t_ref[1], feature_grads(slice(0, ATOMS))) + dl_ref[...]
    for t in range(2):
        backward(own_tiles[t], 128 * t, 0, dinv_ref, 128 * t)
        backward(next_tiles[t], 512 + 128 * t, NEXT)
    grads = [a + b for a, b in zip(vector_grads(OWN, SLOTS, 0), vector_grads(NEXT, SLOTS, NEXT))]
    grads = jnp.concatenate(grads + [jnp.zeros((5, SLOTS), f32)], axis=0)

    def own_table_grads(x):
        own = gathered(x, hot_t_ref[:, 0:ATOMS], 2)
        for k in range(4):
            own = own - x[:, k * ATOMS : (k + 1) * ATOMS]
        return own

    def ghost_table_grads(x):
        return gathered(x, hot_t_ref[:, ATOMS:TABLE], 2)

    def merged(inbox, group, tiles):
        tiles = dict.fromkeys(tiles)
        for o in group:
            g, q = place(o)
            x = jnp.where(quarter == q, inbox[SLOT[o]], 0.0)
            tiles[g] = x if tiles[g] is None else tiles[g] + x
        return jnp.concatenate([tiles[g] for g in sorted(tiles)], axis=1)

    def merged_vectors(inbox, group, tiles):
        at = {place(o): inbox[SLOT[o]] for o in group}
        zero = jnp.zeros((4, 128), f32)
        return jnp.concatenate(
            [unpacked([at.get((g, q), zero) for q in range(4)]) for g in tiles], axis=1
        )

    def merged_rows(inbox, group, tiles):
        out = merged(inbox, group, tiles)
        return jnp.concatenate([out, jnp.zeros_like(out)], axis=0)

    def returned(stage, inboxes, merge):
        wait_plane(stage, inboxes)
        out = gathered(merge(inboxes[0], PLANE, range(3)), route_t_ref[0:384, :], 2)
        wait_above(stage, inboxes)
        return out + gathered(merge(inboxes[1], ABOVE, range(3, 8)), route_t_ref[384:SLOTS, :], 2)

    own_grads = own_table_grads(grads)
    ghost_grads = ghost_table_grads(grads)
    from_ghosts = returned(2, r3, merged_vectors)
    from_ghosts = jnp.concatenate(
        [from_ghosts[env_row(k) : env_row(k) + 4] for k in range(4)], axis=1
    )
    from_ghosts = jnp.concatenate([from_ghosts, jnp.zeros((4, SLOTS), f32)], axis=0)
    ghost_grads = (ghost_grads + ghost_table_grads(from_ghosts))[0:4]
    tail = ghost_grads[:, 128:256]
    s4_ref[1] = tail + pltpu.roll(tail, 64, 1)
    s4_ref[0] = ghost_grads[:, 0:128]
    send(3, lambda o: s4_ref.at[1 if o[2] else 0], r4, SLOWEST_FIRST)
    own_grads = own_grads + own_table_grads(from_ghosts)
    last = returned(3, r4, merged_rows)
    force_ref[...] = -(own_grads + last)[0:3]
    for stage, inboxes in enumerate((r1, r2, r3, r4)):
        for part in range(2):
            copies(stage, inboxes, part).wait_send()


def hand_over(energy_ref, force_ref, energy_out, force_out, sem):
    copies = [
        pltpu.make_async_copy(energy_ref, energy_out, sem.at[0]),
        pltpu.make_async_copy(force_ref, force_out, sem.at[1]),
    ]
    for copy in copies:
        copy.start()
    for copy in copies:
        copy.wait()


def body(
    sizes,
    positions,
    species,
    live_count,
    send_lists,
    neighbours,
    embed,
    radial_in,
    radial_out,
    w_up,
    w_skip,
    w_mix,
    readout,
):
    vmem = pl.BlockSpec(memory_space=pltpu.VMEM)
    hbm = pl.BlockSpec(memory_space=pltpu.HBM)
    energy, forces = pl.pallas_call(
        functools.partial(kernel, sizes),
        out_shape=(pltpu.VMEM((1, ATOMS), f32), pltpu.VMEM((3, ATOMS), f32)),
        in_specs=[pl.BlockSpec(memory_space=pltpu.SMEM)] + [hbm] * 11,
        out_specs=(vmem, vmem),
        scratch_shapes=[
            pltpu.VMEM((3, ATOMS), f32),
            pltpu.VMEM((1, ATOMS), jnp.int32),
            pltpu.VMEM((6, 32), jnp.int32),
            pltpu.VMEM((8, 128), jnp.int32),
            pltpu.VMEM((6, 128), f32),
            pltpu.VMEM((2, 128), f32),
            pltpu.VMEM((2, 8, 64), f32),
            pltpu.VMEM((2, 64, 384), f32),
            pltpu.VMEM((2, 128, 128), f32),
            pltpu.VMEM((2, 128, 128), f32),
            pltpu.VMEM((2, 128, 512), f32),
            pltpu.VMEM((8, ATOMS), f32),
            pltpu.VMEM((8, 128), f32),
            pltpu.VMEM((8, 8, 128), f32),
            pltpu.VMEM((18, 8, 128), f32),
            pltpu.VMEM((32, 4, 128), f32),
            pltpu.VMEM((8, 4, 128), f32),
            pltpu.VMEM((18, 4, 128), f32),
            pltpu.VMEM((4, 4, 128), f32),
            pltpu.VMEM((2, 4, 128), f32),
            pltpu.VMEM((8, 4, 128), f32),
            pltpu.VMEM((18, 4, 128), f32),
            pltpu.VMEM((2, 4, 128), f32),
            pltpu.VMEM((8, 4, 128), f32),
            pltpu.VMEM((18, 4, 128), f32),
            pltpu.VMEM((TABLE, SLOTS), bf16),
            pltpu.VMEM((SLOTS, TABLE), bf16),
            pltpu.VMEM((ATOMS, SLOTS), bf16),
            pltpu.VMEM((SLOTS, ATOMS), bf16),
            pltpu.VMEM((2, 64, 32), bf16),
            pltpu.VMEM((2, 384, 192), bf16),
            pltpu.VMEM((2, 128, 512), bf16),
            pltpu.VMEM((2, 512, 128), bf16),
            pltpu.VMEM((512, ATOMS), f32),
            pltpu.VMEM((512, ATOMS), f32),
            pltpu.VMEM((512, ATOMS), f32),
            pltpu.VMEM((768, LANES), f32),
            pltpu.VMEM((128, LANES), f32),
            pltpu.VMEM((1152, 768), f32),
            pltpu.VMEM((8, 8, NEXT), f32),
            pltpu.VMEM((512, ATOMS), f32),
            pltpu.VMEM((256, SLOTS), bf16),
            pltpu.VMEM((384, SLOTS), f32),
            pltpu.VMEM((16, LANES), f32),
            pltpu.VMEM((8, NEXT), f32),
            pltpu.VMEM((16, ATOMS), f32),
            pltpu.SemaphoreType.DMA((11,)),
            pltpu.SemaphoreType.DMA((4, 2)),
            pltpu.SemaphoreType.DMA((4, 2)),
        ],
        compiler_params=pltpu.CompilerParams(
            collective_id=0, has_side_effects=True, vmem_limit_bytes=VMEM_BYTES
        ),
        name="potential",
    )(
        live_count,
        *(
            pltpu.with_memory_space_constraint(x, pltpu.HBM)
            for x in (
                positions,
                species.reshape(1, ATOMS),
                send_lists,
                neighbours.reshape(8, 128),
                embed.T,
                readout,
                radial_in.transpose(0, 2, 1),
                radial_out.transpose(0, 2, 1),
                w_up,
                w_skip,
                w_mix,
            )
        ),
    )
    energy, forces = pl.pallas_call(
        hand_over,
        out_shape=(
            jax.ShapeDtypeStruct((1, ATOMS), f32),
            jax.ShapeDtypeStruct((3, ATOMS), f32),
        ),
        in_specs=[vmem, vmem],
        out_specs=(hbm, hbm),
        scratch_shapes=[pltpu.SemaphoreType.DMA((2,))],
        name="hand_over",
    )(*(pltpu.with_memory_space_constraint(x, pltpu.VMEM) for x in (energy, forces)))
    return energy.reshape(ATOMS), forces


def solution(mesh):
    sizes = {axis: mesh.shape[axis] for axis in AXES}
    split_all = ("gx", "gy", "gz")
    return jax.shard_map(
        functools.partial(body, sizes),
        mesh=mesh,
        in_specs=(
            P(None, split_all),
            P(split_all),
            P(split_all),
            P(None, split_all),
            P(split_all),
            P(),
            P(),
            P(),
            P(),
            P(),
            P(),
            P(),
        ),
        out_specs=(P(split_all), P(None, split_all)),
        check_vma=False,
    )
```
